32 devices in a mesh: dp: 8 (over y, x, core), tensor: 4 (over z).
Axes of the slice: x: 2, y: 2, z: 4, core: 2. Of those that a mesh axis runs over, the one named last changes fastest.
Arguments:
- inputs: bfloat16 [8192, 1536], P(('dp', 'tensor')), may hold values from -6 to 6
- first_gain: bfloat16 [1536], P('dp'), may hold values from 0.5 to 1.5
- query_weight: bfloat16 [1536, 1536], P('dp', 'tensor'), may hold values from -0.15625 to 0.15625
- key_matrix: bfloat16 [1536, 768], P('dp', 'tensor'), may hold values from -0.15625 to 0.15625
- value_matrix: bfloat16 [1536, 768], P('dp', 'tensor'), may hold values from -0.15625 to 0.15625
- output_weight: bfloat16 [1536, 1536], P('tensor', 'dp'), may hold values from -1 to 1
- second_gain: bfloat16 [1536], P('dp'), may hold values from 0.5 to 1.5
- gate_weight: bfloat16 [1536, 4096], P('dp', 'tensor'), may hold values from -0.15625 to 0.15625
- up_weight: bfloat16 [1536, 4096], P('dp', 'tensor'), may hold values from -0.15625 to 0.15625
- down_weight: bfloat16 [4096, 1536], P('tensor', 'dp'), may hold values from -0.09375 to 0.09375
- seq_lengths: int32 [3], replicated, may hold values from 1 to 4096, as said below
- piece_starts: int32 [7], replicated, may hold values from 896 to 7424, as said below
- out_cotangent: bfloat16 [8192, 1536], P(('dp', 'tensor')), may hold values from -6 to 6
Outputs:
- layer_out: bfloat16 [8192, 1536], P(('dp', 'tensor'))
- input_grad: bfloat16 [8192, 1536], P(('dp', 'tensor'))
- first_gain_grad: float32 [1536], P('dp')
- query_grad: float32 [1536, 1536], P('dp', 'tensor')
- key_grad: float32 [1536, 768], P('dp', 'tensor')
- value_grad: float32 [1536, 768], P('dp', 'tensor')
- output_grad: float32 [1536, 1536], P('tensor', 'dp')
- second_gain_grad: float32 [1536], P('dp')
- gate_grad: float32 [1536, 4096], P('dp', 'tensor')
- up_grad: float32 [1536, 4096], P('dp', 'tensor')
- down_grad: float32 [4096, 1536], P('tensor', 'dp')
The draws below stay inside these ranges and needn't reach their ends.
Inputs may be any that keep to these rules, and one draw needn't show every extreme that they name: `seq_lengths`: the sequences fill all 8192 tokens; the first has exactly 4096 tokens and the last 2048. `piece_starts`: piece p starts at p * 1024 + 1024 // 2 plus an offset of 0 to 768; the first and the last piece take the offset 1024 // 2 - 256 // 2; pieces never intersect and end within the tokens, and may cross ends of sequences.
All inputs are finite; a program needn't handle non-finite values.
Results may differ from the reference program's by a relative error of at most 0.02.
Values may be sent and summed in bfloat16 or wider, within the bound.
No kernel may reach another device: no remote copies, remote signals or barrier semaphores. Data moves between devices by JAX's collectives and lax.ppermute only.
A program may use at most 192 MiB of HBM per device.

```python
import math
import jax
import jax.numpy as jnp
from jax import lax

MODEL_WIDTH = 1536
QUERY_HEADS = 16
KEY_HEADS = 8
HEAD_WIDTH = 96
FF = 4096
TOK_DEV = 1024
LEN_MAX = 4096
PIECE = 256
TOKEN_TOTAL = 8192
NSEQ = 3
NPIECE = 7


def draw_piece_starts(key, part):
    offsets = jax.random.randint(key, (NPIECE,), 0, TOK_DEV - PIECE + 1).astype(jnp.int32)
    edge_offset = TOK_DEV // 2 - PIECE // 2
    offsets = offsets.at[0].set(edge_offset).at[NPIECE - 1].set(edge_offset)
    return (jnp.arange(NPIECE, dtype=jnp.int32) * TOK_DEV + TOK_DEV // 2 + offsets).astype(jnp.int32)


def draw_seq_lengths(key, part):
    middle_count = NSEQ - 2
    middle_total = TOKEN_TOTAL - LEN_MAX - LEN_MAX // 2
    quotient = middle_total // middle_count
    remainder = middle_total - quotient * middle_count
    spread = max(0, min(quotient - 1, LEN_MAX - quotient - 2))
    base_lengths = jnp.full((middle_count,), quotient, jnp.int32) + (jnp.arange(middle_count, dtype=jnp.int32) < remainder).astype(jnp.int32)
    order = jax.random.permutation(jax.random.fold_in(key, 11), middle_count)
    half_count = middle_count // 2
    moves = jax.random.randint(jax.random.fold_in(key, 12), (half_count,), -spread, spread + 1).astype(jnp.int32)
    change = jnp.zeros((middle_count,), jnp.int32).at[order[:half_count]].add(moves).at[order[half_count:2 * half_count]].add(-moves)
    middle = (base_lengths + change).astype(jnp.int32)
    return jnp.concatenate([jnp.array([LEN_MAX], jnp.int32), middle, jnp.array([LEN_MAX // 2], jnp.int32)]).astype(jnp.int32)


def block_levels(own_key, extent, split, low, high):
    level = 1.0
    for dim, shards_of in split:
        heights = jax.random.uniform(jax.random.fold_in(jax.random.fold_in(own_key, 6), dim), (shards_of,), jnp.float32, low / len(split), high / len(split))
        level = level * jnp.repeat(jnp.exp(heights), extent[dim] // shards_of).reshape((-1,) + (1,) * (len(extent) - 1 - dim))
    return level


def bell_draw(stream_key, dims, scale, most, cuts=(), kind=jnp.bfloat16):
    entries = jax.random.normal(stream_key, dims, jnp.float32) * scale
    if len(cuts) > 0:
        entries = block_levels(stream_key, dims, cuts, -0.22, 0.18) * entries
    return jnp.clip(entries, min=-most, max=most).astype(kind)


def setup_inputs(seed: int = 0) -> dict:
    key_of = jax.random.split(jax.random.key(seed), 14)
    return {
        "inputs": bell_draw(key_of[0], (TOKEN_TOTAL, MODEL_WIDTH), 1.0, 6.0, ((0, 32),)),
        "first_gain": jnp.clip(1.0 + 0.1 * jax.random.normal(key_of[1], (MODEL_WIDTH,), jnp.float32), 0.5, 1.5).astype(jnp.bfloat16),
        "query_weight": bell_draw(key_of[2], (MODEL_WIDTH, QUERY_HEADS * HEAD_WIDTH), MODEL_WIDTH ** -0.5, 0.15625, ((0, 8), (1, 4))),
        "key_matrix": bell_draw(key_of[3], (MODEL_WIDTH, KEY_HEADS * HEAD_WIDTH), MODEL_WIDTH ** -0.5, 0.15625, ((0, 8), (1, 4))),
        "value_matrix": bell_draw(key_of[4], (MODEL_WIDTH, KEY_HEADS * HEAD_WIDTH), MODEL_WIDTH ** -0.5, 0.15625, ((0, 8), (1, 4))),
        "output_weight": bell_draw(key_of[5], (QUERY_HEADS * HEAD_WIDTH, MODEL_WIDTH), (QUERY_HEADS * HEAD_WIDTH // 48) ** -0.5, 1.0, ((0, 4), (1, 8))),
        "second_gain": jnp.clip(1.0 + 0.1 * jax.random.normal(key_of[6], (MODEL_WIDTH,), jnp.float32), 0.5, 1.5).astype(jnp.bfloat16),
        "gate_weight": bell_draw(key_of[7], (MODEL_WIDTH, FF), MODEL_WIDTH ** -0.5, 0.15625, ((0, 8), (1, 4))),
        "up_weight": bell_draw(key_of[8], (MODEL_WIDTH, FF), MODEL_WIDTH ** -0.5, 0.15625, ((0, 8), (1, 4))),
        "down_weight": bell_draw(key_of[9], (FF, MODEL_WIDTH), FF ** -0.5, 0.09375, ((0, 4), (1, 8))),
        "seq_lengths": draw_seq_lengths(jax.random.fold_in(key_of[13], 71), 0),
        "piece_starts": draw_piece_starts(jax.random.fold_in(key_of[13], 71), 0),
        "out_cotangent": bell_draw(key_of[12], (TOKEN_TOTAL, MODEL_WIDTH), 1.0, 6.0, ((0, 32),)),
    }


@jax.custom_vjp
def lower_result(v):
    return lax.optimization_barrier(v.astype(jnp.bfloat16)).astype(jnp.float32)

@jax.custom_vjp
def lower_backward(v):
    return v

def low_keep(v):
    return (lower_result(v), None)

def low_pass(kept, grad):
    return (grad,)

def back_keep(v):
    return (v, None)

def back_low(kept, grad):
    return (lower_result(grad),)
lower_result.defvjp(low_keep, low_pass)
lower_backward.defvjp(back_keep, back_low)
epsilon = 1e-05
rope_base = 100000.0
negative = -1e+30

def matrix_product(left_side, right_side):
    return jnp.dot(left_side, right_side, precision=lax.Precision.HIGHEST)

def token_tables(token_index, seq_lengths, piece_starts):
    ends = jnp.cumsum(seq_lengths).astype(jnp.int32)
    after = (token_index[:, None] >= ends[None, :]).astype(jnp.int32)
    segment = lax.optimization_barrier(jnp.sum(after, axis=1)).astype(jnp.int32)
    position = (token_index - lax.optimization_barrier(jnp.sum(after * seq_lengths[None, :], axis=1))).astype(jnp.int32)
    inside = (token_index[:, None] >= piece_starts[None, :]) & (token_index[:, None] < piece_starts[None, :] + PIECE)
    labels = jnp.arange(piece_starts.shape[0], dtype=jnp.int32)[None, :] + 1
    piece_id = (lax.optimization_barrier(jnp.sum(jnp.where(inside, labels, 0), axis=1)) - 1).astype(jnp.int32)
    return (segment, position, piece_id)

def rotate(values, position):
    half_width = values.shape[-1] // 2
    frequency = rope_base ** (-(2.0 / values.shape[-1]) * jnp.arange(half_width, dtype=jnp.float32))
    angles = position.astype(jnp.float32)[:, None] * frequency[None, :]
    cosine = jnp.cos(angles)[:, None, :]
    sine_part = jnp.sin(angles)[:, None, :]
    front_half = values[..., :half_width]
    back_half = values[..., half_width:]
    return jnp.concatenate([front_half * cosine - back_half * sine_part, back_half * cosine + front_half * sine_part], axis=-1)

def rms_norm(values, gain):
    return values * lax.rsqrt(lax.optimization_barrier(jnp.mean(values * values, axis=-1, keepdims=True)) + epsilon) * gain

def attention(query_states, keys, values, segment, token_index, piece_id):
    rows_per_block = min(512, TOKEN_TOTAL)
    query_group_width = QUERY_HEADS // KEY_HEADS
    width = LEN_MAX + 2 * rows_per_block
    padding = (LEN_MAX, 2 * rows_per_block)
    pad_keys = jnp.pad(keys, (padding, (0, 0), (0, 0)))
    pad_values = jnp.pad(values, (padding, (0, 0), (0, 0)))
    pad_segment = jnp.pad(segment, padding, constant_values=-1)
    pad_index = jnp.pad(token_index, padding, constant_values=0)
    pad_piece = jnp.pad(piece_id, padding, constant_values=-2)
    scaling = 1.0 / math.sqrt(HEAD_WIDTH)

    @jax.checkpoint
    def one_block(first_row_index):
        query_rows = lax.dynamic_slice_in_dim(query_states, first_row_index, rows_per_block, 0).reshape(rows_per_block, KEY_HEADS, query_group_width, HEAD_WIDTH)
        k_rows = lax.dynamic_slice_in_dim(pad_keys, first_row_index, width, 0)
        v_rows = lax.dynamic_slice_in_dim(pad_values, first_row_index, width, 0)
        seg_q = lax.dynamic_slice_in_dim(segment, first_row_index, rows_per_block, 0)
        idx_q = lax.dynamic_slice_in_dim(token_index, first_row_index, rows_per_block, 0)
        piece_q = lax.dynamic_slice_in_dim(piece_id, first_row_index, rows_per_block, 0)
        seg_k = lax.dynamic_slice_in_dim(pad_segment, first_row_index, width, 0)
        idx_k = lax.dynamic_slice_in_dim(pad_index, first_row_index, width, 0)
        piece_k = lax.dynamic_slice_in_dim(pad_piece, first_row_index, width, 0)
        allowed = (seg_q[:, None] == seg_k[None, :]) & ((idx_k[None, :] <= idx_q[:, None]) | (piece_q[:, None] == piece_k[None, :]) & (piece_q[:, None] >= 0))
        raw_scores = jnp.einsum('qhgd,khd->hgqk', query_rows, k_rows, precision=lax.Precision.HIGHEST)
        scores = lower_backward(jnp.where(allowed[None, None], raw_scores * scaling, negative))
        running_max = lax.optimization_barrier(jnp.max(scores, axis=-1, keepdims=True))
        expos = jnp.exp(scores - running_max)
        probabilities = lower_result(expos / lax.optimization_barrier(jnp.sum(expos, axis=-1, keepdims=True)))
        mixed_heads = jnp.einsum('hgqk,khd->qhgd', probabilities, v_rows, precision=lax.Precision.HIGHEST)
        return mixed_heads.reshape(rows_per_block, QUERY_HEADS * HEAD_WIDTH)
    starts = jnp.arange(TOKEN_TOTAL // rows_per_block, dtype=jnp.int32) * rows_per_block
    return lax.map(one_block, starts).reshape(TOKEN_TOTAL, QUERY_HEADS * HEAD_WIDTH)

def reference(inputs, first_gain, query_weight, key_matrix, value_matrix, output_weight, second_gain, gate_weight, up_weight, down_weight, seq_lengths, piece_starts, out_cotangent):
    token_index = jnp.arange(TOKEN_TOTAL, dtype=jnp.int32)
    segment, position, piece_id = token_tables(token_index, seq_lengths, piece_starts)

    def whole_layer(stream_in, gain_one, w_query, key_projection_weight, value_projection_weight, w_output, gain_two, w_gate, w_up, w_down):
        first_norm_output = lower_result(rms_norm(stream_in, gain_one))
        q_pre = lower_backward(matrix_product(first_norm_output, w_query)).reshape(TOKEN_TOTAL, QUERY_HEADS, HEAD_WIDTH)
        key_unrotated = lower_backward(matrix_product(first_norm_output, key_projection_weight)).reshape(TOKEN_TOTAL, KEY_HEADS, HEAD_WIDTH)
        value_states_whole = lower_result(lower_backward(matrix_product(first_norm_output, value_projection_weight))).reshape(TOKEN_TOTAL, KEY_HEADS, HEAD_WIDTH)
        query_states = lower_result(rotate(q_pre, position))
        keys = lower_result(rotate(key_unrotated, position))
        mixed = lower_result(lower_backward(attention(query_states, keys, value_states_whole, segment, token_index, piece_id)))
        after_attn = stream_in + lower_backward(matrix_product(mixed, w_output))
        norm_two = lower_result(rms_norm(after_attn, gain_two))
        gate = lower_backward(matrix_product(norm_two, w_gate))
        up_part = lower_backward(matrix_product(norm_two, w_up))
        hidden = lower_result(jax.nn.silu(gate) * up_part)
        return after_attn + lower_backward(matrix_product(hidden, w_down))
    floats = [value.astype(jnp.float32) for value in (inputs, first_gain, query_weight, key_matrix, value_matrix, output_weight, second_gain, gate_weight, up_weight, down_weight)]
    result, pullback = jax.vjp(whole_layer, *floats)
    gradients = pullback(out_cotangent.astype(jnp.float32))
    return (result.astype(jnp.bfloat16), gradients[0].astype(jnp.bfloat16), gradients[1], gradients[2], gradients[3], gradients[4], gradients[5], gradients[6], gradients[7], gradients[8], gradients[9])
```

```python
import functools
import math

import jax
import jax.numpy as jnp
from jax import lax
from jax.experimental import pallas as pl
from jax.experimental.pallas import tpu as pltpu
from jax.sharding import Mesh, PartitionSpec as P

HEAD = 96
LANES = 128
PIECE = 256
LEN_FIRST = 4096
LEN_LAST = 2048
LEN_MAX = 4096
epsilon = 1e-05
rope_base = 100000.0
negative = -1e30
far_away = 1 << 30
log2_e = 1.4426950408889634
score_scale = 1.0 / math.sqrt(HEAD)
BF = jnp.bfloat16
F32 = jnp.float32
AXES = ("g", "c", "zh", "zl")
MIB = 1024 * 1024


def params(mib):
    return pltpu.CompilerParams(vmem_limit_bytes=mib * MIB)


def nn(left, right):
    return lax.dot_general(left, right, (((1,), (0,)), ((), ())), preferred_element_type=F32)


def nt(left, right):
    return lax.dot_general(left, right, (((1,), (1,)), ((), ())), preferred_element_type=F32)


def tn(left, right):
    return lax.dot_general(left, right, (((0,), (0,)), ((), ())), preferred_element_type=F32)


def flip(value, axis, bit=1):
    count = lax.axis_size(axis)
    return lax.ppermute(value, axis, [(s, s ^ bit) for s in range(count)])


def bits_of(count):
    return [1 << b for b in range(count.bit_length() - 1)]


def lowest(k):
    return k & -k


def highest(k):
    return 1 << (k.bit_length() - 1)


def spread(value):
    count = lax.axis_size("g")
    half = value.shape[0] // 2
    front, back, whole = {0: value[:half]}, {0: value[half:]}, {0: value}
    for k in range(1, count):
        if lowest(k) == k:
            whole[k] = flip(value, "g", k)
            front[k], back[k] = whole[k][:half], whole[k][half:]
    for k in range(1, count):
        if k not in front:
            front[k] = flip(front[k ^ highest(k)], "g", highest(k))
    for k in sorted(range(1, count), key=lowest, reverse=True):
        if k not in back:
            back[k] = flip(back[k ^ lowest(k)], "g", lowest(k))
    pieces = []
    for k in range(count):
        pieces.append(whole[k] if k in whole else jnp.concatenate([front[k], back[k]], 0))
    return pieces


def collect(pieces):
    count = len(pieces)
    half = pieces[0].shape[-2] // 2
    front = [p[..., :half, :].astype(F32) for p in pieces]
    back = [p[..., half:, :].astype(F32) for p in pieces]
    for k in range(count - 1, 0, -1):
        h = highest(k)
        front[k ^ h] = front[k ^ h] + flip(front[k].astype(BF), "g", h).astype(F32)
    for k in sorted(range(1, count), key=lambda k: (lowest(k), k)):
        h = lowest(k)
        back[k ^ h] = back[k ^ h] + flip(back[k].astype(BF), "g", h).astype(F32)
    return jnp.concatenate([front[0], back[0]], -2)


def gather_rows(own):
    beside = flip(own, "zl")
    across = flip(own, "c")
    both = flip(beside, "c")
    return [own, beside, across, both]


def reduce_rows(parts):
    across_both = flip(parts[3].astype(BF), "c")
    across = flip(parts[2].astype(BF), "c")
    beside = flip((parts[1].astype(F32) + across_both.astype(F32)).astype(BF), "zl")
    return parts[0].astype(F32) + across.astype(F32) + beside.astype(F32)


def gather_weights(shard):
    c, zh, g = lax.axis_index("c"), lax.axis_index("zh"), lax.axis_index("g")
    rows, _, width = shard.shape
    keep = lax.dynamic_index_in_dim(shard, c, 1, False)
    give = lax.dynamic_index_in_dim(shard, 1 - c, 1, False)
    got = flip(give, "c")
    pair = jnp.where(c == 0, jnp.concatenate([keep, got], 0), jnp.concatenate([got, keep], 0))
    other = flip(pair, "zh")
    count = lax.axis_size("g")
    full = jnp.zeros((2, count * 2 * rows, width), shard.dtype)
    for block, index in ((pair, zh), (other, 1 - zh)):
        for k, piece in enumerate(spread(block)):
            full = lax.dynamic_update_slice(full, piece[None], (index, (g ^ k) * 2 * rows, 0))
    return full


def scatter_weights(partial):
    c, zh, g = lax.axis_index("c"), lax.axis_index("zh"), lax.axis_index("g")
    count = lax.axis_size("g")
    rows = partial.shape[1] // count
    pieces = [lax.dynamic_slice_in_dim(partial, (g ^ k) * rows, rows, 1) for k in range(count)]
    summed = collect(pieces)
    keep = lax.dynamic_index_in_dim(summed, zh, 0, False)
    give = lax.dynamic_index_in_dim(summed, 1 - zh, 0, False)
    mine = keep + flip(give.astype(BF), "zh").astype(F32)
    half = rows // 2
    own = lax.dynamic_slice_in_dim(mine, c * half, half, 0)
    got = flip(lax.dynamic_slice_in_dim(mine, (1 - c) * half, half, 0).astype(BF), "c").astype(F32)
    return jnp.where(c == 0, jnp.stack([own, got], 1), jnp.stack([got, own], 1))


def add_everywhere(value):
    for axis in AXES:
        for bit in bits_of(lax.axis_size(axis)):
            value = value + flip(value, axis, bit)
    return value


def swap_halves(value):
    width = value.shape[1]
    lane = lax.broadcasted_iota(jnp.int32, value.shape, 1)
    front = lax.rem(lane, HEAD) < HEAD // 2
    return jnp.where(front, pltpu.roll(value, width - HEAD // 2, 1), pltpu.roll(value, HEAD // 2, 1))


def widen(value):
    pad = jnp.zeros((value.shape[0], LANES - HEAD), value.dtype)
    return jnp.concatenate([value, pad], 1)


def qkv_kernel(x_ref, gain_ref, weight_ref, cos_ref, sin_ref, norm_ref, query_ref, kv_ref):
    x = x_ref[0].astype(F32)
    r = lax.rsqrt(jnp.mean(x * x, axis=-1, keepdims=True) + epsilon)
    normed = (x * r * gain_ref[...]).astype(BF)
    norm_ref[0] = normed
    packs = []
    for j in range(2):
        pre = nn(normed, weight_ref[j])
        turned = pre * cos_ref[0] + swap_halves(pre) * sin_ref[0]
        query_ref[j, 0, 0:PIECE] = widen(turned[:, 0:HEAD]).astype(BF)
        query_ref[j, 0, PIECE : 2 * PIECE] = widen(turned[:, HEAD : 2 * HEAD]).astype(BF)
        packs.append(turned[:, 2 * HEAD :])
    kv_ref[...] = jnp.concatenate(packs, 1).astype(BF)


def project_qkv(x_rows, gain, weights, cos_table, sin_table):
    count, rows, width = x_rows.shape
    return pl.pallas_call(
        qkv_kernel,
        grid=(count,),
        in_specs=[
            pl.BlockSpec((1, rows, width), lambda i: (i, 0, 0)),
            pl.BlockSpec((1, width), lambda i: (0, 0)),
            pl.BlockSpec((2, width, 4 * HEAD), lambda i: (0, 0, 0)),
            pl.BlockSpec((1, rows, 4 * HEAD), lambda i: (i, 0, 0)),
            pl.BlockSpec((1, rows, 4 * HEAD), lambda i: (i, 0, 0)),
        ],
        out_specs=[
            pl.BlockSpec((1, rows, width), lambda i: (i, 0, 0)),
            pl.BlockSpec((2, 1, 2 * rows, LANES), lambda i: (0, i, 0, 0)),
            pl.BlockSpec((rows, 4 * HEAD), lambda i: (i, 0)),
        ],
        out_shape=[
            jax.ShapeDtypeStruct((count, rows, width), BF),
            jax.ShapeDtypeStruct((2, count, 2 * rows, LANES), BF),
            jax.ShapeDtypeStruct((count * rows, 4 * HEAD), BF),
        ],
        compiler_params=params(40),
        name="project_qkv",
    )(x_rows, gain, weights, cos_table, sin_table)


def qkv_back_kernel(dq_ref, dkv_ref, weight_ref, cos_ref, sin_ref, grad_ref, share_ref):
    total = None
    for j in range(2):
        packed = jnp.concatenate(
            [
                dq_ref[j, 0, 0:PIECE][:, 0:HEAD],
                dq_ref[j, 0, PIECE : 2 * PIECE][:, 0:HEAD],
                dkv_ref[...][:, 2 * HEAD * j : 2 * HEAD * (j + 1)],
            ],
            1,
        )
        turned = (packed * cos_ref[0] - swap_halves(packed) * sin_ref[0]).astype(BF)
        grad_ref[j, 0] = turned
        term = nt(turned, weight_ref[j])
        total = term if total is None else total + term
    share_ref[0] = total.astype(BF)


def project_back(d_query, d_kv, weights, cos_table, sin_table):
    _, count, _, _ = d_query.shape
    rows = PIECE
    width = weights.shape[1]
    return pl.pallas_call(
        qkv_back_kernel,
        grid=(count,),
        in_specs=[
            pl.BlockSpec((2, 1, 2 * rows, LANES), lambda i: (0, i, 0, 0)),
            pl.BlockSpec((rows, 4 * HEAD), lambda i: (i, 0)),
            pl.BlockSpec((2, width, 4 * HEAD), lambda i: (0, 0, 0)),
            pl.BlockSpec((1, rows, 4 * HEAD), lambda i: (i, 0, 0)),
            pl.BlockSpec((1, rows, 4 * HEAD), lambda i: (i, 0, 0)),
        ],
        out_specs=[
            pl.BlockSpec((2, 1, rows, 4 * HEAD), lambda i: (0, i, 0, 0)),
            pl.BlockSpec((1, rows, width), lambda i: (i, 0, 0)),
        ],
        out_shape=[
            jax.ShapeDtypeStruct((2, count, rows, 4 * HEAD), BF),
            jax.ShapeDtypeStruct((count, rows, width), BF),
        ],
        compiler_params=params(40),
        name="project_back",
    )(d_query, d_kv, weights, cos_table, sin_table)


CHUNK = 2 * PIECE


def unpack_kv(block_refs, key_scratch, value_scratch):
    lane = lax.broadcasted_iota(jnp.int32, (CHUNK, LANES - HEAD), 1)
    ones = jnp.where(lane < 3, 1.0, 0.0).astype(BF)
    at = 0
    for ref in block_refs:
        for start in range(0, ref.shape[0], CHUNK):
            block = ref[start : start + CHUNK, :]
            for j in range(2):
                k = block[:, 2 * HEAD * j : 2 * HEAD * j + HEAD]
                v = block[:, 2 * HEAD * j + HEAD : 2 * HEAD * (j + 1)]
                key_scratch[j, at : at + CHUNK, :] = jnp.concatenate([k, ones], 1)
                value_scratch[j, at : at + CHUNK, :] = jnp.concatenate([v, ones], 1)
            at += CHUNK


def chunk_state(info_ref, base, i):
    last = base + (CHUNK - 1)
    touched = (base <= info_ref[i, 3]) & (last >= info_ref[i, 0])
    full = (base >= info_ref[i, 1]) & (last <= info_ref[i, 2])
    return touched, full


def forward_kernel(n_blocks, first, last, info_ref, base_ref, zl_ref, *refs):
    refs = list(refs)
    query_ref, low_ref, high_ref = refs[:3]
    block_refs = refs[3 : 3 + n_blocks]
    refs = refs[3 + n_blocks :]
    if not first:
        acc_in, top_in = refs[:2]
        refs = refs[2:]
    if last:
        mixed_ref, kept_ref = refs[:2]
    else:
        acc_out, top_out = refs[:2]
    key_scratch, value_scratch, acc, top = refs[2:]
    i = pl.program_id(0)

    @pl.when(i == 0)
    def _():
        unpack_kv(block_refs, key_scratch, value_scratch)

    for j in range(2):
        if first:
            acc[j] = jnp.zeros((CHUNK, LANES), F32)
            top[j] = jnp.full((CHUNK, LANES), negative, F32)
        else:
            acc[j] = acc_in[j, 0]
            top[j] = top_in[j, 0]
    n_chunks = sum(r.shape[0] for r in block_refs) // CHUNK

    def visit(n, masked):
        rows = pl.ds(pl.multiple_of(n * CHUNK, CHUNK), CHUNK)
        if masked:
            at = lax.broadcasted_iota(jnp.int32, (PIECE, CHUNK), 1)
            token = base_ref[n] + lax.rem(at + zl_ref[0] * PIECE, CHUNK)
            low = jnp.concatenate([low_ref[0]] * (CHUNK // LANES), 1)
            high = jnp.concatenate([high_ref[0]] * (CHUNK // LANES), 1)
            allowed = (token >= low) & (token <= high)
        for j in range(2):
            scores = nt(query_ref[j, 0], key_scratch[j, rows, :])
            if masked:
                scores = jnp.concatenate(
                    [jnp.where(allowed, scores[h * PIECE : (h + 1) * PIECE], negative) for h in range(2)], 0
                )
            old = top[j]
            new = jnp.maximum(old, jnp.max(scores, axis=1, keepdims=True))
            top[j] = new
            probs = jnp.exp2(scores - jnp.concatenate([new] * (CHUNK // LANES), 1)).astype(BF)
            acc[j] = acc[j] * jnp.exp2(old - new) + nn(probs, value_scratch[j, rows, :])

    @pl.loop(0, n_chunks)
    def _(n):
        touched, full = chunk_state(info_ref, base_ref[n], i)

        @pl.when(touched & full)
        def _():
            visit(n, False)

        @pl.when(touched & jnp.logical_not(full))
        def _():
            visit(n, True)

    if last:
        lane = lax.broadcasted_iota(jnp.int32, (CHUNK, LANES), 1)
        for j in range(2):
            total = acc[j][:, HEAD : HEAD + 1]
            out = acc[j] / total
            kept_ref[j, 0] = jnp.where(lane < HEAD, out, top[j] + jnp.log2(total))
            mixed_ref[j, 0] = jnp.concatenate([out[0:PIECE, 0:HEAD], out[PIECE:, 0:HEAD]], 1).astype(BF)
    else:
        for j in range(2):
            acc_out[j, 0] = acc[j]
            top_out[j, 0] = top[j]


def attend(query, low, high, info, bases, zl, blocks, state, last):
    count = query.shape[1]
    n_keys = sum(b.shape[0] for b in blocks)
    per_piece = pl.BlockSpec((2, 1, CHUNK, LANES), lambda i, *_: (0, i, 0, 0))
    bound = pl.BlockSpec((1, PIECE, LANES), lambda i, *_: (i, 0, 0))
    in_specs = [per_piece, bound, bound]
    in_specs += [pl.BlockSpec(b.shape, lambda i, *_: (0, 0)) for b in blocks]
    args = [query, low, high, *blocks]
    if state is not None:
        in_specs += [per_piece, per_piece]
        args += list(state)
    wide = jax.ShapeDtypeStruct((2, count, CHUNK, LANES), F32)
    if last:
        out_shape = [jax.ShapeDtypeStruct((2, count, PIECE, 2 * HEAD), BF), wide]
        out_specs = [pl.BlockSpec((2, 1, PIECE, 2 * HEAD), lambda i, *_: (0, i, 0, 0)), per_piece]
    else:
        out_shape = [wide, wide]
        out_specs = [per_piece, per_piece]
    return pl.pallas_call(
        functools.partial(forward_kernel, len(blocks), state is None, last),
        grid_spec=pltpu.PrefetchScalarGridSpec(
            num_scalar_prefetch=3,
            grid=(count,),
            in_specs=in_specs,
            out_specs=out_specs,
            scratch_shapes=[
                pltpu.VMEM((2, n_keys, LANES), BF),
                pltpu.VMEM((2, n_keys, LANES), BF),
                pltpu.VMEM((2, CHUNK, LANES), F32),
                pltpu.VMEM((2, CHUNK, LANES), F32),
            ],
        ),
        out_shape=out_shape,
        compiler_params=params(48),
        name="attend",
    )(info, bases, zl, *args)


def split_three(value):
    first = value.astype(BF)
    rest = value - first.astype(F32)
    second = rest.astype(BF)
    third = (rest - second.astype(F32)).astype(BF)
    return first, second, third


def augment(wide, extra):
    lane = lax.broadcasted_iota(jnp.int32, wide.shape, 1)
    a, b, c = (part.astype(F32) for part in split_three(extra))
    out = wide.astype(F32)
    out = jnp.where(lane == HEAD, a, out)
    out = jnp.where(lane == HEAD + 1, b, out)
    out = jnp.where(lane == HEAD + 2, c, out)
    return out.astype(BF)


def backward_kernel(n_blocks, has_dq, info_ref, base_ref, zl_ref, *refs):
    refs = list(refs)
    query_ref, d_mixed_ref, kept_ref, low_ref, high_ref = refs[:5]
    block_refs = refs[5 : 5 + n_blocks]
    refs = refs[5 + n_blocks :]
    if has_dq:
        dq_in = refs.pop(0)
    dq_ref = refs.pop(0)
    out_refs = refs[:n_blocks]
    key_scratch, value_scratch, d_key, d_value, q_aug, o_aug = refs[n_blocks:]
    i = pl.program_id(0)

    @pl.when(i == 0)
    def _():
        unpack_kv(block_refs, key_scratch, value_scratch)
        d_key[...] = jnp.zeros(d_key.shape, F32)
        d_value[...] = jnp.zeros(d_value.shape, F32)

    for j in range(2):
        kept = kept_ref[j, 0]
        grad = d_mixed_ref[j, 0]
        wide = jnp.concatenate([widen(grad[:, 0:HEAD]), widen(grad[:, HEAD:])], 0)
        delta = jnp.sum(wide.astype(F32) * kept, axis=1, keepdims=True)
        q_aug[j] = augment(query_ref[j, 0], -kept[:, HEAD : HEAD + 1])
        o_aug[j] = augment(wide, -delta)
        if has_dq:
            dq_ref[j, 0] = dq_in[j, 0]
        else:
            dq_ref[j, 0] = jnp.zeros((CHUNK, LANES), F32)
    n_chunks = sum(r.shape[0] for r in block_refs) // CHUNK

    def visit(n, masked):
        rows = pl.ds(pl.multiple_of(n * CHUNK, CHUNK), CHUNK)
        if masked:
            at = lax.broadcasted_iota(jnp.int32, (CHUNK, CHUNK), 0)
            token = base_ref[n] + lax.rem(at + zl_ref[0] * PIECE, CHUNK)
            allowed = (token >= low_ref[0, 0:1, :]) & (token <= high_ref[0, 0:1, :])
        for j in range(2):
            keys = key_scratch[j, rows, :]
            probs = jnp.exp2(nt(keys, q_aug[j]))
            if masked:
                probs = jnp.where(allowed, probs, 0.0)
            d_probs = nt(value_scratch[j, rows, :], o_aug[j])
            low_probs = probs.astype(BF)
            d_scores = (probs * d_probs).astype(BF)
            d_value[j, rows, :] += nn(low_probs, o_aug[j])
            d_key[j, rows, :] += nn(d_scores, q_aug[j])
            dq_ref[j, 0] += tn(d_scores, keys)

    @pl.loop(0, n_chunks)
    def _(n):
        touched, full = chunk_state(info_ref, base_ref[n], i)

        @pl.when(touched & full)
        def _():
            visit(n, False)

        @pl.when(touched & jnp.logical_not(full))
        def _():
            visit(n, True)

    @pl.when(i == pl.num_programs(0) - 1)
    def _():
        at = 0
        for ref in out_refs:
            for start in range(0, ref.shape[0], CHUNK):
                parts = []
                for j in range(2):
                    parts.append(d_key[j, at : at + CHUNK, :][:, 0:HEAD])
                    parts.append(d_value[j, at : at + CHUNK, :][:, 0:HEAD])
                ref[start : start + CHUNK, :] = jnp.concatenate(parts, 1).astype(ref.dtype)
                at += CHUNK


def attend_back(query, d_mixed, kept, low, high, info, bases, zl, blocks, d_query, kinds):
    count = query.shape[1]
    n_keys = sum(b.shape[0] for b in blocks)
    per_piece = pl.BlockSpec((2, 1, CHUNK, LANES), lambda i, *_: (0, i, 0, 0))
    grads = pl.BlockSpec((2, 1, PIECE, 2 * HEAD), lambda i, *_: (0, i, 0, 0))
    bound = pl.BlockSpec((1, 8, CHUNK), lambda i, *_: (i, 0, 0))
    whole = [pl.BlockSpec(b.shape, lambda i, *_: (0, 0)) for b in blocks]
    in_specs = [per_piece, grads, per_piece, bound, bound, *whole]
    args = [query, d_mixed, kept, low, high, *blocks]
    if d_query is not None:
        in_specs.append(per_piece)
        args.append(d_query)
    return pl.pallas_call(
        functools.partial(backward_kernel, len(blocks), d_query is not None),
        grid_spec=pltpu.PrefetchScalarGridSpec(
            num_scalar_prefetch=3,
            grid=(count,),
            in_specs=in_specs,
            out_specs=[per_piece, *whole],
            scratch_shapes=[
                pltpu.VMEM((2, n_keys, LANES), BF),
                pltpu.VMEM((2, n_keys, LANES), BF),
                pltpu.VMEM((2, n_keys, LANES), F32),
                pltpu.VMEM((2, n_keys, LANES), F32),
                pltpu.VMEM((2, CHUNK, LANES), BF),
                pltpu.VMEM((2, CHUNK, LANES), BF),
            ],
        ),
        out_shape=[jax.ShapeDtypeStruct((2, count, CHUNK, LANES), F32)]
        + [jax.ShapeDtypeStruct(b.shape, k) for b, k in zip(blocks, kinds)],
        compiler_params=params(56),
        name="attend_back",
    )(info, bases, zl, *args)


def ffn_kernel(norm_ref, grad_ref, gate_ref, up_ref, down_ref, out_ref, back_ref, hidden_ref, dg_ref, du_ref, acc_out, acc_back):
    step = pl.program_id(0)
    rows = norm_ref[...].reshape(-1, norm_ref.shape[-1])
    grad = grad_ref[...].reshape(-1, grad_ref.shape[-1])
    gate_w, up_w, down_w = gate_ref[0], up_ref[0], down_ref[0]
    gate = nn(rows, gate_w)
    up = nn(rows, up_w)
    d_hidden = nn(grad, down_w)
    sig = jax.nn.sigmoid(gate)
    silu = gate * sig
    hidden = (silu * up).astype(BF)
    d_gate = (d_hidden * up * sig * (1.0 + gate * (1.0 - sig))).astype(BF)
    d_up = (d_hidden * silu).astype(BF)
    hidden_ref[0] = hidden
    dg_ref[0] = d_gate
    du_ref[0] = d_up
    out = nt(hidden, down_w)
    back = nt(d_gate, gate_w) + nt(d_up, up_w)

    @pl.when(step == 0)
    def _():
        acc_out[...] = out
        acc_back[...] = back

    @pl.when(step > 0)
    def _():
        acc_out[...] += out
        acc_back[...] += back

    @pl.when(step == pl.num_programs(0) - 1)
    def _():
        out_ref[...] = acc_out[...].astype(BF).reshape(out_ref.shape)
        back_ref[...] = acc_back[...].astype(BF).reshape(back_ref.shape)


def feed_forward(norm_rows, grad_rows, weights):
    count, rows, width = norm_rows.shape
    half = weights.shape[2] // 3
    tile = 256
    tiles = half // tile
    whole = pl.BlockSpec((count, rows, width), lambda s: (0, 0, 0))

    def weight_spec(which):
        return pl.BlockSpec((1, width, tile), lambda s: (s // tiles, 0, which * tiles + s % tiles))

    hid = pl.BlockSpec((1, count * rows, tile), lambda s: (s // tiles, 0, s % tiles))
    return pl.pallas_call(
        ffn_kernel,
        grid=(2 * tiles,),
        in_specs=[whole, whole, weight_spec(0), weight_spec(1), weight_spec(2)],
        out_specs=[whole, whole, hid, hid, hid],
        out_shape=[jax.ShapeDtypeStruct((count, rows, width), BF)] * 2
        + [jax.ShapeDtypeStruct((2, count * rows, half), BF)] * 3,
        scratch_shapes=[pltpu.VMEM((count * rows, width), F32)] * 2,
        compiler_params=params(56),
        name="feed_forward",
    )(norm_rows, grad_rows, weights, weights, weights)


def rms_backward(rows, scaling, gain, upstream):
    weighted = upstream * gain
    gain_part = jnp.sum(upstream * rows * scaling, axis=0)
    inner = jnp.mean(weighted * rows, axis=-1, keepdims=True)
    return scaling * weighted - rows * (scaling * scaling * scaling) * inner, gain_part


def rms_scale(rows):
    return lax.rsqrt(jnp.mean(rows * rows, axis=-1, keepdims=True) + epsilon)


def token_tables(token, seq_lengths, piece_starts):
    n = seq_lengths.shape[0]
    upto = jnp.arange(n)[None, :] <= jnp.arange(n)[:, None]
    ends = jnp.sum(jnp.where(upto, seq_lengths[None, :], 0), axis=1)
    after = token[:, None] >= ends[None, :]
    start = jnp.sum(jnp.where(after, seq_lengths[None, :], 0), axis=1)
    end = jnp.min(jnp.where(after, far_away, ends[None, :]), axis=1)
    inside = (token[:, None] >= piece_starts[None, :]) & (token[:, None] < piece_starts[None, :] + PIECE)
    piece_end = jnp.max(jnp.where(inside, piece_starts[None, :] + PIECE, 0), axis=1)
    high = jnp.maximum(token, jnp.minimum(piece_end, end) - 1)
    return start, high


def may_meet(one, two, group_tokens, count):
    total = group_tokens * count
    regions = ((0, LEN_FIRST, LEN_FIRST), (LEN_FIRST, total - LEN_LAST, LEN_MAX), (total - LEN_LAST, total, LEN_LAST))
    for start, end, longest in regions:
        both = all(g * group_tokens < end and (g + 1) * group_tokens > start for g in (one, two))
        if both and (abs(one - two) - 1) * group_tokens + 1 < longest:
            return True
    return False


def body(
    inputs,
    first_gain,
    query_weight,
    key_matrix,
    value_matrix,
    output_weight,
    second_gain,
    gate_weight,
    up_weight,
    down_weight,
    seq_lengths,
    piece_starts,
    out_cotangent,
):
    g, c, zh, zl = (lax.axis_index(a) for a in AXES)
    groups = lax.axis_size("g")
    rows, width = inputs.shape
    span = 4 * rows
    group_tokens = 2 * span
    shard_rows = query_weight.shape[0]

    def halves(matrix):
        return matrix.reshape(matrix.shape[0], 2, -1)

    spare = jnp.zeros((shard_rows, 2, 62), BF)
    gains = jnp.stack([first_gain, second_gain], 1)
    gains = jnp.broadcast_to(gains[:, None, :], (shard_rows, 2, 2))
    attn_shard = jnp.concatenate(
        [
            halves(query_weight),
            halves(key_matrix),
            halves(value_matrix),
            halves(output_weight.T),
            gains,
            spare,
        ],
        2,
    )
    ffn_shard = jnp.concatenate([halves(gate_weight), halves(up_weight), halves(down_weight.T)], 2)
    x_pieces = gather_rows(inputs)
    attn_w = gather_weights(attn_shard)
    gain_one = attn_w[0, :, 6 * HEAD].astype(F32)[None, :]
    gain_two = attn_w[0, :, 6 * HEAD + 1].astype(F32)[None, :]

    order = jnp.arange(4)
    piece_base = (2 * g + (c ^ (order >> 1))) * span + zh * CHUNK + (zl ^ (order & 1)) * rows
    token = (piece_base[:, None] + jnp.arange(rows)[None, :]).reshape(-1).astype(jnp.int32)
    low, high = token_tables(token, seq_lengths, piece_starts)
    position = (token - low).astype(F32)
    low, high = low.reshape(4, rows), high.reshape(4, rows)
    info = jnp.stack([low.min(1), low.max(1), high.min(1), high.max(1)], 1).astype(jnp.int32)
    low_wide = jnp.broadcast_to(low[:, :, None], (4, rows, LANES)).astype(jnp.int32)
    high_wide = jnp.broadcast_to(high[:, :, None], (4, rows, LANES)).astype(jnp.int32)
    low_rows = jnp.broadcast_to(jnp.tile(low, (1, 2))[:, None, :], (4, 8, CHUNK)).astype(jnp.int32)
    high_rows = jnp.broadcast_to(jnp.tile(high, (1, 2))[:, None, :], (4, 8, CHUNK)).astype(jnp.int32)
    zl_info = jnp.reshape(zl, (1,)).astype(jnp.int32)
    frequency = rope_base ** (-(2.0 / HEAD) * jnp.arange(HEAD // 2, dtype=F32))
    angles = position[:, None] * frequency[None, :]
    cosine, sine = jnp.cos(angles), jnp.sin(angles)
    cos_head = jnp.concatenate([cosine, cosine], 1)
    sin_head = jnp.concatenate([-sine, sine], 1)

    def table(part, q_scale, k_scale, rest):
        wide = jnp.concatenate([part * q_scale, part * q_scale, part * k_scale, jnp.full(part.shape, rest, F32)], 1)
        return wide.reshape(4, rows, 4 * HEAD)

    into = score_scale * log2_e
    x_rows = jnp.stack(x_pieces)
    norm_one, query, kv = project_qkv(
        x_rows, gain_one, attn_w, table(cos_head, into, 1.0, 1.0), table(sin_head, into, 1.0, 0.0)
    )

    def chunk_bases(group, half):
        return jnp.stack([(2 * group + (c ^ i)) * span + half * CHUNK for i in range(2)])

    def shift_pairs(steps):
        return [(s, s + steps) for s in range(groups) if 0 <= s + steps < groups and may_meet(s, s + steps, group_tokens, groups)]

    def present(pairs, bases):
        target = functools.reduce(jnp.logical_or, [g == t for _, t in pairs])
        return jnp.where(target, bases, far_away)

    near, near_bases = [kv], [chunk_bases(g, zh)]
    kv_other = flip(kv, "zh")
    rest, rest_bases = [kv_other], [chunk_bases(g, 1 - zh)]
    shifts = [d for d in range(1, groups) if shift_pairs(d)]
    for d in shifts:
        near.append(lax.ppermute(kv, "g", shift_pairs(d)))
        near_bases.append(present(shift_pairs(d), chunk_bases(g - d, zh)))
    for d in shifts:
        rest.append(lax.ppermute(kv_other, "g", shift_pairs(d)))
        rest_bases.append(present(shift_pairs(d), chunk_bases(g - d, 1 - zh)))
    above_groups = [s for s in range(1, groups) if may_meet(s - 1, s, group_tokens, groups)]
    if above_groups:
        first_chunk = lax.dynamic_slice_in_dim(kv, c * CHUNK, CHUNK, 0)
        above_pairs = [(2 * s, 2 * (s - 1) + 1) for s in above_groups]
        rest.append(lax.ppermute(first_chunk, ("g", "zh"), above_pairs))
        is_target = functools.reduce(jnp.logical_or, [(g == s - 1) & (zh == 1) for s in above_groups])
        rest_bases.append(jnp.where(is_target, jnp.reshape(2 * (g + 1) * span, (1,)), far_away))
    near_bases = jnp.concatenate(near_bases).astype(jnp.int32)
    rest_bases = jnp.concatenate(rest_bases).astype(jnp.int32)

    state = attend(query, low_wide, high_wide, info, near_bases, zl_info, near, None, False)
    mixed, kept = attend(query, low_wide, high_wide, info, rest_bases, zl_info, rest, state, True)

    out_w = attn_w[:, :, 4 * HEAD : 6 * HEAD]

    def out_projection(k):
        return nt(mixed[0, k], out_w[0]) + nt(mixed[1, k], out_w[1])

    stream = inputs.astype(F32)
    after_attn = stream + reduce_rows([out_projection(k) for k in range(4)])
    scale_two = rms_scale(after_attn)
    norm_two_own = (after_attn * scale_two * gain_two).astype(BF)
    norm_two = gather_rows(norm_two_own)
    cotangents = gather_rows(out_cotangent)
    ffn_w = gather_weights(ffn_shard)

    early = feed_forward(jnp.stack([norm_two[0], norm_two[2]]), jnp.stack([cotangents[0], cotangents[2]]), ffn_w)
    late = feed_forward(jnp.stack([norm_two[1], norm_two[3]]), jnp.stack([cotangents[1], cotangents[3]]), ffn_w)

    def ordered(n):
        return [early[n][0], late[n][0], early[n][1], late[n][1]]

    layer_out = (after_attn + reduce_rows(ordered(0))).astype(BF)
    d_norm_two = reduce_rows(ordered(1))

    def weight_term(left, n):
        first = left[0], left[2]
        second = left[1], left[3]
        return [
            (tn(jnp.concatenate(first, 0), early[n][j]) + tn(jnp.concatenate(second, 0), late[n][j])).astype(BF)
            for j in range(2)
        ]

    gate_part = weight_term(norm_two, 3)
    up_part = weight_term(norm_two, 4)
    down_part = weight_term(cotangents, 2)
    ffn_part = jnp.stack([jnp.concatenate([gate_part[j], up_part[j], down_part[j]], 1) for j in range(2)])
    ffn_grads = scatter_weights(ffn_part)

    d_two, gain_two_part = rms_backward(after_attn, scale_two, gain_two, d_norm_two)
    grad_mid = out_cotangent.astype(F32) + d_two
    grad_mid_rows = jnp.stack(gather_rows(grad_mid.astype(BF)))
    d_mixed = jnp.stack(
        [nn(grad_mid_rows.reshape(span, width), out_w[j]).astype(BF).reshape(4, rows, 2 * HEAD) for j in range(2)]
    )

    back_rest = attend_back(
        query, d_mixed, kept, low_rows, high_rows, info, rest_bases, zl_info, rest, None, [BF] * len(rest)
    )
    d_query, d_rest = back_rest[0], list(back_rest[1:])
    n_far = len(shifts)
    back_near = attend_back(
        query, d_mixed, kept, low_rows, high_rows, info, near_bases, zl_info, near, d_query, [F32] + [BF] * n_far
    )
    d_query, d_kv, d_near = back_near[0], back_near[1], list(back_near[2:])

    def reverse(pairs):
        return [(t, s) for s, t in pairs]

    other_sum = d_rest[0].astype(F32)
    for n, d in enumerate(shifts):
        other_sum = other_sum + lax.ppermute(d_rest[1 + n], "g", reverse(shift_pairs(d))).astype(F32)
        d_kv = d_kv + lax.ppermute(d_near[n], "g", reverse(shift_pairs(d))).astype(F32)
    d_kv = d_kv + flip(other_sum.astype(BF), "zh").astype(F32)
    if above_groups:
        returned = lax.ppermute(d_rest[-1], ("g", "zh"), reverse(above_pairs)).astype(F32)
        at = lax.broadcasted_iota(jnp.int32, (2, 1, 1), 0)
        d_kv = d_kv + jnp.where(at == c, returned[None], 0.0).reshape(d_kv.shape)

    d_qkv, shares = project_back(
        d_query,
        d_kv,
        attn_w,
        table(cos_head, score_scale, 1.0 / log2_e, 1.0),
        table(sin_head, score_scale, 1.0 / log2_e, 0.0),
    )
    d_norm_one = reduce_rows([shares[k] for k in range(4)])
    norm_one_rows = norm_one.reshape(span, width)
    grad_mid_all = grad_mid_rows.reshape(span, width)
    attn_part = jnp.stack(
        [
            jnp.concatenate(
                [
                    tn(norm_one_rows, d_qkv[j].reshape(span, 4 * HEAD)).astype(BF),
                    tn(grad_mid_all, mixed[j].reshape(span, 2 * HEAD)).astype(BF),
                    jnp.zeros((width, 64), BF),
                ],
                1,
            )
            for j in range(2)
        ]
    )
    attn_grads = scatter_weights(attn_part)
    d_one, gain_one_part = rms_backward(stream, rms_scale(stream), gain_one, d_norm_one)
    input_grad = (grad_mid + d_one).astype(BF)
    gain_sums = add_everywhere(jnp.stack([gain_one_part, gain_two_part]))
    gain_shard = lax.dynamic_slice_in_dim(gain_sums, (2 * g + c) * shard_rows, shard_rows, 1)

    def both_halves(part, start, size):
        return part[:, :, start : start + size].reshape(shard_rows, 2 * size)

    half = gate_weight.shape[1] // 2
    return (
        layer_out,
        input_grad,
        gain_shard[0],
        both_halves(attn_grads, 0, 2 * HEAD),
        both_halves(attn_grads, 2 * HEAD, HEAD),
        both_halves(attn_grads, 3 * HEAD, HEAD),
        both_halves(attn_grads, 4 * HEAD, 2 * HEAD).T,
        gain_shard[1],
        both_halves(ffn_grads, 0, half),
        both_halves(ffn_grads, half, half),
        both_halves(ffn_grads, 2 * half, half).T,
    )


def solution(mesh):
    outer, inner = mesh.devices.shape
    fine = Mesh(mesh.devices.reshape(outer // 2, 2, inner // 2, 2), AXES)
    data, tensor = ("g", "c"), ("zh", "zl")
    rows, first = P(AXES, None), P(data)
    wide, tall = P(data, tensor), P(tensor, data)
    return jax.shard_map(
        body,
        mesh=fine,
        in_specs=(rows, first, wide, wide, wide, tall, first, wide, wide, tall, P(), P(), rows),
        out_specs=(rows, rows, first, wide, wide, wide, tall, first, wide, wide, tall),
        check_vma=False,
    )
```

```python
import functools
import math

import jax
import jax.numpy as jnp
from jax import lax
from jax.experimental import pallas as pl
from jax.experimental.layout import Layout, with_layout_constraint
from jax.experimental.pallas import tpu as pltpu
from jax.sharding import Mesh, PartitionSpec as P

HEAD = 96
LANES = 128
PIECE = 256
LEN_FIRST = 4096
LEN_LAST = 2048
LEN_MAX = 4096
epsilon = 1e-05
rope_base = 100000.0
negative = -1e30
far_away = 1 << 30
log2_e = 1.4426950408889634
score_scale = 1.0 / math.sqrt(HEAD)
BF = jnp.bfloat16
F32 = jnp.float32
AXES = ("g", "c", "zh", "zl")
MIB = 1024 * 1024
COST_SHARE = 0.01


def params(mib):
    return pltpu.CompilerParams(vmem_limit_bytes=mib * MIB)


def nn(left, right):
    return lax.dot_general(left, right, (((1,), (0,)), ((), ())), preferred_element_type=F32)


def nt(left, right):
    return lax.dot_general(left, right, (((1,), (1,)), ((), ())), preferred_element_type=F32)


def tn(left, right):
    return lax.dot_general(left, right, (((0,), (0,)), ((), ())), preferred_element_type=F32)


def after(value, *earlier):
    return lax.optimization_barrier((value, *earlier))[0]


def sync(*values):
    return lax.optimization_barrier(values)


def all_groups(value):
    return lax.all_gather(value, "g", axis=0, tiled=True)


def flip(value, axis, bit=1):
    count = lax.axis_size(axis)
    return lax.ppermute(value, axis, [(s, s ^ bit) for s in range(count)])


def cost(us):
    us = us * COST_SHARE
    return pl.CostEstimate(flops=int(us * 1.15e9), bytes_accessed=int(us * 3.6e6), transcendentals=0)


def gather_rows(own):
    beside = flip(own, "zl")
    across = flip(own, "c")
    both = flip(beside, "c")
    return [own, beside, across, both]


def from_groups(value):
    return [value] + [flip(value, "g", k) for k in range(1, lax.axis_size("g"))]


def split_core(shard):
    c = lax.axis_index("c")
    keep = lax.dynamic_index_in_dim(shard, c, 0, False)
    got = flip(lax.dynamic_index_in_dim(shard, 1 - c, 0, False), "c")
    return keep, got


def in_order(keep, got, axis=0):
    c = lax.axis_index("c")
    return jnp.where(c == 0, jnp.concatenate([keep, got], axis), jnp.concatenate([got, keep], axis))


def by_rows(value):
    return with_layout_constraint(value, Layout(major_to_minor=(0, 1)))


def over_groups(value):
    return lax.psum_scatter(value, "g", scatter_dimension=0, tiled=True)


def to_owner(mine):
    c = lax.axis_index("c")
    half = mine.shape[0] // 2
    own = lax.dynamic_slice_in_dim(mine, c * half, half, 0).astype(F32)
    got = flip(lax.dynamic_slice_in_dim(mine, (1 - c) * half, half, 0).astype(BF), "c").astype(F32)
    return own, got


def joined(own, got):
    return in_order(own, got, 1)


def swap_halves(value):
    lane = lax.broadcasted_iota(jnp.int32, value.shape, 1)
    return jnp.where(lane < HEAD // 2, pltpu.roll(value, LANES - HEAD // 2, 1), pltpu.roll(value, HEAD // 2, 1))


def turn(value, cosine, sine):
    return value * cosine + swap_halves(value) * sine


def unturn(value, cosine, sine):
    return value * cosine - swap_halves(value) * sine


def widen(value):
    pad = jnp.zeros((value.shape[0], LANES - HEAD), value.dtype)
    return jnp.concatenate([value, pad], 1)


def qkv_kernel(count, where_ref, *refs):
    pieces, refs = refs[: 2 * count], refs[2 * count :]
    x0, x1, x_far, cos_ref, sin_ref, norm_ref, query_ref, kv_ref, weight_ref, gains_ref, x_ref = refs
    step = pl.program_id(0)

    @pl.when(step == 0)
    def _():
        half = pieces[0].shape[0] // 2
        for n, piece in enumerate(pieces):
            for part in range(2):
                at = pl.multiple_of(where_ref[2 * (n % count) + part], 64)
                weight_ref[n // count, pl.ds(at, half), :] = piece[part * half : (part + 1) * half, :]
        row = lax.broadcasted_iota(jnp.int32, (8, LANES), 0)
        lane = lax.broadcasted_iota(jnp.int32, (8, LANES), 1)
        pick = jnp.where(row == lane, 1.0, 0.0).astype(BF)
        gains_ref[...] = nt(pick, weight_ref[0][:, 4 * HEAD :])

    for k in range(4):

        @pl.when(step == k)
        def _():
            x_ref[...] = (x0, x1)[k][...] if k < 2 else x_far[(k - 2) * PIECE : (k - 1) * PIECE, :]

    x = x_ref[...].astype(F32)
    r = lax.rsqrt(jnp.mean(x * x, axis=-1, keepdims=True) + epsilon)
    normed = (x * r * gains_ref[0:1, :]).astype(BF)
    norm_ref[0] = normed
    cosine, sine = cos_ref[0], sin_ref[0]
    packs = []
    for j in range(2):
        pre = nn(normed, weight_ref[j][:, 0 : 4 * HEAD])
        for h in range(2):
            turned = turn(widen(pre[:, h * HEAD : (h + 1) * HEAD]), cosine, sine)
            query_ref[j, 0, h * PIECE : (h + 1) * PIECE] = (turned * (score_scale * log2_e)).astype(BF)
        packs.append(turn(widen(pre[:, 2 * HEAD : 3 * HEAD]), cosine, sine)[:, 0:HEAD])
        packs.append(pre[:, 3 * HEAD :])
    kv_ref[...] = jnp.concatenate(packs, 1).astype(BF)


def project_qkv(where, pieces, x_rows, x_far, cos_table, sin_table):
    rows, width = x_rows[0].shape
    n_cols = pieces[0].shape[1]
    table = pl.BlockSpec((1, rows, LANES), lambda i, *_: (i, 0, 0))
    return pl.pallas_call(
        functools.partial(qkv_kernel, len(pieces) // 2),
        grid_spec=pltpu.PrefetchScalarGridSpec(
            num_scalar_prefetch=1,
            grid=(4,),
            in_specs=[pl.BlockSpec(v.shape, lambda i, *_: (0, 0)) for v in (*pieces, *x_rows, x_far)] + [table, table],
            out_specs=[
                pl.BlockSpec((1, rows, width), lambda i, *_: (i, 0, 0)),
                pl.BlockSpec((2, 1, 2 * rows, LANES), lambda i, *_: (0, i, 0, 0)),
                pl.BlockSpec((rows, 4 * HEAD), lambda i, *_: (i, 0)),
                pl.BlockSpec((2, width, n_cols), lambda i, *_: (0, 0, 0)),
                pl.BlockSpec((8, width), lambda i, *_: (0, 0)),
            ],
            scratch_shapes=[pltpu.VMEM((rows, width), BF)],
        ),
        out_shape=[
            jax.ShapeDtypeStruct((4, rows, width), BF),
            jax.ShapeDtypeStruct((2, 4, 2 * rows, LANES), BF),
            jax.ShapeDtypeStruct((4 * rows, 4 * HEAD), BF),
            jax.ShapeDtypeStruct((2, width, n_cols), BF),
            jax.ShapeDtypeStruct((8, width), F32),
        ],
        compiler_params=params(48),
        cost_estimate=cost(8),
        name="project_qkv",
    )(where, *pieces, *x_rows, x_far, cos_table, sin_table)


def query_back_kernel(core_ref, dq_ref, weight_ref, cos_ref, sin_ref, grad_ref, share_ref):
    total = None
    for j in range(2):
        heads = []
        for h in range(2):
            turned = unturn(dq_ref[j, 0, h * PIECE : (h + 1) * PIECE], cos_ref[0], sin_ref[0])
            heads.append((turned * score_scale)[:, 0:HEAD])
        grad = jnp.concatenate(heads, 1).astype(BF)
        grad_ref[j, 0] = grad
        term = nt(grad, weight_ref[j][:, 0 : 2 * HEAD])
        total = term if total is None else total + term
    share_ref[0] = total.astype(BF)


def kv_back_kernel(n_same, has_above, core_ref, *refs):
    refs = list(refs)
    own_ref, first_ref, second_ref = refs[:3]
    same_refs = refs[3 : 3 + n_same]
    refs = refs[3 + n_same :]
    i = pl.program_id(0)
    late = i >= 2
    d_kv = own_ref[...] + jnp.where(late, second_ref[...], first_ref[...]).astype(F32)
    for ref in same_refs:
        d_kv = d_kv + ref[...].astype(F32)
    if has_above:
        d_kv = d_kv + jnp.where(i == core_ref[0], refs.pop(0)[...], 0).astype(F32)
    share_in_ref, weight_ref, cos_ref, sin_ref, grad_ref, share_ref = refs
    total = share_in_ref[0].astype(F32)
    for j in range(2):
        both = d_kv[:, 2 * HEAD * j : 2 * HEAD * (j + 1)]
        turned = unturn(widen(both[:, 0:HEAD]), cos_ref[0], sin_ref[0]) * (1.0 / log2_e)
        grad = jnp.concatenate([turned[:, 0:HEAD], both[:, HEAD:]], 1).astype(BF)
        grad_ref[j, 0] = grad
        total = total + nt(grad, weight_ref[j][:, 2 * HEAD : 4 * HEAD])
    share_ref[0] = total.astype(BF)


def project_back(kernel, core, args, specs, weights, cos_table, sin_table, name):
    count, rows, _ = cos_table.shape
    width = weights.shape[1]
    piece = pl.BlockSpec((1, rows, width), lambda i, *_: (i, 0, 0))
    table = pl.BlockSpec((1, rows, cos_table.shape[2]), lambda i, *_: (i, 0, 0))
    return pl.pallas_call(
        kernel,
        grid_spec=pltpu.PrefetchScalarGridSpec(
            num_scalar_prefetch=1,
            grid=(count,),
            in_specs=specs + [pl.BlockSpec((2, width, 4 * HEAD), lambda i, *_: (0, 0, 0)), table, table],
            out_specs=[pl.BlockSpec((2, 1, rows, 2 * HEAD), lambda i, *_: (0, i, 0, 0)), piece],
        ),
        out_shape=[
            jax.ShapeDtypeStruct((2, count, rows, 2 * HEAD), BF),
            jax.ShapeDtypeStruct((count, rows, width), BF),
        ],
        compiler_params=params(40),
        cost_estimate=cost(4),
        name=name,
    )(core, *args, weights, cos_table, sin_table)


def query_back(core, d_query, weights, cos_table, sin_table):
    spec = pl.BlockSpec((2, 1, 2 * PIECE, LANES), lambda i, *_: (0, i, 0, 0))
    return project_back(query_back_kernel, core, [d_query], [spec], weights, cos_table, sin_table, "query_back")


def kv_back(core, own, other, same, above, shares, weights, cos_table, sin_table):
    rows = pl.BlockSpec((PIECE, 4 * HEAD), lambda i, *_: (i, 0))
    chunk = pl.BlockSpec((PIECE, 4 * HEAD), lambda i, *_: (i % 2, 0))
    args = [own, *other, *same, *above, shares]
    specs = [rows, chunk, chunk] + [rows] * len(same)
    specs += [pl.BlockSpec((PIECE, 4 * HEAD), lambda i, *_: (0, 0))] * len(above)
    specs.append(pl.BlockSpec((1, *shares.shape[1:]), lambda i, *_: (i, 0, 0)))
    kernel = functools.partial(kv_back_kernel, len(same), bool(above))
    return project_back(kernel, core, args, specs, weights, cos_table, sin_table, "kv_back")


CHUNK = 2 * PIECE


def unpack_kv(swaps, block_refs, key_scratch, value_scratch):
    lane = lax.broadcasted_iota(jnp.int32, (CHUNK, LANES - HEAD), 1)
    ones = jnp.where(lane < 3, 1.0, 0.0).astype(BF)
    at = 0
    for swap, ref in zip(swaps, block_refs):
        for start in range(0, ref.shape[0], CHUNK):
            block = ref[start : start + CHUNK, :]
            for j in range(2):
                first = 2 * HEAD * (j ^ swap)
                k = block[:, first : first + HEAD]
                v = block[:, first + HEAD : first + 2 * HEAD]
                key_scratch[j, at : at + CHUNK, :] = jnp.concatenate([k, ones], 1)
                value_scratch[j, at : at + CHUNK, :] = jnp.concatenate([v, ones], 1)
            at += CHUNK


def chunk_state(info_ref, base, i):
    last = base + (CHUNK - 1)
    touched = (base <= info_ref[i, 3]) & (last >= info_ref[i, 0])
    full = (base >= info_ref[i, 1]) & (last <= info_ref[i, 2])
    return touched, full


def forward_kernel(swaps, first, last, info_ref, base_ref, zl_ref, *refs):
    refs = list(refs)
    n_blocks = len(swaps)
    query_ref, low_ref, high_ref = refs[:3]
    block_refs = refs[3 : 3 + n_blocks]
    refs = refs[3 + n_blocks :]
    if not first:
        acc_in = refs.pop(0)
    if last:
        mixed_ref = refs.pop(0)
    kept_ref = refs.pop(0)
    key_scratch, value_scratch, acc, top = refs
    i = pl.program_id(0)

    @pl.when(i == 0)
    def _():
        unpack_kv(swaps, block_refs, key_scratch, value_scratch)

    for j in range(2):
        if first:
            acc[j] = jnp.zeros((CHUNK, LANES), F32)
            top[j] = jnp.full((CHUNK, LANES), negative, F32)
        else:
            acc[j] = acc_in[j, 0]
            top[j] = jnp.broadcast_to(acc_in[j, 0][:, HEAD + 1 : HEAD + 2], (CHUNK, LANES))
    n_chunks = sum(r.shape[0] for r in block_refs) // CHUNK

    def visit(n, masked):
        rows = pl.ds(pl.multiple_of(n * CHUNK, CHUNK), CHUNK)
        if masked:
            at = lax.broadcasted_iota(jnp.int32, (PIECE, CHUNK), 1)
            token = base_ref[n] + lax.rem(at + zl_ref[0] * PIECE, CHUNK)
            low = jnp.concatenate([low_ref[0]] * (CHUNK // LANES), 1)
            high = jnp.concatenate([high_ref[0]] * (CHUNK // LANES), 1)
            allowed = (token >= low) & (token <= high)
        for j in range(2):
            scores = nt(query_ref[j, 0], key_scratch[j, rows, :])
            if masked:
                scores = jnp.concatenate(
                    [jnp.where(allowed, scores[h * PIECE : (h + 1) * PIECE], negative) for h in range(2)], 0
                )
            old = top[j]
            new = jnp.maximum(old, jnp.max(scores, axis=1, keepdims=True))
            top[j] = new
            probs = jnp.exp2(scores - jnp.concatenate([new] * (CHUNK // LANES), 1)).astype(BF)
            acc[j] = acc[j] * jnp.exp2(old - new) + nn(probs, value_scratch[j, rows, :])

    @pl.loop(0, n_chunks)
    def _(n):
        touched, full = chunk_state(info_ref, base_ref[n], i)

        @pl.when(touched & full)
        def _():
            visit(n, False)

        @pl.when(touched & jnp.logical_not(full))
        def _():
            visit(n, True)

    lane = lax.broadcasted_iota(jnp.int32, (CHUNK, LANES), 1)
    if last:
        for j in range(2):
            total = acc[j][:, HEAD : HEAD + 1]
            out = acc[j] / total
            kept_ref[j, 0] = jnp.where(lane < HEAD, out, top[j] + jnp.log2(total))
            mixed_ref[j, 0] = jnp.concatenate([out[0:PIECE, 0:HEAD], out[PIECE:, 0:HEAD]], 1).astype(BF)
    else:
        for j in range(2):
            kept_ref[j, 0] = jnp.where(lane == HEAD + 1, top[j], acc[j])


def attend(query, low, high, info, bases, zl, blocks, swaps, state, last):
    count = query.shape[1]
    n_keys = sum(b.shape[0] for b in blocks)
    per_piece = pl.BlockSpec((2, 1, CHUNK, LANES), lambda i, *_: (0, i, 0, 0))
    bound = pl.BlockSpec((1, PIECE, LANES), lambda i, *_: (i, 0, 0))
    in_specs = [per_piece, bound, bound]
    in_specs += [pl.BlockSpec(b.shape, lambda i, *_: (0, 0)) for b in blocks]
    args = [query, low, high, *blocks]
    if state is not None:
        in_specs.append(per_piece)
        args.append(state)
    wide = jax.ShapeDtypeStruct((2, count, CHUNK, LANES), F32)
    if last:
        out_shape = [jax.ShapeDtypeStruct((2, count, PIECE, 2 * HEAD), BF), wide]
        out_specs = [pl.BlockSpec((2, 1, PIECE, 2 * HEAD), lambda i, *_: (0, i, 0, 0)), per_piece]
    else:
        out_shape = wide
        out_specs = per_piece
    return pl.pallas_call(
        functools.partial(forward_kernel, swaps, state is None, last),
        grid_spec=pltpu.PrefetchScalarGridSpec(
            num_scalar_prefetch=3,
            grid=(count,),
            in_specs=in_specs,
            out_specs=out_specs,
            scratch_shapes=[
                pltpu.VMEM((2, n_keys, LANES), BF),
                pltpu.VMEM((2, n_keys, LANES), BF),
                pltpu.VMEM((2, CHUNK, LANES), F32),
                pltpu.VMEM((2, CHUNK, LANES), F32),
            ],
        ),
        out_shape=out_shape,
        compiler_params=params(48),
        cost_estimate=cost(n_keys / 100),
        name="attend",
    )(info, bases, zl, *args)


def split_three(value):
    first = value.astype(BF)
    rest = value - first.astype(F32)
    second = rest.astype(BF)
    third = (rest - second.astype(F32)).astype(BF)
    return first, second, third


def augment(wide, extra):
    lane = lax.broadcasted_iota(jnp.int32, wide.shape, 1)
    a, b, c = (part.astype(F32) for part in split_three(extra))
    out = wide.astype(F32)
    out = jnp.where(lane == HEAD, a, out)
    out = jnp.where(lane == HEAD + 1, b, out)
    out = jnp.where(lane == HEAD + 2, c, out)
    return out.astype(BF)


def prepare_kernel(m0, m1, m2, m3, w0, w1, kept_ref, query_ref, q_aug_ref, o_aug_ref, mid_ref):
    step = pl.program_id(0)
    for k, ref in enumerate((m0, m1, m2, m3)):

        @pl.when(step == k)
        def _():
            mid_ref[...] = ref[...]

    mid = mid_ref[...]
    for j, weight_ref in enumerate((w0, w1)):
        grad = nn(mid, weight_ref[...][:, 0 : 2 * HEAD])
        wide = jnp.concatenate([widen(grad[:, 0:HEAD]), widen(grad[:, HEAD : 2 * HEAD])], 0).astype(BF)
        kept = kept_ref[j, 0]
        delta = jnp.sum(wide.astype(F32) * kept, axis=1, keepdims=True)
        q_aug_ref[j, 0] = augment(query_ref[j, 0], -kept[:, HEAD : HEAD + 1])
        o_aug_ref[j, 0] = augment(wide, -delta)


def prepare_back(mid, weights, tile, kept, query):
    count = len(mid)
    rows, width = mid[0].shape
    per_piece = pl.BlockSpec((2, 1, CHUNK, LANES), lambda i: (0, i, 0, 0))
    return pl.pallas_call(
        prepare_kernel,
        grid=(count,),
        in_specs=[pl.BlockSpec((rows, width), lambda i: (0, 0))] * count
        + [pl.BlockSpec((width, 256), lambda i: (0, tile))] * 2
        + [per_piece, per_piece],
        out_specs=[per_piece, per_piece],
        out_shape=[jax.ShapeDtypeStruct(query.shape, BF)] * 2,
        scratch_shapes=[pltpu.VMEM((rows, width), BF)],
        compiler_params=params(40),
        cost_estimate=cost(6),
        name="prepare_back",
    )(*mid, *weights, kept, query)


def backward_kernel(swaps, has_dq, info_ref, base_ref, zl_ref, *refs):
    refs = list(refs)
    n_blocks = len(swaps)
    q_aug, o_aug, low_ref, high_ref = refs[:4]
    block_refs = refs[4 : 4 + n_blocks]
    refs = refs[4 + n_blocks :]
    if has_dq:
        dq_in = refs.pop(0)
    dq_ref = refs.pop(0)
    out_refs = refs[:n_blocks]
    key_scratch, value_scratch, d_key, d_value = refs[n_blocks:]
    i = pl.program_id(0)

    @pl.when(i == 0)
    def _():
        unpack_kv(swaps, block_refs, key_scratch, value_scratch)
        d_key[...] = jnp.zeros(d_key.shape, F32)
        d_value[...] = jnp.zeros(d_value.shape, F32)

    for j in range(2):
        if has_dq:
            dq_ref[j, 0] = dq_in[j, 0]
        else:
            dq_ref[j, 0] = jnp.zeros((CHUNK, LANES), F32)
    n_chunks = sum(r.shape[0] for r in block_refs) // CHUNK

    def visit(n, masked):
        rows = pl.ds(pl.multiple_of(n * CHUNK, CHUNK), CHUNK)
        if masked:
            at = lax.broadcasted_iota(jnp.int32, (CHUNK, CHUNK), 0)
            token = base_ref[n] + lax.rem(at + zl_ref[0] * PIECE, CHUNK)
            allowed = (token >= low_ref[0, 0:1, :]) & (token <= high_ref[0, 0:1, :])
        for j in range(2):
            keys = key_scratch[j, rows, :]
            probs = jnp.exp2(nt(keys, q_aug[j, 0]))
            if masked:
                probs = jnp.where(allowed, probs, 0.0)
            d_probs = nt(value_scratch[j, rows, :], o_aug[j, 0])
            low_probs = probs.astype(BF)
            d_scores = (probs * d_probs).astype(BF)
            d_value[j, rows, :] += nn(low_probs, o_aug[j, 0])
            d_key[j, rows, :] += nn(d_scores, q_aug[j, 0])
            dq_ref[j, 0] += tn(d_scores, keys)

    @pl.loop(0, n_chunks)
    def _(n):
        touched, full = chunk_state(info_ref, base_ref[n], i)

        @pl.when(touched & full)
        def _():
            visit(n, False)

        @pl.when(touched & jnp.logical_not(full))
        def _():
            visit(n, True)

    @pl.when(i == pl.num_programs(0) - 1)
    def _():
        at = 0
        for swap, ref in zip(swaps, out_refs):
            for start in range(0, ref.shape[0], CHUNK):
                parts = []
                for j in (swap, 1 - swap):
                    parts.append(d_key[j, at : at + CHUNK, :][:, 0:HEAD])
                    parts.append(d_value[j, at : at + CHUNK, :][:, 0:HEAD])
                ref[start : start + CHUNK, :] = jnp.concatenate(parts, 1).astype(ref.dtype)
                at += CHUNK


def attend_back(q_aug, o_aug, low, high, info, bases, zl, blocks, swaps, d_query, kinds):
    count = q_aug.shape[1]
    n_keys = sum(b.shape[0] for b in blocks)
    per_piece = pl.BlockSpec((2, 1, CHUNK, LANES), lambda i, *_: (0, i, 0, 0))
    bound = pl.BlockSpec((1, 8, CHUNK), lambda i, *_: (i, 0, 0))
    whole = [pl.BlockSpec(b.shape, lambda i, *_: (0, 0)) for b in blocks]
    in_specs = [per_piece, per_piece, bound, bound, *whole]
    args = [q_aug, o_aug, low, high, *blocks]
    if d_query is not None:
        in_specs.append(per_piece)
        args.append(d_query)
    return pl.pallas_call(
        functools.partial(backward_kernel, swaps, d_query is not None),
        grid_spec=pltpu.PrefetchScalarGridSpec(
            num_scalar_prefetch=3,
            grid=(count,),
            in_specs=in_specs,
            out_specs=[per_piece, *whole],
            scratch_shapes=[
                pltpu.VMEM((2, n_keys, LANES), BF),
                pltpu.VMEM((2, n_keys, LANES), BF),
                pltpu.VMEM((2, n_keys, LANES), F32),
                pltpu.VMEM((2, n_keys, LANES), F32),
            ],
        ),
        out_shape=[jax.ShapeDtypeStruct((2, count, CHUNK, LANES), F32)]
        + [jax.ShapeDtypeStruct(b.shape, k) for b, k in zip(blocks, kinds)],
        compiler_params=params(56),
        cost_estimate=cost(n_keys / 64),
        name="attend_back",
    )(info, bases, zl, *args)


def ffn_kernel(tiles, n0, n1, g0, g1, *refs):
    own_refs, other_refs, refs = refs[0:3], refs[3:6], refs[6:]
    o0, o1, b0, b1, hidden_ref, dg_ref, du_ref, norm_t, grad_t, norm_ref, grad_ref, acc_out, acc_back = refs
    step = pl.program_id(0)

    @pl.when(step == 0)
    def _():
        norm_ref[0:PIECE] = n0[...]
        norm_ref[PIECE:] = n1[...]
        grad_ref[0:PIECE] = g0[...]
        grad_ref[PIECE:] = g1[...]

    def run(gate_ref, up_ref, down_ref, first):
        gate_w, up_w, down_w = gate_ref[...], up_ref[...], down_ref[...]
        gate = nn(norm_ref[...], gate_w)
        up = nn(norm_ref[...], up_w)
        d_hidden = nn(grad_ref[...], down_w)
        sig = jax.nn.sigmoid(gate)
        silu = gate * sig
        hidden = (silu * up).astype(BF)
        d_gate = (d_hidden * up * sig * (1.0 + gate * (1.0 - sig))).astype(BF)
        d_up = (d_hidden * silu).astype(BF)
        hidden_ref[...] = hidden
        dg_ref[...] = d_gate
        du_ref[...] = d_up
        norm_t[...] = norm_ref[pl.ds(pl.multiple_of(step * LANES, LANES), LANES), :].T
        grad_t[...] = grad_ref[pl.ds(pl.multiple_of(step * LANES, LANES), LANES), :].T
        out = nt(hidden, down_w)
        back = nt(d_gate, gate_w) + nt(d_up, up_w)
        if first:
            acc_out[...] = out
            acc_back[...] = back
        else:
            acc_out[...] += out
            acc_back[...] += back

    @pl.when(step == 0)
    def _():
        run(*own_refs, True)

    @pl.when((step > 0) & (step < tiles))
    def _():
        run(*own_refs, False)

    @pl.when(step >= tiles)
    def _():
        run(*other_refs, False)

    @pl.when(step == pl.num_programs(0) - 1)
    def _():
        o0[...] = acc_out[0:PIECE].astype(BF)
        o1[...] = acc_out[PIECE:].astype(BF)
        b0[...] = acc_back[0:PIECE].astype(BF)
        b1[...] = acc_back[PIECE:].astype(BF)


def feed_forward(norm_rows, grad_rows, own, other):
    rows, width = norm_rows[0].shape
    half = 512
    tile = 256
    tiles = half // tile
    whole = pl.BlockSpec((rows, width), lambda s: (0, 0))

    def own_spec(at):
        return pl.BlockSpec((width, tile), lambda s: (0, at // tile + jnp.minimum(s, tiles - 1)))

    def other_spec(at):
        return pl.BlockSpec((width, tile), lambda s: (0, at // tile + jnp.maximum(s - tiles, 0)))

    hid = pl.BlockSpec((2 * rows, tile), lambda s: (0, s))
    turned = pl.BlockSpec((width, LANES), lambda s: (0, s))
    return pl.pallas_call(
        functools.partial(ffn_kernel, tiles),
        grid=(2 * tiles,),
        in_specs=[whole] * 4 + [own_spec(at) for _, at in own] + [other_spec(at) for _, at in other],
        out_specs=[whole] * 4 + [hid] * 3 + [turned] * 2,
        out_shape=[jax.ShapeDtypeStruct((rows, width), BF)] * 4
        + [jax.ShapeDtypeStruct((2 * rows, 2 * half), BF)] * 3
        + [jax.ShapeDtypeStruct((width, 2 * rows), BF)] * 2,
        scratch_shapes=[pltpu.VMEM((2 * rows, width), BF)] * 2 + [pltpu.VMEM((2 * rows, width), F32)] * 2,
        compiler_params=params(56),
        cost_estimate=cost(18),
        name="feed_forward",
    )(*norm_rows, *grad_rows, *(w for w, _ in own), *(w for w, _ in other))


def weight_grad_kernel(n_jobs, *refs):
    out_ref = refs[-1]
    for n in range(n_jobs):
        left_early, left_late, early, late = refs[4 * n : 4 * n + 4]

        @pl.when(pl.program_id(1) == n)
        def _():
            total = nn(left_early[...], early[...]) + nn(left_late[...], late[...])
            out_ref[...] = total.astype(BF)


def weight_grad(jobs, us):
    width, depth = jobs[0][0].shape
    half = jobs[0][2].shape[1] // 2
    count = len(jobs)
    left = pl.BlockSpec((width, depth), lambda s, n: (0, 0))
    cols = pl.BlockSpec((depth, half), lambda s, n: (0, s))
    return pl.pallas_call(
        functools.partial(weight_grad_kernel, count),
        grid=(2, count),
        in_specs=[left, left, cols, cols] * count,
        out_specs=pl.BlockSpec((width, half), lambda s, n: (0, s * count + n)),
        out_shape=jax.ShapeDtypeStruct((width, 2 * count * half), BF),
        compiler_params=params(48),
        cost_estimate=cost(us),
        name="weight_grad",
    )(*(value for job in jobs for value in job))


def head_grad_kernel(l0, l1, l2, l3, right_ref, out_ref):
    for j in range(2):
        total = None
        for k, left in enumerate((l0, l1, l2, l3)):
            term = tn(left[...], right_ref[j, k])
            total = term if total is None else total + term
        wide = jnp.concatenate([total, jnp.zeros((total.shape[0], 256 - 2 * HEAD), F32)], 1)
        out_ref[:, j * 256 : (j + 1) * 256] = wide.astype(BF)


def head_grad(left, right):
    rows, width = left[0].shape
    tile = 512
    return pl.pallas_call(
        head_grad_kernel,
        grid=(width // tile,),
        in_specs=[pl.BlockSpec((rows, tile), lambda s: (0, s))] * 4 + [pl.BlockSpec(right.shape, lambda s: (0, 0, 0, 0))],
        out_specs=pl.BlockSpec((tile, 512), lambda s: (s, 0)),
        out_shape=jax.ShapeDtypeStruct((width, 512), BF),
        compiler_params=params(40),
        cost_estimate=cost(3),
        name="head_grad",
    )(*left, right)


def gain_kernel(lane, *refs):
    out_ref = refs[-1]
    count = (len(refs) - 1) // 2
    at = lax.broadcasted_iota(jnp.int32, (PIECE, LANES), 1)
    pick = jnp.where(at == lane, 1.0, 0.0).astype(BF)
    total = None
    for share, normed in zip(refs[:count], refs[count : 2 * count]):
        product = (share[...].astype(F32) * normed[...].astype(F32)).astype(BF)
        term = tn(product, pick)
        total = term if total is None else total + term
    out_ref[...] = total


def gain_columns(shares, normed, lane):
    rows, width = shares[0].shape
    tile = 512
    spec = pl.BlockSpec((rows, tile), lambda s: (0, s))
    return pl.pallas_call(
        functools.partial(gain_kernel, lane),
        grid=(width // tile,),
        in_specs=[spec] * 8,
        out_specs=pl.BlockSpec((tile, LANES), lambda s: (s, 0)),
        out_shape=jax.ShapeDtypeStruct((width, LANES), F32),
        compiler_params=params(40),
        cost_estimate=cost(3),
        name="gain_columns",
    )(*shares, *normed)


def kv_grad_kernel(norm_ref, share_ref, dkv_ref, column_ref, *refs):
    out_ref = refs[-1]
    at = lax.broadcasted_iota(jnp.int32, (PIECE, LANES), 1)
    pick = jnp.where(at == 0, 1.0, 0.0).astype(BF)
    columns = column_ref[...]
    totals = [None, None]
    for k in range(4):
        normed = norm_ref[k]
        product = (share_ref[k].astype(F32) * normed.astype(F32)).astype(BF)
        columns = columns + tn(product, pick)
        for j in range(2):
            term = tn(normed, dkv_ref[j, k])
            totals[j] = term if totals[j] is None else totals[j] + term
    for j in range(2):
        out_ref[:, j * 256 : (j + 1) * 256] = jnp.concatenate([totals[j], columns[:, 0 : 256 - 2 * HEAD]], 1).astype(BF)


def kv_grad(normed, shares, d_kvs, columns):
    count, rows, width = normed.shape
    tile = 512
    spec = pl.BlockSpec((count, rows, tile), lambda s: (0, 0, s))
    return pl.pallas_call(
        kv_grad_kernel,
        grid=(width // tile,),
        in_specs=[
            spec,
            spec,
            pl.BlockSpec(d_kvs.shape, lambda s: (0, 0, 0, 0)),
            pl.BlockSpec((tile, LANES), lambda s: (s, 0)),
        ],
        out_specs=pl.BlockSpec((tile, 512), lambda s: (s, 0)),
        out_shape=jax.ShapeDtypeStruct((width, 512), BF),
        compiler_params=params(40),
        cost_estimate=cost(4),
        name="kv_grad",
    )(normed, shares, d_kvs, columns)


def output_kernel(mixed_ref, w0, w1, far_ref, near_ref):
    step = pl.program_id(0)
    total = None
    for j, weight in enumerate((w0, w1)):
        heads = jnp.concatenate([mixed_ref[j, 0], mixed_ref[j, 1]], 0)
        term = nt(heads, weight[...][:, 0 : 2 * HEAD])
        total = term if total is None else total + term

    @pl.when(step == 0)
    def _():
        far_ref[...] = total.astype(BF)

    @pl.when(step == 1)
    def _():
        near_ref[...] = total


def output_projection(mixed, weights, tile):
    _, count, rows, width_heads = mixed.shape
    width = weights[0].shape[0]
    whole = pl.BlockSpec((2 * rows, width), lambda s: (0, 0))
    return pl.pallas_call(
        output_kernel,
        grid=(2,),
        in_specs=[pl.BlockSpec((2, 2, rows, width_heads), lambda s: (0, 1 - s, 0, 0))]
        + [pl.BlockSpec((width, 256), lambda s: (0, tile))] * 2,
        out_specs=[whole, whole],
        out_shape=[jax.ShapeDtypeStruct((2 * rows, width), BF), jax.ShapeDtypeStruct((2 * rows, width), F32)],
        compiler_params=params(40),
        cost_estimate=cost(4),
        name="output_projection",
    )(mixed, *weights)


def add_kernel(near_ref, across_ref, out_ref):
    out_ref[...] = (near_ref[...].astype(F32) + across_ref[...].astype(F32)).astype(BF)


def add_rows(near, near_at, across, across_at):
    rows, width = PIECE, near.shape[1]
    return pl.pallas_call(
        add_kernel,
        grid=(1,),
        in_specs=[
            pl.BlockSpec((rows, width), lambda s: (near_at, 0)),
            pl.BlockSpec((rows, width), lambda s: (across_at, 0)),
        ],
        out_specs=pl.BlockSpec((rows, width), lambda s: (0, 0)),
        out_shape=jax.ShapeDtypeStruct((rows, width), BF),
        compiler_params=params(32),
        cost_estimate=cost(1),
        name="add_rows",
    )(near, across)


def forward_norm_kernel(x_ref, near_ref, across_ref, beside_ref, gain_ref, after_ref, norm_ref):
    rows = x_ref[...].astype(F32) + (near_ref[...] + across_ref[...].astype(F32) + beside_ref[...].astype(F32))
    after_ref[...] = rows
    r = lax.rsqrt(jnp.mean(rows * rows, axis=-1, keepdims=True) + epsilon)
    norm_ref[...] = (rows * r * gain_ref[1:2, :]).astype(BF)


def row_specs(width, n):
    return [pl.BlockSpec((LANES, width), lambda i: (i, 0))] * n


def forward_norm(x, near, across, beside, gain_rows):
    rows, width = x.shape
    return pl.pallas_call(
        forward_norm_kernel,
        grid=(rows // LANES,),
        in_specs=row_specs(width, 4) + [pl.BlockSpec((8, width), lambda i: (0, 0))],
        out_specs=row_specs(width, 2),
        out_shape=[jax.ShapeDtypeStruct((rows, width), F32), jax.ShapeDtypeStruct((rows, width), BF)],
        compiler_params=params(32),
        cost_estimate=cost(2),
        name="forward_norm",
    )(x, near, across, beside, gain_rows)


def backward_norm_kernel(which, share_ref, across_ref, beside_ref, rows_ref, base_ref, gain_ref, *out_refs):
    upstream = share_ref[...].astype(F32) + across_ref[...].astype(F32) + beside_ref[...].astype(F32)
    rows = rows_ref[...].astype(F32)
    r = lax.rsqrt(jnp.mean(rows * rows, axis=-1, keepdims=True) + epsilon)
    weighted = upstream * gain_ref[which : which + 1, :]
    inner = jnp.mean(weighted * rows, axis=-1, keepdims=True)
    out = base_ref[...].astype(F32) + (r * weighted - rows * (r * r * r) * inner)
    for ref in out_refs:
        ref[...] = out.astype(ref.dtype)


def backward_norm(which, share, across, beside, rows, base, gain_rows, kinds):
    count, width = rows.shape
    return pl.pallas_call(
        functools.partial(backward_norm_kernel, which),
        grid=(count // LANES,),
        in_specs=row_specs(width, 5) + [pl.BlockSpec((8, width), lambda i: (0, 0))],
        out_specs=row_specs(width, len(kinds)),
        out_shape=[jax.ShapeDtypeStruct((count, width), kind) for kind in kinds],
        compiler_params=params(32),
        cost_estimate=cost(2),
        name="backward_norm",
    )(share, across, beside, rows, base, gain_rows)


def token_tables(token, seq_lengths, piece_starts):
    n = seq_lengths.shape[0]
    upto = jnp.arange(n)[None, :] <= jnp.arange(n)[:, None]
    ends = jnp.sum(jnp.where(upto, seq_lengths[None, :], 0), axis=1)
    after = token[:, None] >= ends[None, :]
    start = jnp.sum(jnp.where(after, seq_lengths[None, :], 0), axis=1)
    end = jnp.min(jnp.where(after, far_away, ends[None, :]), axis=1)
    inside = (token[:, None] >= piece_starts[None, :]) & (token[:, None] < piece_starts[None, :] + PIECE)
    piece_end = jnp.max(jnp.where(inside, piece_starts[None, :] + PIECE, 0), axis=1)
    high = jnp.maximum(token, jnp.minimum(piece_end, end) - 1)
    return start, high


def may_meet(one, two, group_tokens, count):
    total = group_tokens * count
    regions = ((0, LEN_FIRST, LEN_FIRST), (LEN_FIRST, total - LEN_LAST, LEN_MAX), (total - LEN_LAST, total, LEN_LAST))
    for start, end, longest in regions:
        both = all(g * group_tokens < end and (g + 1) * group_tokens > start for g in (one, two))
        if both and (abs(one - two) - 1) * group_tokens + 1 < longest:
            return True
    return False


def body(
    inputs,
    first_gain,
    query_weight,
    key_matrix,
    value_matrix,
    output_weight,
    second_gain,
    gate_weight,
    up_weight,
    down_weight,
    seq_lengths,
    piece_starts,
    out_cotangent,
):
    g, c, zh, zl = (lax.axis_index(a) for a in AXES)
    groups = lax.axis_size("g")
    rows, width = inputs.shape
    span = 4 * rows
    group_tokens = 2 * span
    shard_rows = query_weight.shape[0]

    order = jnp.arange(4)
    piece_base = (2 * g + (c ^ (order >> 1))) * span + zh * CHUNK + (zl ^ (order & 1)) * rows
    token = (piece_base[:, None] + jnp.arange(rows)[None, :]).reshape(-1).astype(jnp.int32)
    low, high = token_tables(token, seq_lengths, piece_starts)
    position = (token - low).astype(F32)
    low, high = low.reshape(4, rows), high.reshape(4, rows)
    info = jnp.stack([low.min(1), low.max(1), high.min(1), high.max(1)], 1).astype(jnp.int32)
    low_wide = jnp.broadcast_to(low[:, :, None], (4, rows, LANES)).astype(jnp.int32)
    high_wide = jnp.broadcast_to(high[:, :, None], (4, rows, LANES)).astype(jnp.int32)
    low_rows = jnp.broadcast_to(jnp.tile(low, (1, 2))[:, None, :], (4, 8, CHUNK)).astype(jnp.int32)
    high_rows = jnp.broadcast_to(jnp.tile(high, (1, 2))[:, None, :], (4, 8, CHUNK)).astype(jnp.int32)
    zl_info = jnp.reshape(zl, (1,)).astype(jnp.int32)
    frequency = rope_base ** (-(2.0 / HEAD) * jnp.arange(HEAD // 2, dtype=F32))
    angles = position[:, None] * frequency[None, :]
    cosine, sine = jnp.cos(angles), jnp.sin(angles)
    pad = jnp.zeros((span, LANES - HEAD), F32)
    cos_table = jnp.concatenate([cosine, cosine, pad], 1).reshape(4, rows, LANES)
    sin_table = jnp.concatenate([-sine, sine, pad], 1).reshape(4, rows, LANES)

    def halves(matrix):
        return matrix.reshape(matrix.shape[0], 2, -1).transpose(1, 0, 2)

    blank = functools.partial(jnp.zeros, dtype=BF)
    half = gate_weight.shape[1] // 2
    zl_info = jnp.reshape(zl, (1,)).astype(jnp.int32)
    core = jnp.reshape(2 * c + zl, (1,)).astype(jnp.int32)
    shard_pair = 2 * shard_rows

    gains = jnp.broadcast_to(jnp.stack([first_gain, second_gain], 1)[None], (2, shard_rows, 2))
    qkv_shard = jnp.concatenate(
        [halves(query_weight), halves(key_matrix), halves(value_matrix), gains, blank((2, shard_rows, 126))], 2
    )
    qkv_keep, qkv_got = split_core(qkv_shard)
    ffn_shard = jnp.concatenate(
        [halves(gate_weight), halves(output_weight.T), blank((2, shard_rows, 64)), halves(up_weight), halves(down_weight.T)],
        2,
    )
    ffn_keep, ffn_got = split_core(ffn_shard)
    qkv_pair = jnp.concatenate([qkv_keep, qkv_got], 0)
    inputs, out_cotangent, qkv_pair, ffn_keep, ffn_got = sync(inputs, out_cotangent, qkv_pair, ffn_keep, ffn_got)

    qkv_other = flip(qkv_pair, "zh")
    qkv_near = from_groups(qkv_pair)
    x_beside = flip(inputs, "zl")
    ffn_pair = in_order(ffn_keep, ffn_got)
    up_at = half + 2 * HEAD + 64
    first_pair = ffn_pair[:, :up_at]
    up_pair, down_pair = ffn_pair[:, up_at : up_at + half], ffn_pair[:, up_at + half :]
    (
        qkv_near, qkv_other, x_beside, ffn_pair, first_pair, up_pair, down_pair, cos_table, sin_table,
        info, low_wide, high_wide, low_rows, high_rows,
    ) = sync(
        qkv_near, qkv_other, x_beside, ffn_pair, first_pair, up_pair, down_pair, cos_table, sin_table,
        info, low_wide, high_wide, low_rows, high_rows,
    )
    x_near = jnp.concatenate([inputs, x_beside], 0)

    ffn_own = all_groups(ffn_pair)
    qkv_far = from_groups(qkv_other)
    x_far = flip(x_near, "c")
    first_other = flip(first_pair, "zh")
    qkv_far, x_far, first_other, up_pair = sync(qkv_far, x_far, first_other, up_pair)

    up_other = flip(up_pair, "zh")
    k_order = jnp.arange(groups)[:, None]
    piece_rows = (g ^ k_order) * shard_pair + (c ^ jnp.arange(2)[None, :]) * shard_rows
    norm_one, query, kv, qkv_w, gain_rows = project_qkv(
        piece_rows.reshape(-1).astype(jnp.int32),
        [*qkv_near, *qkv_far],
        [inputs, x_beside],
        x_far,
        cos_table,
        sin_table,
    )
    first_piece = lax.dynamic_slice_in_dim(kv, (2 * c + zl) * rows, rows, 0)
    norm_one, query, kv, qkv_w, gain_rows, kv_chunks, first_piece, out_cotangent, up_other, down_pair, first_other = sync(
        norm_one,
        query,
        kv,
        qkv_w,
        gain_rows,
        [kv[n * CHUNK : (n + 1) * CHUNK] for n in range(2)],
        first_piece,
        out_cotangent,
        up_other,
        down_pair,
        first_other,
    )
    first_far = all_groups(first_other)

    def chunk_bases(group, side):
        return jnp.stack([(2 * group + (c ^ i)) * span + side * CHUNK for i in range(2)]).astype(jnp.int32)

    def shift_pairs(steps):
        return [(s, s + steps) for s in range(groups) if 0 <= s + steps < groups and may_meet(s, s + steps, group_tokens, groups)]

    def present(pairs, bases):
        target = functools.reduce(jnp.logical_or, [g == t for _, t in pairs])
        return jnp.where(target, bases, far_away).astype(jnp.int32)

    def reverse(pairs):
        return [(t, s) for s, t in pairs]

    shifts = [d for d in range(1, groups) if shift_pairs(d)]
    above_groups = [s for s in range(1, groups) if may_meet(s - 1, s, group_tokens, groups)]
    above_pairs = [(2 * s, 2 * (s - 1) + 1) for s in above_groups]
    own_bases, other_bases = chunk_bases(g, zh), chunk_bases(g, 1 - zh)
    same_bases = [present(shift_pairs(d), chunk_bases(g - d, zh)) for d in shifts]
    far_bases = [present(shift_pairs(d), chunk_bases(g - d, 1 - zh)) for d in shifts]
    if above_groups:
        is_target = functools.reduce(jnp.logical_or, [(g == s - 1) & (zh == 1) for s in above_groups])
        far_bases.append(jnp.where(is_target, jnp.reshape(2 * (g + 1) * span, (1,)), far_away).astype(jnp.int32))
    same_bases, far_bases = jnp.concatenate(same_bases), jnp.concatenate(far_bases)

    def step(blocks, bases, swap, state, last=False):
        swaps = [swap] * len(blocks)
        return attend(query, low_wide, high_wide, info, bases, zl_info, blocks, swaps, state, last)

    other = [flip(kv_chunks[0], "zh")]
    same = [lax.ppermute(kv, "g", shift_pairs(d)) for d in shifts]
    g_beside, g_across = flip(out_cotangent, "zl"), flip(out_cotangent, "c")
    state = step([kv], own_bases, 0, None)
    other, same, g_beside, g_across, state, kv_late = sync(other, same, g_beside, g_across, state, kv_chunks[1])

    other.append(flip(kv_late, "zh"))
    far_blocks = [[lax.ppermute(other[0], "g", shift_pairs(d))] for d in shifts]
    g_both = flip(g_beside, "c")
    state = step(same, same_bases, 0, state)
    other, far_blocks, g_both, state, down_pair, first_piece, ffn_own = sync(
        other, far_blocks, g_both, state, down_pair, first_piece, ffn_own
    )

    for n, d in enumerate(shifts):
        far_blocks[n].append(lax.ppermute(other[1], "g", shift_pairs(d)))
    far_blocks = [b for pair in far_blocks for b in pair]
    if above_groups:
        above = lax.ppermute(first_piece, ("g", "zh"), above_pairs)
        far_blocks.append(lax.dynamic_update_slice(jnp.zeros((CHUNK, 4 * HEAD), BF), above, (zl * rows, 0)))
    down_other = flip(down_pair, "zh")
    state = step(other, other_bases, 1, state)
    far_blocks, down_other, state = sync(far_blocks, down_other, state)

    second_far = all_groups(jnp.concatenate([up_other, down_other], 1))
    mixed, kept = step(far_blocks, far_bases, 1, state, True)
    mixed, kept, first_far = sync(mixed, kept, first_far)

    o_tile = half // 256
    far_shares, near_shares = output_projection(mixed, (ffn_own, first_far), o_tile)
    across = flip(far_shares, "c")
    beside_sum = add_rows(near_shares, 1, across, 1)
    beside = flip(beside_sum, "zl")
    after_attn, norm_own = sync(*forward_norm(inputs, near_shares, across, beside, gain_rows))

    norm_beside, norm_across = flip(norm_own, "zl"), flip(norm_own, "c")
    near_w = [(ffn_own, 0), (ffn_own, up_at), (ffn_own, up_at + half)]
    far_w = [(first_far, 0), (second_far, 0), (second_far, half)]
    early = feed_forward([norm_own, norm_across], [out_cotangent, g_across], near_w, far_w)
    norm_beside, norm_across, early = sync(norm_beside, norm_across, early)
    norm_both = flip(norm_beside, "c")
    late = feed_forward([norm_beside, norm_both], [g_beside, g_both], near_w, far_w)
    late, norm_both = sync(late, norm_both)

    across_both = flip(late[3], "c")
    beside_sum = add_rows(late[2], 0, across_both, 0)
    beside_sum, late, early = sync(beside_sum, late, early)
    beside = flip(beside_sum, "zl")
    across = flip(early[3], "c")
    out_across = [flip(late[1], "c"), flip(early[1], "c")]
    gate_part = weight_grad([(early[7], late[7], early[5], late[5])], 4)
    beside, across, out_across, gate_part, early, late = sync(beside, across, out_across, gate_part, early, late)
    gate_sum = over_groups(gate_part)
    grad_mid, mid_low = backward_norm(1, early[2], across, beside, after_attn, out_cotangent, gain_rows, [F32, BF])
    grad_mid, mid_low, early, late = sync(grad_mid, mid_low, early, late)

    mid_beside, mid_across = flip(mid_low, "zl"), flip(mid_low, "c")
    up_down_part = weight_grad(
        [(early[7], late[7], early[6], late[6]), (early[8], late[8], early[4], late[4])], 8
    )
    out_sum = add_rows(late[0], 0, out_across[0], 0)
    mid_beside, mid_across, up_down_part, out_sum, early, late = sync(
        mid_beside, mid_across, up_down_part, out_sum, early, late
    )
    up_down_sum = over_groups(up_down_part)
    mid_rows = [mid_low, mid_beside, mid_across, flip(mid_beside, "c")]
    q_aug, o_aug = prepare_back(mid_rows, (ffn_own, first_far), o_tile, kept, query)
    q_aug, o_aug, mid_rows, out_sum, mixed, early, late = sync(q_aug, o_aug, mid_rows, out_sum, mixed, early, late)

    def step_back(blocks, bases, swap, d_query, kinds):
        swaps = [swap] * len(blocks)
        out = attend_back(q_aug, o_aug, low_rows, high_rows, info, bases, zl_info, blocks, swaps, d_query, kinds)
        return out[0], list(out[1:])

    def other_half(summed):
        return flip(summed[:, summed.shape[1] // 2 :], "zh")

    out_beside = flip(out_sum, "zl")
    d_query, d_far = step_back(far_blocks, far_bases, 1, None, [BF] * len(far_blocks))
    o_part = head_grad(mid_rows, mixed)
    second_column = gain_columns([early[2], late[2], early[3], late[3]], [norm_own, norm_beside, norm_across, norm_both], 1)
    out_beside, d_query, d_far, o_part, gate_sum, second_column = sync(
        out_beside, d_query, d_far, o_part, gate_sum, second_column
    )
    o_sum = over_groups(o_part)

    back = [lax.ppermute(d_far[2 * n + m], "g", reverse(shift_pairs(d))) for n, d in enumerate(shifts) for m in range(2)]
    gate_far = other_half(gate_sum)
    d_query, d_other = step_back(other, other_bases, 1, d_query, [BF] * 2)
    other_sum = [d_other[m].astype(F32) for m in range(2)]
    for n in range(len(shifts)):
        for m in range(2):
            other_sum[m] = other_sum[m] + back[2 * n + m].astype(F32)
    other_sum = [o.astype(BF) for o in other_sum]
    d_query, other_sum, gate_far = sync(d_query, other_sum, gate_far)

    other_back = [flip(other_sum[0], "zh")]
    d_query, d_same = step_back(same, same_bases, 0, d_query, [BF] * len(same))
    d_query, d_same, other_back, d_far, other_late = sync(d_query, d_same, other_back, d_far, other_sum[1])

    other_back.append(flip(other_late, "zh"))
    same_back = [lax.ppermute(d_same[n], "g", reverse(shift_pairs(d))) for n, d in enumerate(shifts)]
    d_query, d_own = step_back([kv], own_bases, 0, d_query, [F32])
    d_q, shares = query_back(core, d_query, qkv_w, cos_table, sin_table)
    q_part = head_grad([norm_one[k] for k in range(4)], d_q)
    above_back = []
    if above_groups:
        above = lax.dynamic_slice_in_dim(d_far[-1], zl * rows, rows, 0)
        above_back.append(lax.ppermute(above, ("g", "zh"), reverse(above_pairs)))
    other_back, same_back, above_back, d_own, d_q, shares, q_part, up_down_sum = sync(
        other_back, same_back, above_back, d_own, d_q, shares, q_part, up_down_sum
    )

    d_kvs, shares = kv_back(core, d_own[0], other_back, same_back, above_back, shares, qkv_w, cos_table, sin_table)
    share_rows = shares.reshape(span, width)
    across = flip(share_rows[2 * rows :], "c")
    kv_part = kv_grad(norm_one, shares, d_kvs, second_column)
    beside_sum = add_rows(share_rows, 1, across, 1)
    def group_slice(part, k):
        return lax.dynamic_slice_in_dim(part, (g ^ k) * shard_pair, shard_pair, 0)

    def one_hop(k):
        return k & -k == k

    q_got = {k: flip(group_slice(q_part, k), "g", k) for k in range(1, groups) if one_hop(k)}
    up_far = flip(up_down_sum[:, 2 * half : 3 * half], "zh")
    beside_sum, kv_part, across, share_rows, up_far, o_sum, q_got, q_part, gate_far, gate_sum, up_down_sum = sync(
        beside_sum, kv_part, across, share_rows, up_far, o_sum, q_got, q_part, gate_far, gate_sum, up_down_sum
    )

    kv_got = [flip(group_slice(kv_part, k), "g", k) for k in range(1, groups) if one_hop(k)]
    diagonal = [
        flip(jnp.concatenate([group_slice(kv_part, k), group_slice(q_part, k)], 1), "g", k)
        for k in range(1, groups)
        if not one_hop(k)
    ]
    beside = flip(beside_sum, "zl")
    do_far = flip(jnp.concatenate([up_down_sum[:, 3 * half :], o_sum[:, 256:]], 1), "zh")
    kv_got, diagonal, beside, do_far, up_far, gate_far = sync(kv_got, diagonal, beside, do_far, up_far, gate_far)

    kv_sum = group_slice(kv_part, 0).astype(F32) + sum(v.astype(F32) for v in kv_got)
    q_sum = group_slice(q_part, 0).astype(F32) + sum(v.astype(F32) for v in q_got.values())
    for value in diagonal:
        kv_sum, q_sum = kv_sum + value[:, :512].astype(F32), q_sum + value[:, 512:].astype(F32)
    kvq_own = jnp.concatenate([kv_sum[:, :256], q_sum[:, :256]], 1)
    kvq_give = jnp.concatenate([kv_sum[:, 256:], q_sum[:, 256:]], 1).astype(BF)
    kvq_own, kvq_give, do_far, beside, gate_far = sync(kvq_own, kvq_give, do_far, beside, gate_far)
    kvq_far = flip(kvq_give, "zh")
    [input_grad] = backward_norm(0, share_rows, across, beside, inputs, grad_mid, gain_rows, [BF])
    gate_up = jnp.concatenate([gate_sum[:, :half], up_down_sum[:, :half]], 1).astype(F32)
    gu_own, gu_got = to_owner(gate_up + jnp.concatenate([gate_far, up_far], 1).astype(F32))
    do_own = jnp.concatenate([up_down_sum[:, half : 2 * half], o_sum[:, :256]], 1)
    do_own, do_got = to_owner(do_own.astype(F32) + do_far.astype(F32))
    layer_out = (after_attn + (early[0].astype(F32) + out_across[1].astype(F32) + out_beside.astype(F32))).astype(BF)
    kvq_far, do_own, do_got, gu_own, gu_got, input_grad, layer_out = sync(
        kvq_far, do_own, do_got, gu_own, gu_got, input_grad, layer_out
    )

    kvq_own, kvq_got = to_owner(kvq_own + kvq_far.astype(F32))
    gain_sums = (kvq_own + kvq_got)[:, 2 * HEAD : 2 * HEAD + 2]
    gain_sums = gain_sums + flip(gain_sums, "zl")

    def columns(own, got, start, size):
        return in_order(own[:, start : start + size], got[:, start : start + size], 1)

    return (
        layer_out,
        input_grad,
        gain_sums[:, 0] / first_gain.astype(F32),
        columns(kvq_own, kvq_got, 256, 2 * HEAD),
        columns(kvq_own, kvq_got, 0, HEAD),
        columns(kvq_own, kvq_got, HEAD, HEAD),
        columns(do_own, do_got, half, 2 * HEAD).T,
        gain_sums[:, 1] / second_gain.astype(F32),
        columns(gu_own, gu_got, 0, half),
        columns(gu_own, gu_got, half, half),
        columns(do_own, do_got, 0, half).T,
    )


def solution(mesh):
    outer, inner = mesh.devices.shape
    fine = Mesh(mesh.devices.reshape(outer // 2, 2, inner // 2, 2), AXES)
    data, tensor = ("g", "c"), ("zh", "zl")
    rows, first = P(AXES, None), P(data)
    wide, tall = P(data, tensor), P(tensor, data)
    return jax.shard_map(
        body,
        mesh=fine,
        in_specs=(rows, first, wide, wide, wide, tall, first, wide, wide, tall, P(), P(), rows),
        out_specs=(rows, rows, first, wide, wide, wide, tall, first, wide, wide, tall),
        check_vma=False,
    )
```

```python
import functools
import math

import jax
import jax.numpy as jnp
from jax import lax
from jax.experimental import pallas as pl
from jax.experimental.layout import Layout, with_layout_constraint
from jax.experimental.pallas import tpu as pltpu
from jax.sharding import Mesh, PartitionSpec as P

HEAD = 96
LANES = 128
PIECE = 256
LEN_FIRST = 4096
LEN_LAST = 2048
LEN_MAX = 4096
epsilon = 1e-05
rope_base = 100000.0
negative = -1e30
far_away = 1 << 30
log2_e = 1.4426950408889634
score_scale = 1.0 / math.sqrt(HEAD)
BF = jnp.bfloat16
F32 = jnp.float32
AXES = ("g", "c", "zh", "zl")
MIB = 1024 * 1024
COST_SHARE = 0.01


def params(mib):
    return pltpu.CompilerParams(vmem_limit_bytes=mib * MIB)


def nn(left, right):
    return lax.dot_general(left, right, (((1,), (0,)), ((), ())), preferred_element_type=F32)


def nt(left, right):
    return lax.dot_general(left, right, (((1,), (1,)), ((), ())), preferred_element_type=F32)


def tn(left, right):
    return lax.dot_general(left, right, (((0,), (0,)), ((), ())), preferred_element_type=F32)


def after(value, *earlier):
    return lax.optimization_barrier((value, *earlier))[0]


def sync(*values):
    return lax.optimization_barrier(values)


def all_groups(value):
    return lax.all_gather(value, "g", axis=0, tiled=True)


def flip(value, axis, bit=1):
    count = lax.axis_size(axis)
    return lax.ppermute(value, axis, [(s, s ^ bit) for s in range(count)])


def cost(us):
    us = us * COST_SHARE
    return pl.CostEstimate(flops=int(us * 1.15e9), bytes_accessed=int(us * 3.6e6), transcendentals=0)


def gather_rows(own):
    beside = flip(own, "zl")
    across = flip(own, "c")
    both = flip(beside, "c")
    return [own, beside, across, both]


def from_groups(value):
    return [value] + [flip(value, "g", k) for k in range(1, lax.axis_size("g"))]


def split_core(shard):
    c = lax.axis_index("c")
    keep = lax.dynamic_index_in_dim(shard, c, 0, False)
    got = flip(lax.dynamic_index_in_dim(shard, 1 - c, 0, False), "c")
    return keep, got


def in_order(keep, got, axis=0):
    c = lax.axis_index("c")
    return jnp.where(c == 0, jnp.concatenate([keep, got], axis), jnp.concatenate([got, keep], axis))


def by_rows(value):
    return with_layout_constraint(value, Layout(major_to_minor=(0, 1)))


def over_groups(value):
    return lax.psum_scatter(value, "g", scatter_dimension=0, tiled=True)


def to_owner(mine):
    c = lax.axis_index("c")
    half = mine.shape[0] // 2
    own = lax.dynamic_slice_in_dim(mine, c * half, half, 0).astype(F32)
    got = flip(lax.dynamic_slice_in_dim(mine, (1 - c) * half, half, 0).astype(BF), "c").astype(F32)
    return own, got


def joined(own, got):
    return in_order(own, got, 1)


def swap_halves(value):
    lane = lax.broadcasted_iota(jnp.int32, value.shape, 1)
    return jnp.where(lane < HEAD // 2, pltpu.roll(value, LANES - HEAD // 2, 1), pltpu.roll(value, HEAD // 2, 1))


def turn(value, cosine, sine):
    return value * cosine + swap_halves(value) * sine


def unturn(value, cosine, sine):
    return value * cosine - swap_halves(value) * sine


def widen(value):
    pad = jnp.zeros((value.shape[0], LANES - HEAD), value.dtype)
    return jnp.concatenate([value, pad], 1)


def qkv_kernel(count, n_jumps, where_ref, *refs):
    pieces, refs = refs[: 2 * count], refs[2 * count :]
    jumps, refs = refs[:n_jumps], refs[n_jumps:]
    x0, x1, x_far, cos_ref, sin_ref, norm_ref, query_ref, kv_ref, weight_ref, gains_ref, x_ref = refs
    step = pl.program_id(0)

    @pl.when(step == 0)
    def _():
        half = pieces[0].shape[0] // 2

        def place(block, n, value):
            for part in range(2):
                at = pl.multiple_of(where_ref[2 * n + part], 64)
                weight_ref[block, pl.ds(at, half), :] = value[part * half : (part + 1) * half, :]

        for block in range(2):
            for n in range(count):
                place(block, n, pieces[block * count + n])
            for n in range(n_jumps):
                place(block, count + n, jumps[n][2 * half * block : 2 * half * (block + 1), :])
        row = lax.broadcasted_iota(jnp.int32, (8, LANES), 0)
        lane = lax.broadcasted_iota(jnp.int32, (8, LANES), 1)
        pick = jnp.where(row == lane, 1.0, 0.0).astype(BF)
        gains_ref[...] = nt(pick, weight_ref[0][:, 4 * HEAD :])

    for k in range(4):

        @pl.when(step == k)
        def _():
            x_ref[...] = (x0, x1)[k][...] if k < 2 else x_far[(k - 2) * PIECE : (k - 1) * PIECE, :]

    x = x_ref[...].astype(F32)
    r = lax.rsqrt(jnp.mean(x * x, axis=-1, keepdims=True) + epsilon)
    normed = (x * r * gains_ref[0:1, :]).astype(BF)
    norm_ref[0] = normed
    cosine, sine = cos_ref[0], sin_ref[0]
    packs = []
    for j in range(2):
        pre = nn(normed, weight_ref[j][:, 0 : 4 * HEAD])
        for h in range(2):
            turned = turn(widen(pre[:, h * HEAD : (h + 1) * HEAD]), cosine, sine)
            query_ref[j, 0, h * PIECE : (h + 1) * PIECE] = (turned * (score_scale * log2_e)).astype(BF)
        packs.append(turn(widen(pre[:, 2 * HEAD : 3 * HEAD]), cosine, sine)[:, 0:HEAD])
        packs.append(pre[:, 3 * HEAD :])
    kv_ref[...] = jnp.concatenate(packs, 1).astype(BF)


def project_qkv(where, pieces, jumps, x_rows, x_far, cos_table, sin_table):
    rows, width = x_rows[0].shape
    n_cols = pieces[0].shape[1]
    table = pl.BlockSpec((1, rows, LANES), lambda i, *_: (i, 0, 0))
    return pl.pallas_call(
        functools.partial(qkv_kernel, len(pieces) // 2, len(jumps)),
        grid_spec=pltpu.PrefetchScalarGridSpec(
            num_scalar_prefetch=1,
            grid=(4,),
            in_specs=[pl.BlockSpec(v.shape, lambda i, *_: (0, 0)) for v in (*pieces, *jumps, *x_rows, x_far)] + [table, table],
            out_specs=[
                pl.BlockSpec((1, rows, width), lambda i, *_: (i, 0, 0)),
                pl.BlockSpec((2, 1, 2 * rows, LANES), lambda i, *_: (0, i, 0, 0)),
                pl.BlockSpec((rows, 4 * HEAD), lambda i, *_: (i, 0)),
                pl.BlockSpec((2, width, n_cols), lambda i, *_: (0, 0, 0)),
                pl.BlockSpec((8, width), lambda i, *_: (0, 0)),
            ],
            scratch_shapes=[pltpu.VMEM((rows, width), BF)],
        ),
        out_shape=[
            jax.ShapeDtypeStruct((4, rows, width), BF),
            jax.ShapeDtypeStruct((2, 4, 2 * rows, LANES), BF),
            jax.ShapeDtypeStruct((4 * rows, 4 * HEAD), BF),
            jax.ShapeDtypeStruct((2, width, n_cols), BF),
            jax.ShapeDtypeStruct((8, width), F32),
        ],
        compiler_params=params(58),
        cost_estimate=cost(8),
        name="project_qkv",
    )(where, *pieces, *jumps, *x_rows, x_far, cos_table, sin_table)


def query_back_kernel(core_ref, dq_ref, weight_ref, cos_ref, sin_ref, grad_ref, share_ref):
    total = None
    for j in range(2):
        heads = []
        for h in range(2):
            turned = unturn(dq_ref[j, 0, h * PIECE : (h + 1) * PIECE], cos_ref[0], sin_ref[0])
            heads.append((turned * score_scale)[:, 0:HEAD])
        grad = jnp.concatenate(heads, 1).astype(BF)
        grad_ref[j, 0] = grad
        term = nt(grad, weight_ref[j][:, 0 : 2 * HEAD])
        total = term if total is None else total + term
    share_ref[0] = total.astype(BF)


def kv_back_kernel(n_same, has_above, core_ref, *refs):
    refs = list(refs)
    own_ref, first_ref, second_ref = refs[:3]
    same_refs = refs[3 : 3 + n_same]
    refs = refs[3 + n_same :]
    i = pl.program_id(0)
    late = i >= 2
    d_kv = own_ref[...] + jnp.where(late, second_ref[...], first_ref[...]).astype(F32)
    for ref in same_refs:
        d_kv = d_kv + ref[...].astype(F32)
    if has_above:
        d_kv = d_kv + jnp.where(i == core_ref[0], refs.pop(0)[...], 0).astype(F32)
    share_in_ref, weight_ref, cos_ref, sin_ref, grad_ref, share_ref = refs
    total = share_in_ref[0].astype(F32)
    for j in range(2):
        both = d_kv[:, 2 * HEAD * j : 2 * HEAD * (j + 1)]
        turned = unturn(widen(both[:, 0:HEAD]), cos_ref[0], sin_ref[0]) * (1.0 / log2_e)
        grad = jnp.concatenate([turned[:, 0:HEAD], both[:, HEAD:]], 1).astype(BF)
        grad_ref[j, 0] = grad
        total = total + nt(grad, weight_ref[j][:, 2 * HEAD : 4 * HEAD])
    share_ref[0] = total.astype(BF)


def project_back(kernel, core, args, specs, weights, cos_table, sin_table, name):
    count, rows, _ = cos_table.shape
    width = weights.shape[1]
    piece = pl.BlockSpec((1, rows, width), lambda i, *_: (i, 0, 0))
    table = pl.BlockSpec((1, rows, cos_table.shape[2]), lambda i, *_: (i, 0, 0))
    return pl.pallas_call(
        kernel,
        grid_spec=pltpu.PrefetchScalarGridSpec(
            num_scalar_prefetch=1,
            grid=(count,),
            in_specs=specs + [pl.BlockSpec((2, width, 4 * HEAD), lambda i, *_: (0, 0, 0)), table, table],
            out_specs=[pl.BlockSpec((2, 1, rows, 2 * HEAD), lambda i, *_: (0, i, 0, 0)), piece],
        ),
        out_shape=[
            jax.ShapeDtypeStruct((2, count, rows, 2 * HEAD), BF),
            jax.ShapeDtypeStruct((count, rows, width), BF),
        ],
        compiler_params=params(58),
        cost_estimate=cost(4),
        name=name,
    )(core, *args, weights, cos_table, sin_table)


def query_back(core, d_query, weights, cos_table, sin_table):
    spec = pl.BlockSpec((2, 1, 2 * PIECE, LANES), lambda i, *_: (0, i, 0, 0))
    return project_back(query_back_kernel, core, [d_query], [spec], weights, cos_table, sin_table, "query_back")


def kv_back(core, own, other, same, above, shares, weights, cos_table, sin_table):
    rows = pl.BlockSpec((PIECE, 4 * HEAD), lambda i, *_: (i, 0))
    chunk = pl.BlockSpec((PIECE, 4 * HEAD), lambda i, *_: (i % 2, 0))
    args = [own, *other, *same, *above, shares]
    specs = [rows, chunk, chunk] + [rows] * len(same)
    specs += [pl.BlockSpec((PIECE, 4 * HEAD), lambda i, *_: (0, 0))] * len(above)
    specs.append(pl.BlockSpec((1, *shares.shape[1:]), lambda i, *_: (i, 0, 0)))
    kernel = functools.partial(kv_back_kernel, len(same), bool(above))
    return project_back(kernel, core, args, specs, weights, cos_table, sin_table, "kv_back")


CHUNK = 2 * PIECE


def unpack_kv(swaps, block_refs, key_scratch, value_scratch):
    lane = lax.broadcasted_iota(jnp.int32, (CHUNK, LANES - HEAD), 1)
    ones = jnp.where(lane < 3, 1.0, 0.0).astype(BF)
    at = 0
    for swap, ref in zip(swaps, block_refs):
        for start in range(0, ref.shape[0], CHUNK):
            block = ref[start : start + CHUNK, :]
            for j in range(2):
                first = 2 * HEAD * (j ^ swap)
                k = block[:, first : first + HEAD]
                v = block[:, first + HEAD : first + 2 * HEAD]
                key_scratch[j, at : at + CHUNK, :] = jnp.concatenate([k, ones], 1)
                value_scratch[j, at : at + CHUNK, :] = jnp.concatenate([v, ones], 1)
            at += CHUNK


def chunk_state(info_ref, base, i):
    last = base + (CHUNK - 1)
    touched = (base <= info_ref[i, 3]) & (last >= info_ref[i, 0])
    full = (base >= info_ref[i, 1]) & (last <= info_ref[i, 2])
    return touched, full


def forward_kernel(swaps, first, last, info_ref, base_ref, zl_ref, *refs):
    refs = list(refs)
    n_blocks = len(swaps)
    query_ref, low_ref, high_ref = refs[:3]
    block_refs = refs[3 : 3 + n_blocks]
    refs = refs[3 + n_blocks :]
    if not first:
        acc_in = refs.pop(0)
    if last:
        mixed_ref = refs.pop(0)
    kept_ref = refs.pop(0)
    key_scratch, value_scratch, acc, top = refs
    i = pl.program_id(0)

    @pl.when(i == 0)
    def _():
        unpack_kv(swaps, block_refs, key_scratch, value_scratch)

    for j in range(2):
        if first:
            acc[j] = jnp.zeros((CHUNK, LANES), F32)
            top[j] = jnp.full((CHUNK, LANES), negative, F32)
        else:
            acc[j] = acc_in[j, 0]
            top[j] = jnp.broadcast_to(acc_in[j, 0][:, HEAD + 1 : HEAD + 2], (CHUNK, LANES))
    n_chunks = sum(r.shape[0] for r in block_refs) // CHUNK

    def visit(n, masked):
        rows = pl.ds(pl.multiple_of(n * CHUNK, CHUNK), CHUNK)
        if masked:
            at = lax.broadcasted_iota(jnp.int32, (PIECE, CHUNK), 1)
            token = base_ref[n] + lax.rem(at + zl_ref[0] * PIECE, CHUNK)
            low = jnp.concatenate([low_ref[0]] * (CHUNK // LANES), 1)
            high = jnp.concatenate([high_ref[0]] * (CHUNK // LANES), 1)
            allowed = (token >= low) & (token <= high)
        for j in range(2):
            scores = nt(query_ref[j, 0], key_scratch[j, rows, :])
            if masked:
                scores = jnp.concatenate(
                    [jnp.where(allowed, scores[h * PIECE : (h + 1) * PIECE], negative) for h in range(2)], 0
                )
            old = top[j]
            new = jnp.maximum(old, jnp.max(scores, axis=1, keepdims=True))
            top[j] = new
            probs = jnp.exp2(scores - jnp.concatenate([new] * (CHUNK // LANES), 1)).astype(BF)
            acc[j] = acc[j] * jnp.exp2(old - new) + nn(probs, value_scratch[j, rows, :])

    @pl.loop(0, n_chunks)
    def _(n):
        touched, full = chunk_state(info_ref, base_ref[n], i)

        @pl.when(touched & full)
        def _():
            visit(n, False)

        @pl.when(touched & jnp.logical_not(full))
        def _():
            visit(n, True)

    lane = lax.broadcasted_iota(jnp.int32, (CHUNK, LANES), 1)
    if last:
        for j in range(2):
            total = acc[j][:, HEAD : HEAD + 1]
            out = acc[j] / total
            kept_ref[j, 0] = jnp.where(lane < HEAD, out, top[j] + jnp.log2(total))
            mixed_ref[j, 0] = jnp.concatenate([out[0:PIECE, 0:HEAD], out[PIECE:, 0:HEAD]], 1).astype(BF)
    else:
        for j in range(2):
            kept_ref[j, 0] = jnp.where(lane == HEAD + 1, top[j], acc[j])


def attend(query, low, high, info, bases, zl, blocks, swaps, state, last):
    count = query.shape[1]
    n_keys = sum(b.shape[0] for b in blocks)
    per_piece = pl.BlockSpec((2, 1, CHUNK, LANES), lambda i, *_: (0, i, 0, 0))
    bound = pl.BlockSpec((1, PIECE, LANES), lambda i, *_: (i, 0, 0))
    in_specs = [per_piece, bound, bound]
    in_specs += [pl.BlockSpec(b.shape, lambda i, *_: (0, 0)) for b in blocks]
    args = [query, low, high, *blocks]
    if state is not None:
        in_specs.append(per_piece)
        args.append(state)
    wide = jax.ShapeDtypeStruct((2, count, CHUNK, LANES), F32)
    if last:
        out_shape = [jax.ShapeDtypeStruct((2, count, PIECE, 2 * HEAD), BF), wide]
        out_specs = [pl.BlockSpec((2, 1, PIECE, 2 * HEAD), lambda i, *_: (0, i, 0, 0)), per_piece]
    else:
        out_shape = wide
        out_specs = per_piece
    return pl.pallas_call(
        functools.partial(forward_kernel, swaps, state is None, last),
        grid_spec=pltpu.PrefetchScalarGridSpec(
            num_scalar_prefetch=3,
            grid=(count,),
            in_specs=in_specs,
            out_specs=out_specs,
            scratch_shapes=[
                pltpu.VMEM((2, n_keys, LANES), BF),
                pltpu.VMEM((2, n_keys, LANES), BF),
                pltpu.VMEM((2, CHUNK, LANES), F32),
                pltpu.VMEM((2, CHUNK, LANES), F32),
            ],
        ),
        out_shape=out_shape,
        compiler_params=params(48),
        cost_estimate=cost(n_keys / 100),
        name="attend",
    )(info, bases, zl, *args)


def split_three(value):
    first = value.astype(BF)
    rest = value - first.astype(F32)
    second = rest.astype(BF)
    third = (rest - second.astype(F32)).astype(BF)
    return first, second, third


def augment(wide, extra):
    lane = lax.broadcasted_iota(jnp.int32, wide.shape, 1)
    a, b, c = (part.astype(F32) for part in split_three(extra))
    out = wide.astype(F32)
    out = jnp.where(lane == HEAD, a, out)
    out = jnp.where(lane == HEAD + 1, b, out)
    out = jnp.where(lane == HEAD + 2, c, out)
    return out.astype(BF)


def prepare_kernel(m0, m1, m2, m3, w0, w1, kept_ref, query_ref, q_aug_ref, o_aug_ref, mid_ref):
    step = pl.program_id(0)
    for k, ref in enumerate((m0, m1, m2, m3)):

        @pl.when(step == k)
        def _():
            mid_ref[...] = ref[...]

    mid = mid_ref[...]
    for j, weight_ref in enumerate((w0, w1)):
        grad = nn(mid, weight_ref[...][:, 0 : 2 * HEAD])
        wide = jnp.concatenate([widen(grad[:, 0:HEAD]), widen(grad[:, HEAD : 2 * HEAD])], 0).astype(BF)
        kept = kept_ref[j, 0]
        delta = jnp.sum(wide.astype(F32) * kept, axis=1, keepdims=True)
        q_aug_ref[j, 0] = augment(query_ref[j, 0], -kept[:, HEAD : HEAD + 1])
        o_aug_ref[j, 0] = augment(wide, -delta)


def prepare_back(mid, weights, tile, kept, query):
    count = len(mid)
    rows, width = mid[0].shape
    per_piece = pl.BlockSpec((2, 1, CHUNK, LANES), lambda i: (0, i, 0, 0))
    return pl.pallas_call(
        prepare_kernel,
        grid=(count,),
        in_specs=[pl.BlockSpec((rows, width), lambda i: (0, 0))] * count
        + [pl.BlockSpec((width, 256), lambda i: (0, tile))] * 2
        + [per_piece, per_piece],
        out_specs=[per_piece, per_piece],
        out_shape=[jax.ShapeDtypeStruct(query.shape, BF)] * 2,
        scratch_shapes=[pltpu.VMEM((rows, width), BF)],
        compiler_params=params(58),
        cost_estimate=cost(6),
        name="prepare_back",
    )(*mid, *weights, kept, query)


def backward_kernel(swaps, has_dq, info_ref, base_ref, zl_ref, *refs):
    refs = list(refs)
    n_blocks = len(swaps)
    q_aug, o_aug, low_ref, high_ref = refs[:4]
    block_refs = refs[4 : 4 + n_blocks]
    refs = refs[4 + n_blocks :]
    if has_dq:
        dq_in = refs.pop(0)
    dq_ref = refs.pop(0)
    out_refs = refs[:n_blocks]
    key_scratch, value_scratch, d_key, d_value = refs[n_blocks:]
    i = pl.program_id(0)

    @pl.when(i == 0)
    def _():
        unpack_kv(swaps, block_refs, key_scratch, value_scratch)
        d_key[...] = jnp.zeros(d_key.shape, F32)
        d_value[...] = jnp.zeros(d_value.shape, F32)

    for j in range(2):
        if has_dq:
            dq_ref[j, 0] = dq_in[j, 0]
        else:
            dq_ref[j, 0] = jnp.zeros((CHUNK, LANES), F32)
    n_chunks = sum(r.shape[0] for r in block_refs) // CHUNK

    def visit(n, masked):
        rows = pl.ds(pl.multiple_of(n * CHUNK, CHUNK), CHUNK)
        if masked:
            at = lax.broadcasted_iota(jnp.int32, (CHUNK, CHUNK), 0)
            token = base_ref[n] + lax.rem(at + zl_ref[0] * PIECE, CHUNK)
            allowed = (token >= low_ref[0, 0:1, :]) & (token <= high_ref[0, 0:1, :])
        for j in range(2):
            keys = key_scratch[j, rows, :]
            probs = jnp.exp2(nt(keys, q_aug[j, 0]))
            if masked:
                probs = jnp.where(allowed, probs, 0.0)
            d_probs = nt(value_scratch[j, rows, :], o_aug[j, 0])
            low_probs = probs.astype(BF)
            d_scores = (probs * d_probs).astype(BF)
            d_value[j, rows, :] += nn(low_probs, o_aug[j, 0])
            d_key[j, rows, :] += nn(d_scores, q_aug[j, 0])
            dq_ref[j, 0] += tn(d_scores, keys)

    @pl.loop(0, n_chunks)
    def _(n):
        touched, full = chunk_state(info_ref, base_ref[n], i)

        @pl.when(touched & full)
        def _():
            visit(n, False)

        @pl.when(touched & jnp.logical_not(full))
        def _():
            visit(n, True)

    @pl.when(i == pl.num_programs(0) - 1)
    def _():
        at = 0
        for swap, ref in zip(swaps, out_refs):
            for start in range(0, ref.shape[0], CHUNK):
                parts = []
                for j in (swap, 1 - swap):
                    parts.append(d_key[j, at : at + CHUNK, :][:, 0:HEAD])
                    parts.append(d_value[j, at : at + CHUNK, :][:, 0:HEAD])
                ref[start : start + CHUNK, :] = jnp.concatenate(parts, 1).astype(ref.dtype)
                at += CHUNK


def attend_back(q_aug, o_aug, low, high, info, bases, zl, blocks, swaps, d_query, kinds):
    count = q_aug.shape[1]
    n_keys = sum(b.shape[0] for b in blocks)
    per_piece = pl.BlockSpec((2, 1, CHUNK, LANES), lambda i, *_: (0, i, 0, 0))
    bound = pl.BlockSpec((1, 8, CHUNK), lambda i, *_: (i, 0, 0))
    whole = [pl.BlockSpec(b.shape, lambda i, *_: (0, 0)) for b in blocks]
    in_specs = [per_piece, per_piece, bound, bound, *whole]
    args = [q_aug, o_aug, low, high, *blocks]
    if d_query is not None:
        in_specs.append(per_piece)
        args.append(d_query)
    return pl.pallas_call(
        functools.partial(backward_kernel, swaps, d_query is not None),
        grid_spec=pltpu.PrefetchScalarGridSpec(
            num_scalar_prefetch=3,
            grid=(count,),
            in_specs=in_specs,
            out_specs=[per_piece, *whole],
            scratch_shapes=[
                pltpu.VMEM((2, n_keys, LANES), BF),
                pltpu.VMEM((2, n_keys, LANES), BF),
                pltpu.VMEM((2, n_keys, LANES), F32),
                pltpu.VMEM((2, n_keys, LANES), F32),
            ],
        ),
        out_shape=[jax.ShapeDtypeStruct((2, count, CHUNK, LANES), F32)]
        + [jax.ShapeDtypeStruct(b.shape, k) for b, k in zip(blocks, kinds)],
        compiler_params=params(56),
        cost_estimate=cost(n_keys / 64),
        name="attend_back",
    )(info, bases, zl, *args)


def ffn_kernel(tiles, n0, n1, g0, g1, *refs):
    own_refs, other_refs, refs = refs[0:3], refs[3:6], refs[6:]
    o0, o1, b0, b1, hidden_ref, dg_ref, du_ref, norm_t, grad_t, norm_ref, grad_ref, acc_out, acc_back = refs
    step = pl.program_id(0)

    @pl.when(step == 0)
    def _():
        norm_ref[0:PIECE] = n0[...]
        norm_ref[PIECE:] = n1[...]
        grad_ref[0:PIECE] = g0[...]
        grad_ref[PIECE:] = g1[...]

    def run(gate_ref, up_ref, down_ref, first):
        gate_w, up_w, down_w = gate_ref[...], up_ref[...], down_ref[...]
        gate = nn(norm_ref[...], gate_w)
        up = nn(norm_ref[...], up_w)
        d_hidden = nn(grad_ref[...], down_w)
        sig = jax.nn.sigmoid(gate)
        silu = gate * sig
        hidden = (silu * up).astype(BF)
        d_gate = (d_hidden * up * sig * (1.0 + gate * (1.0 - sig))).astype(BF)
        d_up = (d_hidden * silu).astype(BF)
        hidden_ref[...] = hidden
        dg_ref[...] = d_gate
        du_ref[...] = d_up
        norm_t[...] = norm_ref[pl.ds(pl.multiple_of(step * LANES, LANES), LANES), :].T
        grad_t[...] = grad_ref[pl.ds(pl.multiple_of(step * LANES, LANES), LANES), :].T
        out = nt(hidden, down_w)
        back = nt(d_gate, gate_w) + nt(d_up, up_w)
        if first:
            acc_out[...] = out
            acc_back[...] = back
        else:
            acc_out[...] += out
            acc_back[...] += back

    @pl.when(step == 0)
    def _():
        run(*own_refs, True)

    @pl.when((step > 0) & (step < tiles))
    def _():
        run(*own_refs, False)

    @pl.when(step >= tiles)
    def _():
        run(*other_refs, False)

    @pl.when(step == pl.num_programs(0) - 1)
    def _():
        o0[...] = acc_out[0:PIECE].astype(BF)
        o1[...] = acc_out[PIECE:].astype(BF)
        b0[...] = acc_back[0:PIECE].astype(BF)
        b1[...] = acc_back[PIECE:].astype(BF)


def feed_forward(norm_rows, grad_rows, own, other):
    rows, width = norm_rows[0].shape
    half = 512
    tile = 256
    tiles = half // tile
    whole = pl.BlockSpec((rows, width), lambda s: (0, 0))

    def own_spec(at):
        return pl.BlockSpec((width, tile), lambda s: (0, at // tile + jnp.minimum(s, tiles - 1)))

    def other_spec(at):
        return pl.BlockSpec((width, tile), lambda s: (0, at // tile + jnp.maximum(s - tiles, 0)))

    hid = pl.BlockSpec((2 * rows, tile), lambda s: (0, s))
    turned = pl.BlockSpec((width, LANES), lambda s: (0, s))
    return pl.pallas_call(
        functools.partial(ffn_kernel, tiles),
        grid=(2 * tiles,),
        in_specs=[whole] * 4 + [own_spec(at) for _, at in own] + [other_spec(at) for _, at in other],
        out_specs=[whole] * 4 + [hid] * 3 + [turned] * 2,
        out_shape=[jax.ShapeDtypeStruct((rows, width), BF)] * 4
        + [jax.ShapeDtypeStruct((2 * rows, 2 * half), BF)] * 3
        + [jax.ShapeDtypeStruct((width, 2 * rows), BF)] * 2,
        scratch_shapes=[pltpu.VMEM((2 * rows, width), BF)] * 2 + [pltpu.VMEM((2 * rows, width), F32)] * 2,
        compiler_params=params(56),
        cost_estimate=cost(18),
        name="feed_forward",
    )(*norm_rows, *grad_rows, *(w for w, _ in own), *(w for w, _ in other))


def weight_grad_kernel(n_jobs, *refs):
    out_ref = refs[-1]
    for n in range(n_jobs):
        left_early, left_late, early, late = refs[4 * n : 4 * n + 4]

        @pl.when(pl.program_id(1) == n)
        def _():
            total = nn(left_early[...], early[...]) + nn(left_late[...], late[...])
            out_ref[...] = total.astype(BF)


def weight_grad(jobs, us):
    width, depth = jobs[0][0].shape
    half = jobs[0][2].shape[1] // 2
    count = len(jobs)
    left = pl.BlockSpec((width, depth), lambda s, n: (0, 0))
    cols = pl.BlockSpec((depth, half), lambda s, n: (0, s))
    return pl.pallas_call(
        functools.partial(weight_grad_kernel, count),
        grid=(2, count),
        in_specs=[left, left, cols, cols] * count,
        out_specs=pl.BlockSpec((width, half), lambda s, n: (0, s * count + n)),
        out_shape=jax.ShapeDtypeStruct((width, 2 * count * half), BF),
        compiler_params=params(48),
        cost_estimate=cost(us),
        name="weight_grad",
    )(*(value for job in jobs for value in job))


def head_grad_kernel(l0, l1, l2, l3, right_ref, out_ref):
    for j in range(2):
        total = None
        for k, left in enumerate((l0, l1, l2, l3)):
            term = tn(left[...], right_ref[j, k])
            total = term if total is None else total + term
        wide = jnp.concatenate([total, jnp.zeros((total.shape[0], 256 - 2 * HEAD), F32)], 1)
        out_ref[:, j * 256 : (j + 1) * 256] = wide.astype(BF)


def head_grad(left, right):
    rows, width = left[0].shape
    tile = 512
    return pl.pallas_call(
        head_grad_kernel,
        grid=(width // tile,),
        in_specs=[pl.BlockSpec((rows, tile), lambda s: (0, s))] * 4 + [pl.BlockSpec(right.shape, lambda s: (0, 0, 0, 0))],
        out_specs=pl.BlockSpec((tile, 512), lambda s: (s, 0)),
        out_shape=jax.ShapeDtypeStruct((width, 512), BF),
        compiler_params=params(40),
        cost_estimate=cost(3),
        name="head_grad",
    )(*left, right)


def gain_kernel(lane, *refs):
    out_ref = refs[-1]
    count = (len(refs) - 1) // 2
    at = lax.broadcasted_iota(jnp.int32, (PIECE, LANES), 1)
    pick = jnp.where(at == lane, 1.0, 0.0).astype(BF)
    total = None
    for share, normed in zip(refs[:count], refs[count : 2 * count]):
        product = (share[...].astype(F32) * normed[...].astype(F32)).astype(BF)
        term = tn(product, pick)
        total = term if total is None else total + term
    out_ref[...] = total


def gain_columns(shares, normed, lane):
    rows, width = shares[0].shape
    tile = 512
    spec = pl.BlockSpec((rows, tile), lambda s: (0, s))
    return pl.pallas_call(
        functools.partial(gain_kernel, lane),
        grid=(width // tile,),
        in_specs=[spec] * 8,
        out_specs=pl.BlockSpec((tile, LANES), lambda s: (s, 0)),
        out_shape=jax.ShapeDtypeStruct((width, LANES), F32),
        compiler_params=params(40),
        cost_estimate=cost(3),
        name="gain_columns",
    )(*shares, *normed)


def kv_grad_kernel(norm_ref, share_ref, dkv_ref, column_ref, *refs):
    out_ref = refs[-1]
    at = lax.broadcasted_iota(jnp.int32, (PIECE, LANES), 1)
    pick = jnp.where(at == 0, 1.0, 0.0).astype(BF)
    columns = column_ref[...]
    totals = [None, None]
    for k in range(4):
        normed = norm_ref[k]
        product = (share_ref[k].astype(F32) * normed.astype(F32)).astype(BF)
        columns = columns + tn(product, pick)
        for j in range(2):
            term = tn(normed, dkv_ref[j, k])
            totals[j] = term if totals[j] is None else totals[j] + term
    for j in range(2):
        out_ref[:, j * 256 : (j + 1) * 256] = jnp.concatenate([totals[j], columns[:, 0 : 256 - 2 * HEAD]], 1).astype(BF)


def kv_grad(normed, shares, d_kvs, columns):
    count, rows, width = normed.shape
    tile = 512
    spec = pl.BlockSpec((count, rows, tile), lambda s: (0, 0, s))
    return pl.pallas_call(
        kv_grad_kernel,
        grid=(width // tile,),
        in_specs=[
            spec,
            spec,
            pl.BlockSpec(d_kvs.shape, lambda s: (0, 0, 0, 0)),
            pl.BlockSpec((tile, LANES), lambda s: (s, 0)),
        ],
        out_specs=pl.BlockSpec((tile, 512), lambda s: (s, 0)),
        out_shape=jax.ShapeDtypeStruct((width, 512), BF),
        compiler_params=params(40),
        cost_estimate=cost(4),
        name="kv_grad",
    )(normed, shares, d_kvs, columns)


def output_kernel(mixed_ref, w0, w1, far_ref, near_ref):
    step = pl.program_id(0)
    total = None
    for j, weight in enumerate((w0, w1)):
        heads = jnp.concatenate([mixed_ref[j, 0], mixed_ref[j, 1]], 0)
        term = nt(heads, weight[...][:, 0 : 2 * HEAD])
        total = term if total is None else total + term

    @pl.when(step == 0)
    def _():
        far_ref[...] = total.astype(BF)

    @pl.when(step == 1)
    def _():
        near_ref[...] = total


def output_projection(mixed, weights, tile):
    _, count, rows, width_heads = mixed.shape
    width = weights[0].shape[0]
    whole = pl.BlockSpec((2 * rows, width), lambda s: (0, 0))
    return pl.pallas_call(
        output_kernel,
        grid=(2,),
        in_specs=[pl.BlockSpec((2, 2, rows, width_heads), lambda s: (0, 1 - s, 0, 0))]
        + [pl.BlockSpec((width, 256), lambda s: (0, tile))] * 2,
        out_specs=[whole, whole],
        out_shape=[jax.ShapeDtypeStruct((2 * rows, width), BF), jax.ShapeDtypeStruct((2 * rows, width), F32)],
        compiler_params=params(58),
        cost_estimate=cost(4),
        name="output_projection",
    )(mixed, *weights)


def add_kernel(near_ref, across_ref, out_ref):
    out_ref[...] = (near_ref[...].astype(F32) + across_ref[...].astype(F32)).astype(BF)


def add_rows(near, near_at, across, across_at):
    rows, width = PIECE, near.shape[1]
    return pl.pallas_call(
        add_kernel,
        grid=(1,),
        in_specs=[
            pl.BlockSpec((rows, width), lambda s: (near_at, 0)),
            pl.BlockSpec((rows, width), lambda s: (across_at, 0)),
        ],
        out_specs=pl.BlockSpec((rows, width), lambda s: (0, 0)),
        out_shape=jax.ShapeDtypeStruct((rows, width), BF),
        compiler_params=params(32),
        cost_estimate=cost(1),
        name="add_rows",
    )(near, across)


def forward_norm_kernel(x_ref, near_ref, across_ref, beside_ref, gain_ref, after_ref, norm_ref):
    rows = x_ref[...].astype(F32) + (near_ref[...] + across_ref[...].astype(F32) + beside_ref[...].astype(F32))
    after_ref[...] = rows
    r = lax.rsqrt(jnp.mean(rows * rows, axis=-1, keepdims=True) + epsilon)
    norm_ref[...] = (rows * r * gain_ref[1:2, :]).astype(BF)


def row_specs(width, n):
    return [pl.BlockSpec((LANES, width), lambda i: (i, 0))] * n


def forward_norm(x, near, across, beside, gain_rows):
    rows, width = x.shape
    return pl.pallas_call(
        forward_norm_kernel,
        grid=(rows // LANES,),
        in_specs=row_specs(width, 4) + [pl.BlockSpec((8, width), lambda i: (0, 0))],
        out_specs=row_specs(width, 2),
        out_shape=[jax.ShapeDtypeStruct((rows, width), F32), jax.ShapeDtypeStruct((rows, width), BF)],
        compiler_params=params(32),
        cost_estimate=cost(2),
        name="forward_norm",
    )(x, near, across, beside, gain_rows)


def backward_norm_kernel(which, share_ref, across_ref, beside_ref, rows_ref, base_ref, gain_ref, *out_refs):
    upstream = share_ref[...].astype(F32) + across_ref[...].astype(F32) + beside_ref[...].astype(F32)
    rows = rows_ref[...].astype(F32)
    r = lax.rsqrt(jnp.mean(rows * rows, axis=-1, keepdims=True) + epsilon)
    weighted = upstream * gain_ref[which : which + 1, :]
    inner = jnp.mean(weighted * rows, axis=-1, keepdims=True)
    out = base_ref[...].astype(F32) + (r * weighted - rows * (r * r * r) * inner)
    for ref in out_refs:
        ref[...] = out.astype(ref.dtype)


def backward_norm(which, share, across, beside, rows, base, gain_rows, kinds):
    count, width = rows.shape
    return pl.pallas_call(
        functools.partial(backward_norm_kernel, which),
        grid=(count // LANES,),
        in_specs=row_specs(width, 5) + [pl.BlockSpec((8, width), lambda i: (0, 0))],
        out_specs=row_specs(width, len(kinds)),
        out_shape=[jax.ShapeDtypeStruct((count, width), kind) for kind in kinds],
        compiler_params=params(32),
        cost_estimate=cost(2),
        name="backward_norm",
    )(share, across, beside, rows, base, gain_rows)


def token_tables(token, seq_lengths, piece_starts):
    n = seq_lengths.shape[0]
    upto = jnp.arange(n)[None, :] <= jnp.arange(n)[:, None]
    ends = jnp.sum(jnp.where(upto, seq_lengths[None, :], 0), axis=1)
    after = token[:, None] >= ends[None, :]
    start = jnp.sum(jnp.where(after, seq_lengths[None, :], 0), axis=1)
    end = jnp.min(jnp.where(after, far_away, ends[None, :]), axis=1)
    inside = (token[:, None] >= piece_starts[None, :]) & (token[:, None] < piece_starts[None, :] + PIECE)
    piece_end = jnp.max(jnp.where(inside, piece_starts[None, :] + PIECE, 0), axis=1)
    high = jnp.maximum(token, jnp.minimum(piece_end, end) - 1)
    return start, high


def may_meet(one, two, group_tokens, count):
    total = group_tokens * count
    regions = ((0, LEN_FIRST, LEN_FIRST), (LEN_FIRST, total - LEN_LAST, LEN_MAX), (total - LEN_LAST, total, LEN_LAST))
    for start, end, longest in regions:
        both = all(g * group_tokens < end and (g + 1) * group_tokens > start for g in (one, two))
        if both and (abs(one - two) - 1) * group_tokens + 1 < longest:
            return True
    return False


def body(
    inputs,
    first_gain,
    query_weight,
    key_matrix,
    value_matrix,
    output_weight,
    second_gain,
    gate_weight,
    up_weight,
    down_weight,
    seq_lengths,
    piece_starts,
    out_cotangent,
):
    g, c, zh, zl = (lax.axis_index(a) for a in AXES)
    groups = lax.axis_size("g")
    rows, width = inputs.shape
    span = 4 * rows
    group_tokens = 2 * span
    shard_rows = query_weight.shape[0]

    order = jnp.arange(4)
    piece_base = (2 * g + (c ^ (order >> 1))) * span + zh * CHUNK + (zl ^ (order & 1)) * rows
    token = (piece_base[:, None] + jnp.arange(rows)[None, :]).reshape(-1).astype(jnp.int32)
    low, high = token_tables(token, seq_lengths, piece_starts)
    position = (token - low).astype(F32)
    low, high = low.reshape(4, rows), high.reshape(4, rows)
    info = jnp.stack([low.min(1), low.max(1), high.min(1), high.max(1)], 1).astype(jnp.int32)
    low_wide = jnp.broadcast_to(low[:, :, None], (4, rows, LANES)).astype(jnp.int32)
    high_wide = jnp.broadcast_to(high[:, :, None], (4, rows, LANES)).astype(jnp.int32)
    low_rows = jnp.broadcast_to(jnp.tile(low, (1, 2))[:, None, :], (4, 8, CHUNK)).astype(jnp.int32)
    high_rows = jnp.broadcast_to(jnp.tile(high, (1, 2))[:, None, :], (4, 8, CHUNK)).astype(jnp.int32)
    zl_info = jnp.reshape(zl, (1,)).astype(jnp.int32)
    frequency = rope_base ** (-(2.0 / HEAD) * jnp.arange(HEAD // 2, dtype=F32))
    angles = position[:, None] * frequency[None, :]
    cosine, sine = jnp.cos(angles), jnp.sin(angles)
    pad = jnp.zeros((span, LANES - HEAD), F32)
    cos_table = jnp.concatenate([cosine, cosine, pad], 1).reshape(4, rows, LANES)
    sin_table = jnp.concatenate([-sine, sine, pad], 1).reshape(4, rows, LANES)

    def halves(matrix):
        return matrix.reshape(matrix.shape[0], 2, -1).transpose(1, 0, 2)

    blank = functools.partial(jnp.zeros, dtype=BF)
    half = gate_weight.shape[1] // 2
    zl_info = jnp.reshape(zl, (1,)).astype(jnp.int32)
    core = jnp.reshape(2 * c + zl, (1,)).astype(jnp.int32)
    shard_pair = 2 * shard_rows

    gains = jnp.broadcast_to(jnp.stack([first_gain, second_gain], 1)[None], (2, shard_rows, 2))
    qkv_shard = jnp.concatenate(
        [halves(query_weight), halves(key_matrix), halves(value_matrix), gains, blank((2, shard_rows, 126))], 2
    )
    qkv_keep, qkv_got = split_core(qkv_shard)
    ffn_shard = jnp.concatenate(
        [halves(gate_weight), halves(output_weight.T), blank((2, shard_rows, 64)), halves(up_weight), halves(down_weight.T)],
        2,
    )
    ffn_keep, ffn_got = split_core(ffn_shard)
    qkv_pair = jnp.concatenate([qkv_keep, qkv_got], 0)
    inputs, out_cotangent, qkv_pair, ffn_keep, ffn_got = sync(inputs, out_cotangent, qkv_pair, ffn_keep, ffn_got)

    qkv_other = flip(qkv_pair, "zh")
    hops = [k for k in range(1, groups) if k & -k == k]
    jumps = [k for k in range(1, groups) if k & -k != k]
    qkv_near = [flip(qkv_pair, "g", k) for k in (*hops, *jumps)]
    x_beside = flip(inputs, "zl")
    ffn_pair = in_order(ffn_keep, ffn_got)
    up_at = half + 2 * HEAD + 64
    first_pair = ffn_pair[:, :up_at]
    up_pair, down_pair = ffn_pair[:, up_at : up_at + half], ffn_pair[:, up_at + half :]
    (
        qkv_near, qkv_other, x_beside, ffn_pair, first_pair, up_pair, down_pair, cos_table, sin_table,
        info, low_wide, high_wide, low_rows, high_rows,
    ) = sync(
        qkv_near, qkv_other, x_beside, ffn_pair, first_pair, up_pair, down_pair, cos_table, sin_table,
        info, low_wide, high_wide, low_rows, high_rows,
    )
    x_near = jnp.concatenate([inputs, x_beside], 0)

    ffn_own = all_groups(ffn_pair)
    qkv_far = [flip(qkv_other, "g", k) for k in (*hops, *jumps)]
    x_far = flip(x_near, "c")
    first_other = flip(first_pair, "zh")
    qkv_far, x_far, first_other, up_pair, out_cotangent = sync(qkv_far, x_far, first_other, up_pair, out_cotangent)

    up_other = flip(up_pair, "zh")
    g_beside = flip(out_cotangent, "zl")
    k_order = jnp.array([0, *hops, *jumps])[:, None]
    piece_rows = (g ^ k_order) * shard_pair + (c ^ jnp.arange(2)[None, :]) * shard_rows
    norm_one, query, kv, qkv_w, gain_rows = project_qkv(
        piece_rows.reshape(-1).astype(jnp.int32),
        [qkv_pair, *qkv_near, qkv_other, *qkv_far],
        [],
        [inputs, x_beside],
        x_far,
        cos_table,
        sin_table,
    )
    first_piece = lax.dynamic_slice_in_dim(kv, (2 * c + zl) * rows, rows, 0)
    norm_one, query, kv, qkv_w, gain_rows, kv_chunks, first_piece, out_cotangent, g_beside, up_other, down_pair, first_other = sync(
        norm_one,
        query,
        kv,
        qkv_w,
        gain_rows,
        [kv[n * CHUNK : (n + 1) * CHUNK] for n in range(2)],
        first_piece,
        out_cotangent,
        g_beside,
        up_other,
        down_pair,
        first_other,
    )
    first_far = all_groups(first_other)

    def chunk_bases(group, side):
        return jnp.stack([(2 * group + (c ^ i)) * span + side * CHUNK for i in range(2)]).astype(jnp.int32)

    def shift_pairs(steps):
        return [(s, s + steps) for s in range(groups) if 0 <= s + steps < groups and may_meet(s, s + steps, group_tokens, groups)]

    def present(pairs, bases):
        target = functools.reduce(jnp.logical_or, [g == t for _, t in pairs])
        return jnp.where(target, bases, far_away).astype(jnp.int32)

    def reverse(pairs):
        return [(t, s) for s, t in pairs]

    shifts = [d for d in range(1, groups) if shift_pairs(d)]
    above_groups = [s for s in range(1, groups) if may_meet(s - 1, s, group_tokens, groups)]
    above_pairs = [(2 * s, 2 * (s - 1) + 1) for s in above_groups]
    own_bases, other_bases = chunk_bases(g, zh), chunk_bases(g, 1 - zh)
    same_bases = [present(shift_pairs(d), chunk_bases(g - d, zh)) for d in shifts]
    far_bases = [present(shift_pairs(d), chunk_bases(g - d, 1 - zh)) for d in shifts]
    if above_groups:
        is_target = functools.reduce(jnp.logical_or, [(g == s - 1) & (zh == 1) for s in above_groups])
        far_bases.append(jnp.where(is_target, jnp.reshape(2 * (g + 1) * span, (1,)), far_away).astype(jnp.int32))
    same_bases, far_bases = jnp.concatenate(same_bases), jnp.concatenate(far_bases)

    def step(blocks, bases, swap, state, last=False):
        swaps = [swap] * len(blocks)
        return attend(query, low_wide, high_wide, info, bases, zl_info, blocks, swaps, state, last)

    other = [flip(kv_chunks[0], "zh")]
    same = [lax.ppermute(kv, "g", shift_pairs(d)) for d in shifts]
    g_across = flip(out_cotangent, "c")
    state = step([kv], own_bases, 0, None)
    other, same, g_across, state, kv_late = sync(other, same, g_across, state, kv_chunks[1])

    other.append(flip(kv_late, "zh"))
    far_blocks = [[lax.ppermute(other[0], "g", shift_pairs(d))] for d in shifts]
    g_both = flip(g_beside, "c")
    state = step(same, same_bases, 0, state)
    other, far_blocks, g_both, state, down_pair, first_piece, ffn_own = sync(
        other, far_blocks, g_both, state, down_pair, first_piece, ffn_own
    )

    for n, d in enumerate(shifts):
        far_blocks[n].append(lax.ppermute(other[1], "g", shift_pairs(d)))
    far_blocks = [b for pair in far_blocks for b in pair]
    if above_groups:
        above = lax.ppermute(first_piece, ("g", "zh"), above_pairs)
        far_blocks.append(lax.dynamic_update_slice(jnp.zeros((CHUNK, 4 * HEAD), BF), above, (zl * rows, 0)))
    down_other = flip(down_pair, "zh")
    state = step(other, other_bases, 1, state)
    far_blocks, down_other, state = sync(far_blocks, down_other, state)

    second_far = all_groups(jnp.concatenate([up_other, down_other], 1))
    mixed, kept = step(far_blocks, far_bases, 1, state, True)
    mixed, kept, first_far = sync(mixed, kept, first_far)

    o_tile = half // 256
    far_shares, near_shares = output_projection(mixed, (ffn_own, first_far), o_tile)
    across = flip(far_shares, "c")
    beside_sum = add_rows(near_shares, 1, across, 1)
    beside = flip(beside_sum, "zl")
    after_attn, norm_own = sync(*forward_norm(inputs, near_shares, across, beside, gain_rows))

    norm_beside, norm_across = flip(norm_own, "zl"), flip(norm_own, "c")
    near_w = [(ffn_own, 0), (ffn_own, up_at), (ffn_own, up_at + half)]
    far_w = [(first_far, 0), (second_far, 0), (second_far, half)]
    early = feed_forward([norm_own, norm_across], [out_cotangent, g_across], near_w, far_w)
    norm_beside, norm_across, early = sync(norm_beside, norm_across, early)
    norm_both = flip(norm_beside, "c")
    late = feed_forward([norm_beside, norm_both], [g_beside, g_both], near_w, far_w)
    late, norm_both = sync(late, norm_both)

    across_both = flip(late[3], "c")
    beside_sum = add_rows(late[2], 0, across_both, 0)
    beside_sum, late, early = sync(beside_sum, late, early)
    beside = flip(beside_sum, "zl")
    across = flip(early[3], "c")
    out_across = [flip(late[1], "c"), flip(early[1], "c")]
    gate_up_part = weight_grad(
        [(early[7], late[7], early[5], late[5]), (early[7], late[7], early[6], late[6])], 8
    )
    beside, across, out_across, gate_up_part, early, late = sync(beside, across, out_across, gate_up_part, early, late)
    gate_up_sum = over_groups(gate_up_part)
    grad_mid, mid_low = backward_norm(1, early[2], across, beside, after_attn, out_cotangent, gain_rows, [F32, BF])
    grad_mid, mid_low, early, late = sync(grad_mid, mid_low, early, late)

    mid_beside, mid_across = flip(mid_low, "zl"), flip(mid_low, "c")
    down_part = weight_grad([(early[8], late[8], early[4], late[4])], 4)
    second_column = gain_columns([early[2], late[2], early[3], late[3]], [norm_own, norm_beside, norm_across, norm_both], 1)
    out_sum = add_rows(late[0], 0, out_across[0], 0)
    mid_beside, mid_across, down_part, second_column, out_sum = sync(
        mid_beside, mid_across, down_part, second_column, out_sum
    )
    mid_rows = [mid_low, mid_beside, mid_across, flip(mid_beside, "c")]
    q_aug, o_aug = prepare_back(mid_rows, (ffn_own, first_far), o_tile, kept, query)
    q_aug, o_aug, mid_rows, out_sum, mixed, early, late = sync(q_aug, o_aug, mid_rows, out_sum, mixed, early, late)

    def step_back(blocks, bases, swap, d_query, kinds):
        swaps = [swap] * len(blocks)
        out = attend_back(q_aug, o_aug, low_rows, high_rows, info, bases, zl_info, blocks, swaps, d_query, kinds)
        return out[0], list(out[1:])

    def other_half(summed):
        return flip(summed[:, summed.shape[1] // 2 :], "zh")

    out_beside = flip(out_sum, "zl")
    d_query, d_far = step_back(far_blocks, far_bases, 1, None, [BF] * len(far_blocks))
    o_part = head_grad(mid_rows, mixed)
    down_o_part = jnp.concatenate([down_part[:, :half], o_part[:, :256], down_part[:, half:], o_part[:, 256:]], 1)
    out_beside, d_query, d_far, gate_up_sum, down_o_part, early, late = sync(
        out_beside, d_query, d_far, gate_up_sum, down_o_part, early, late
    )
    down_o_sum = over_groups(down_o_part)

    back = [lax.ppermute(d_far[2 * n + m], "g", reverse(shift_pairs(d))) for n, d in enumerate(shifts) for m in range(2)]
    gate_up_far = other_half(gate_up_sum)
    d_query, d_other = step_back(other, other_bases, 1, d_query, [BF] * 2)
    d_query, d_same = step_back(same, same_bases, 0, d_query, [BF] * len(same))
    d_query, d_other, d_same, d_far, back, gate_up_far = sync(d_query, d_other, d_same, d_far, back, gate_up_far)

    other_sum = [d_other[m].astype(F32) for m in range(2)]
    for n in range(len(shifts)):
        for m in range(2):
            other_sum[m] = other_sum[m] + back[2 * n + m].astype(F32)
    other_sum = [o.astype(BF) for o in other_sum]
    other_back = [flip(other_sum[0], "zh")]
    same_back = [lax.ppermute(d_same[n], "g", reverse(shift_pairs(d))) for n, d in enumerate(shifts)]
    above_back = []
    if above_groups:
        above = lax.dynamic_slice_in_dim(d_far[-1], zl * rows, rows, 0)
        above_back.append(lax.ppermute(above, ("g", "zh"), reverse(above_pairs)))
    d_query, d_own = step_back([kv], own_bases, 0, d_query, [F32])
    core = jnp.reshape(2 * c + zl, (1,)).astype(jnp.int32)
    d_q, shares = query_back(core, d_query, qkv_w, cos_table, sin_table)
    q_part = head_grad([norm_one[k] for k in range(4)], d_q)
    other_back, same_back, above_back, d_own, shares, q_part, other_late, early, late = sync(
        other_back, same_back, above_back, d_own, shares, q_part, other_sum[1], early, late
    )

    def group_slice(part, k):
        return lax.dynamic_slice_in_dim(part, (g ^ k) * shard_pair, shard_pair, 0)

    other_back.append(flip(other_late, "zh"))
    q_got = [flip(group_slice(q_part, k), "g", k) for k in range(1, groups)]
    layer_out = (after_attn + (early[0].astype(F32) + out_across[1].astype(F32) + out_beside.astype(F32))).astype(BF)
    other_back, same_back, above_back, d_own, shares, q_part, q_got, down_o_sum, layer_out = sync(
        other_back, same_back, above_back, d_own, shares, q_part, q_got, down_o_sum, layer_out
    )

    d_kvs, shares = kv_back(core, d_own[0], other_back, same_back, above_back, shares, qkv_w, cos_table, sin_table)
    share_rows = shares.reshape(span, width)
    across = flip(share_rows[2 * rows :], "c")
    kv_part = kv_grad(norm_one, shares, d_kvs, second_column)
    beside_sum = add_rows(share_rows, 1, across, 1)
    down_at = half + 256
    down_far = flip(down_o_sum[:, down_at : down_at + half], "zh")
    beside_sum, kv_part, across, share_rows, down_far, down_o_sum, gate_up_far, gate_up_sum = sync(
        beside_sum, kv_part, across, share_rows, down_far, down_o_sum, gate_up_far, gate_up_sum
    )

    kv_got = [flip(group_slice(kv_part, k), "g", k) for k in range(1, groups)]
    q_sum = group_slice(q_part, 0).astype(F32) + sum(v.astype(F32) for v in q_got)
    beside = flip(beside_sum, "zl")
    o_far = flip(down_o_sum[:, down_at + half :], "zh")
    middle = 2 * half
    gu_own, gu_got = to_owner(gate_up_sum[:, :middle].astype(F32) + gate_up_far.astype(F32))
    kv_got, q_sum, beside, gu_own, gu_got, o_far, down_far = sync(kv_got, q_sum, beside, gu_own, gu_got, o_far, down_far)

    kv_sum = group_slice(kv_part, 0).astype(F32) + sum(v.astype(F32) for v in kv_got)
    kvq_own = jnp.concatenate([kv_sum[:, :256], q_sum[:, :256]], 1)
    kvq_give = jnp.concatenate([kv_sum[:, 256:], q_sum[:, 256:]], 1).astype(BF)
    kvq_own, kvq_give, o_far, down_far, beside = sync(kvq_own, kvq_give, o_far, down_far, beside)
    down_o_far = jnp.concatenate([down_far, o_far], 1)
    kvq_far = flip(kvq_give, "zh")
    [input_grad] = backward_norm(0, share_rows, across, beside, inputs, grad_mid, gain_rows, [BF])
    do_own, do_got = to_owner(down_o_sum[:, : half + 256].astype(F32) + down_o_far.astype(F32))
    kvq_far, do_own, do_got, input_grad = sync(kvq_far, do_own, do_got, input_grad)

    kvq_own, kvq_got = to_owner(kvq_own + kvq_far.astype(F32))
    gain_sums = (kvq_own + kvq_got)[:, 2 * HEAD : 2 * HEAD + 2]
    gain_sums = gain_sums + flip(gain_sums, "zl")

    def columns(own, got, start, size):
        return in_order(own[:, start : start + size], got[:, start : start + size], 1)

    return (
        layer_out,
        input_grad,
        gain_sums[:, 0] / first_gain.astype(F32),
        columns(kvq_own, kvq_got, 256, 2 * HEAD),
        columns(kvq_own, kvq_got, 0, HEAD),
        columns(kvq_own, kvq_got, HEAD, HEAD),
        columns(do_own, do_got, half, 2 * HEAD).T,
        gain_sums[:, 1] / second_gain.astype(F32),
        columns(gu_own, gu_got, 0, half),
        columns(gu_own, gu_got, half, half),
        columns(do_own, do_got, 0, half).T,
    )


def solution(mesh):
    outer, inner = mesh.devices.shape
    fine = Mesh(mesh.devices.reshape(outer // 2, 2, inner // 2, 2), AXES)
    data, tensor = ("g", "c"), ("zh", "zl")
    rows, first = P(AXES, None), P(data)
    wide, tall = P(data, tensor), P(tensor, data)
    return jax.shard_map(
        body,
        mesh=fine,
        in_specs=(rows, first, wide, wide, wide, tall, first, wide, wide, tall, P(), P(), rows),
        out_specs=(rows, rows, first, wide, wide, wide, tall, first, wide, wide, tall),
        check_vma=False,
    )
```

```python
import functools
import math

import jax
import jax.numpy as jnp
from jax import lax
from jax.experimental import pallas as pl
from jax.experimental.layout import Layout, with_layout_constraint
from jax.experimental.pallas import tpu as pltpu
from jax.sharding import Mesh, PartitionSpec as P

HEAD = 96
LANES = 128
PIECE = 256
LEN_FIRST = 4096
LEN_LAST = 2048
LEN_MAX = 4096
epsilon = 1e-05
rope_base = 100000.0
negative = -1e30
far_away = 1 << 30
log2_e = 1.4426950408889634
score_scale = 1.0 / math.sqrt(HEAD)
BF = jnp.bfloat16
F32 = jnp.float32
AXES = ("g", "c", "zh", "zl")
MIB = 1024 * 1024
COST_SHARE = 0.01


def params(mib):
    return pltpu.CompilerParams(vmem_limit_bytes=mib * MIB)


def nn(left, right):
    return lax.dot_general(left, right, (((1,), (0,)), ((), ())), preferred_element_type=F32)


def nt(left, right):
    return lax.dot_general(left, right, (((1,), (1,)), ((), ())), preferred_element_type=F32)


def tn(left, right):
    return lax.dot_general(left, right, (((0,), (0,)), ((), ())), preferred_element_type=F32)


def after(value, *earlier):
    return lax.optimization_barrier((value, *earlier))[0]


def sync(*values):
    return lax.optimization_barrier(values)


def all_groups(value):
    return lax.all_gather(value, "g", axis=0, tiled=True)


def flip(value, axis, bit=1):
    count = lax.axis_size(axis)
    return lax.ppermute(value, axis, [(s, s ^ bit) for s in range(count)])


def cost(us):
    us = us * COST_SHARE
    return pl.CostEstimate(flops=int(us * 1.15e9), bytes_accessed=int(us * 3.6e6), transcendentals=0)


def gather_rows(own):
    beside = flip(own, "zl")
    across = flip(own, "c")
    both = flip(beside, "c")
    return [own, beside, across, both]


def from_groups(value):
    return [value] + [flip(value, "g", k) for k in range(1, lax.axis_size("g"))]


def split_core(shard):
    c = lax.axis_index("c")
    keep = lax.dynamic_index_in_dim(shard, c, 0, False)
    got = flip(lax.dynamic_index_in_dim(shard, 1 - c, 0, False), "c")
    return keep, got


def in_order(keep, got, axis=0):
    c = lax.axis_index("c")
    return jnp.where(c == 0, jnp.concatenate([keep, got], axis), jnp.concatenate([got, keep], axis))


def by_rows(value):
    return with_layout_constraint(value, Layout(major_to_minor=(0, 1)))


def over_groups(value):
    return lax.psum_scatter(value, "g", scatter_dimension=0, tiled=True)


def to_owner(mine):
    c = lax.axis_index("c")
    half = mine.shape[0] // 2
    own = lax.dynamic_slice_in_dim(mine, c * half, half, 0).astype(F32)
    got = flip(lax.dynamic_slice_in_dim(mine, (1 - c) * half, half, 0).astype(BF), "c").astype(F32)
    return own, got


def joined(own, got):
    return in_order(own, got, 1)


def swap_halves(value):
    lane = lax.broadcasted_iota(jnp.int32, value.shape, 1)
    return jnp.where(lane < HEAD // 2, pltpu.roll(value, LANES - HEAD // 2, 1), pltpu.roll(value, HEAD // 2, 1))


def turn(value, cosine, sine):
    return value * cosine + swap_halves(value) * sine


def unturn(value, cosine, sine):
    return value * cosine - swap_halves(value) * sine


def widen(value):
    pad = jnp.zeros((value.shape[0], LANES - HEAD), value.dtype)
    return jnp.concatenate([value, pad], 1)


def qkv_kernel(count, n_jumps, where_ref, *refs):
    pieces, refs = refs[: 2 * count], refs[2 * count :]
    jumps, refs = refs[:n_jumps], refs[n_jumps:]
    x0, x1, x_far, cos_ref, sin_ref, norm_ref, query_ref, kv_ref, weight_ref, gains_ref, x_ref = refs
    step = pl.program_id(0)

    @pl.when(step == 0)
    def _():
        half = pieces[0].shape[0] // 2

        def place(block, n, value):
            for part in range(2):
                at = pl.multiple_of(where_ref[2 * n + part], 64)
                weight_ref[block, pl.ds(at, half), :] = value[part * half : (part + 1) * half, :]

        for block in range(2):
            for n in range(count):
                place(block, n, pieces[block * count + n])
            for n in range(n_jumps):
                place(block, count + n, jumps[n][2 * half * block : 2 * half * (block + 1), :])
        row = lax.broadcasted_iota(jnp.int32, (8, LANES), 0)
        lane = lax.broadcasted_iota(jnp.int32, (8, LANES), 1)
        pick = jnp.where(row == lane, 1.0, 0.0).astype(BF)
        gains_ref[...] = nt(pick, weight_ref[0][:, 4 * HEAD :])

    for k in range(4):

        @pl.when(step == k)
        def _():
            x_ref[...] = (x0, x1)[k][...] if k < 2 else x_far[(k - 2) * PIECE : (k - 1) * PIECE, :]

    x = x_ref[...].astype(F32)
    r = lax.rsqrt(jnp.mean(x * x, axis=-1, keepdims=True) + epsilon)
    normed = (x * r * gains_ref[0:1, :]).astype(BF)
    norm_ref[0] = normed
    cosine, sine = cos_ref[0], sin_ref[0]
    packs = []
    for j in range(2):
        pre = nn(normed, weight_ref[j][:, 0 : 4 * HEAD])
        for h in range(2):
            turned = turn(widen(pre[:, h * HEAD : (h + 1) * HEAD]), cosine, sine)
            query_ref[j, 0, h * PIECE : (h + 1) * PIECE] = (turned * (score_scale * log2_e)).astype(BF)
        packs.append(turn(widen(pre[:, 2 * HEAD : 3 * HEAD]), cosine, sine)[:, 0:HEAD])
        packs.append(pre[:, 3 * HEAD :])
    kv_ref[...] = jnp.concatenate(packs, 1).astype(BF)


def project_qkv(where, pieces, jumps, x_rows, x_far, cos_table, sin_table):
    rows, width = x_rows[0].shape
    n_cols = pieces[0].shape[1]
    table = pl.BlockSpec((1, rows, LANES), lambda i, *_: (i, 0, 0))
    return pl.pallas_call(
        functools.partial(qkv_kernel, len(pieces) // 2, len(jumps)),
        grid_spec=pltpu.PrefetchScalarGridSpec(
            num_scalar_prefetch=1,
            grid=(4,),
            in_specs=[pl.BlockSpec(v.shape, lambda i, *_: (0, 0)) for v in (*pieces, *jumps, *x_rows, x_far)] + [table, table],
            out_specs=[
                pl.BlockSpec((1, rows, width), lambda i, *_: (i, 0, 0)),
                pl.BlockSpec((2, 1, 2 * rows, LANES), lambda i, *_: (0, i, 0, 0)),
                pl.BlockSpec((rows, 4 * HEAD), lambda i, *_: (i, 0)),
                pl.BlockSpec((2, width, n_cols), lambda i, *_: (0, 0, 0)),
                pl.BlockSpec((8, width), lambda i, *_: (0, 0)),
            ],
            scratch_shapes=[pltpu.VMEM((rows, width), BF)],
        ),
        out_shape=[
            jax.ShapeDtypeStruct((4, rows, width), BF),
            jax.ShapeDtypeStruct((2, 4, 2 * rows, LANES), BF),
            jax.ShapeDtypeStruct((4 * rows, 4 * HEAD), BF),
            jax.ShapeDtypeStruct((2, width, n_cols), BF),
            jax.ShapeDtypeStruct((8, width), F32),
        ],
        compiler_params=params(58),
        cost_estimate=cost(8),
        name="project_qkv",
    )(where, *pieces, *jumps, *x_rows, x_far, cos_table, sin_table)


def query_back_kernel(core_ref, dq_ref, weight_ref, cos_ref, sin_ref, grad_ref, share_ref):
    total = None
    for j in range(2):
        heads = []
        for h in range(2):
            turned = unturn(dq_ref[j, 0, h * PIECE : (h + 1) * PIECE], cos_ref[0], sin_ref[0])
            heads.append((turned * score_scale)[:, 0:HEAD])
        grad = jnp.concatenate(heads, 1).astype(BF)
        grad_ref[j, 0] = grad
        term = nt(grad, weight_ref[j][:, 0 : 2 * HEAD])
        total = term if total is None else total + term
    share_ref[0] = total.astype(BF)


def kv_back_kernel(n_same, has_above, core_ref, *refs):
    refs = list(refs)
    own_ref, first_ref, second_ref = refs[:3]
    same_refs = refs[3 : 3 + n_same]
    refs = refs[3 + n_same :]
    i = pl.program_id(0)
    late = i >= 2
    d_kv = own_ref[...] + jnp.where(late, second_ref[...], first_ref[...]).astype(F32)
    for ref in same_refs:
        d_kv = d_kv + ref[...].astype(F32)
    if has_above:
        d_kv = d_kv + jnp.where(i == core_ref[0], refs.pop(0)[...], 0).astype(F32)
    share_in_ref, weight_ref, cos_ref, sin_ref, grad_ref, share_ref = refs
    total = share_in_ref[0].astype(F32)
    for j in range(2):
        both = d_kv[:, 2 * HEAD * j : 2 * HEAD * (j + 1)]
        turned = unturn(widen(both[:, 0:HEAD]), cos_ref[0], sin_ref[0]) * (1.0 / log2_e)
        grad = jnp.concatenate([turned[:, 0:HEAD], both[:, HEAD:]], 1).astype(BF)
        grad_ref[j, 0] = grad
        total = total + nt(grad, weight_ref[j][:, 2 * HEAD : 4 * HEAD])
    share_ref[0] = total.astype(BF)


def project_back(kernel, core, args, specs, weights, cos_table, sin_table, name, mib):
    count, rows, _ = cos_table.shape
    width = weights.shape[1]
    piece = pl.BlockSpec((1, rows, width), lambda i, *_: (i, 0, 0))
    table = pl.BlockSpec((1, rows, cos_table.shape[2]), lambda i, *_: (i, 0, 0))
    return pl.pallas_call(
        kernel,
        grid_spec=pltpu.PrefetchScalarGridSpec(
            num_scalar_prefetch=1,
            grid=(count,),
            in_specs=specs + [pl.BlockSpec((2, width, 4 * HEAD), lambda i, *_: (0, 0, 0)), table, table],
            out_specs=[pl.BlockSpec((2, 1, rows, 2 * HEAD), lambda i, *_: (0, i, 0, 0)), piece],
        ),
        out_shape=[
            jax.ShapeDtypeStruct((2, count, rows, 2 * HEAD), BF),
            jax.ShapeDtypeStruct((count, rows, width), BF),
        ],
        compiler_params=params(mib),
        cost_estimate=cost(4),
        name=name,
    )(core, *args, weights, cos_table, sin_table)


def query_back(core, d_query, weights, cos_table, sin_table):
    spec = pl.BlockSpec((2, 1, 2 * PIECE, LANES), lambda i, *_: (0, i, 0, 0))
    return project_back(query_back_kernel, core, [d_query], [spec], weights, cos_table, sin_table, "query_back", 40)


def kv_back(core, own, other, same, above, shares, weights, cos_table, sin_table):
    rows = pl.BlockSpec((PIECE, 4 * HEAD), lambda i, *_: (i, 0))
    chunk = pl.BlockSpec((PIECE, 4 * HEAD), lambda i, *_: (i % 2, 0))
    args = [own, *other, *same, *above, shares]
    specs = [rows, chunk, chunk] + [rows] * len(same)
    specs += [pl.BlockSpec((PIECE, 4 * HEAD), lambda i, *_: (0, 0))] * len(above)
    specs.append(pl.BlockSpec((1, *shares.shape[1:]), lambda i, *_: (i, 0, 0)))
    kernel = functools.partial(kv_back_kernel, len(same), bool(above))
    return project_back(kernel, core, args, specs, weights, cos_table, sin_table, "kv_back", 58)


CHUNK = 2 * PIECE


def unpack_kv(swaps, block_refs, key_scratch, value_scratch):
    lane = lax.broadcasted_iota(jnp.int32, (CHUNK, LANES - HEAD), 1)
    ones = jnp.where(lane < 3, 1.0, 0.0).astype(BF)
    at = 0
    for swap, ref in zip(swaps, block_refs):
        for start in range(0, ref.shape[0], CHUNK):
            block = ref[start : start + CHUNK, :]
            for j in range(2):
                first = 2 * HEAD * (j ^ swap)
                k = block[:, first : first + HEAD]
                v = block[:, first + HEAD : first + 2 * HEAD]
                key_scratch[j, at : at + CHUNK, :] = jnp.concatenate([k, ones], 1)
                value_scratch[j, at : at + CHUNK, :] = jnp.concatenate([v, ones], 1)
            at += CHUNK


def chunk_state(info_ref, base, i):
    last = base + (CHUNK - 1)
    touched = (base <= info_ref[i, 3]) & (last >= info_ref[i, 0])
    full = (base >= info_ref[i, 1]) & (last <= info_ref[i, 2])
    return touched, full


def forward_kernel(swaps, first, last, offset, stride, n_kept, info_ref, base_ref, zl_ref, *refs):
    refs = list(refs)
    n_blocks = len(swaps)
    query_ref, low_ref, high_ref = refs[:3]
    block_refs = refs[3 : 3 + n_blocks]
    refs = refs[3 + n_blocks :]
    if not first:
        acc_in = refs.pop(0)
    refs = refs[n_kept:]
    if last:
        mixed_ref = refs.pop(0)
    kept_ref = refs.pop(0)
    key_scratch, value_scratch, acc, top = refs
    i = offset + stride * pl.program_id(0)

    @pl.when(pl.program_id(0) == 0)
    def _():
        unpack_kv(swaps, block_refs, key_scratch, value_scratch)

    for j in range(2):
        if first:
            acc[j] = jnp.zeros((CHUNK, LANES), F32)
            top[j] = jnp.full((CHUNK, LANES), negative, F32)
        else:
            acc[j] = acc_in[j, 0]
            top[j] = jnp.broadcast_to(acc_in[j, 0][:, HEAD + 1 : HEAD + 2], (CHUNK, LANES))
    n_chunks = sum(r.shape[0] for r in block_refs) // CHUNK

    def visit(n, masked):
        rows = pl.ds(pl.multiple_of(n * CHUNK, CHUNK), CHUNK)
        if masked:
            at = lax.broadcasted_iota(jnp.int32, (PIECE, CHUNK), 1)
            token = base_ref[n] + lax.rem(at + zl_ref[0] * PIECE, CHUNK)
            low = jnp.concatenate([low_ref[0]] * (CHUNK // LANES), 1)
            high = jnp.concatenate([high_ref[0]] * (CHUNK // LANES), 1)
            allowed = (token >= low) & (token <= high)
        for j in range(2):
            scores = nt(query_ref[j, 0], key_scratch[j, rows, :])
            if masked:
                scores = jnp.concatenate(
                    [jnp.where(allowed, scores[h * PIECE : (h + 1) * PIECE], negative) for h in range(2)], 0
                )
            old = top[j]
            new = jnp.maximum(old, jnp.max(scores, axis=1, keepdims=True))
            top[j] = new
            probs = jnp.exp2(scores - jnp.concatenate([new] * (CHUNK // LANES), 1)).astype(BF)
            acc[j] = acc[j] * jnp.exp2(old - new) + nn(probs, value_scratch[j, rows, :])

    @pl.loop(0, n_chunks)
    def _(n):
        touched, full = chunk_state(info_ref, base_ref[n], i)

        @pl.when(touched & full)
        def _():
            visit(n, False)

        @pl.when(touched & jnp.logical_not(full))
        def _():
            visit(n, True)

    lane = lax.broadcasted_iota(jnp.int32, (CHUNK, LANES), 1)
    if last:
        for j in range(2):
            total = acc[j][:, HEAD : HEAD + 1]
            out = acc[j] / total
            kept_ref[j, 0] = jnp.where(lane < HEAD, out, top[j] + jnp.log2(total))
            mixed_ref[j, 0] = jnp.concatenate([out[0:PIECE, 0:HEAD], out[PIECE:, 0:HEAD]], 1).astype(BF)
    else:
        for j in range(2):
            kept_ref[j, 0] = jnp.where(lane == HEAD + 1, top[j], acc[j])


def attend(query, low, high, info, bases, zl, blocks, swaps, state, last, offset=0, stride=1, kept=()):
    count = query.shape[1]
    n_keys = sum(b.shape[0] for b in blocks)
    per_piece = pl.BlockSpec((2, 1, CHUNK, LANES), lambda i, *_: (0, offset + stride * i, 0, 0))
    bound = pl.BlockSpec((1, PIECE, LANES), lambda i, *_: (offset + stride * i, 0, 0))
    in_specs = [per_piece, bound, bound]
    in_specs += [pl.BlockSpec(b.shape, lambda i, *_: (0, 0)) for b in blocks]
    args = [query, low, high, *blocks]
    if state is not None:
        in_specs.append(per_piece)
        args.append(state)
    aliases = {3 + len(args) + n: n for n in range(len(kept))}
    in_specs += [pl.BlockSpec(memory_space=pl.ANY)] * len(kept)
    args += list(kept)
    wide = jax.ShapeDtypeStruct((2, count, CHUNK, LANES), F32)
    if last:
        out_shape = [jax.ShapeDtypeStruct((2, count, PIECE, 2 * HEAD), BF), wide]
        out_specs = [pl.BlockSpec((2, 1, PIECE, 2 * HEAD), lambda i, *_: (0, offset + stride * i, 0, 0)), per_piece]
    else:
        out_shape = wide
        out_specs = per_piece
    return pl.pallas_call(
        functools.partial(forward_kernel, swaps, state is None, last, offset, stride, len(kept)),
        grid_spec=pltpu.PrefetchScalarGridSpec(
            num_scalar_prefetch=3,
            grid=(count // stride,),
            in_specs=in_specs,
            out_specs=out_specs,
            scratch_shapes=[
                pltpu.VMEM((2, n_keys, LANES), BF),
                pltpu.VMEM((2, n_keys, LANES), BF),
                pltpu.VMEM((2, CHUNK, LANES), F32),
                pltpu.VMEM((2, CHUNK, LANES), F32),
            ],
        ),
        out_shape=out_shape,
        input_output_aliases=aliases,
        compiler_params=params(48),
        cost_estimate=cost(n_keys / 100),
        name="attend",
    )(info, bases, zl, *args)


def split_three(value):
    first = value.astype(BF)
    rest = value - first.astype(F32)
    second = rest.astype(BF)
    third = (rest - second.astype(F32)).astype(BF)
    return first, second, third


def augment(wide, extra):
    lane = lax.broadcasted_iota(jnp.int32, wide.shape, 1)
    a, b, c = (part.astype(F32) for part in split_three(extra))
    out = wide.astype(F32)
    out = jnp.where(lane == HEAD, a, out)
    out = jnp.where(lane == HEAD + 1, b, out)
    out = jnp.where(lane == HEAD + 2, c, out)
    return out.astype(BF)


def prepare_kernel(n_kept, m0, m1, w0, w1, kept_ref, query_ref, *refs):
    q_aug_ref, o_aug_ref, mid_ref = refs[n_kept:]
    step = pl.program_id(0)
    for k, ref in enumerate((m0, m1)):

        @pl.when(step == k)
        def _():
            mid_ref[...] = ref[...]

    mid = mid_ref[...]
    for j, weight_ref in enumerate((w0, w1)):
        grad = nn(mid, weight_ref[...][:, 0 : 2 * HEAD])
        wide = jnp.concatenate([widen(grad[:, 0:HEAD]), widen(grad[:, HEAD : 2 * HEAD])], 0).astype(BF)
        kept = kept_ref[j, 0]
        delta = jnp.sum(wide.astype(F32) * kept, axis=1, keepdims=True)
        q_aug_ref[j, 0] = augment(query_ref[j, 0], -kept[:, HEAD : HEAD + 1])
        o_aug_ref[j, 0] = augment(wide, -delta)


def prepare_back(mid, offset, weights, tile, kept, query, done=()):
    rows, width = mid[0].shape
    per_piece = pl.BlockSpec((2, 1, CHUNK, LANES), lambda i: (0, offset + 2 * i, 0, 0))
    return pl.pallas_call(
        functools.partial(prepare_kernel, len(done)),
        grid=(2,),
        in_specs=[pl.BlockSpec((rows, width), lambda i: (0, 0))] * 2
        + [pl.BlockSpec((width, 256), lambda i: (0, tile))] * 2
        + [per_piece, per_piece]
        + [pl.BlockSpec(memory_space=pl.ANY)] * len(done),
        out_specs=[per_piece, per_piece],
        out_shape=[jax.ShapeDtypeStruct(query.shape, BF)] * 2,
        scratch_shapes=[pltpu.VMEM((rows, width), BF)],
        input_output_aliases={6 + n: n for n in range(len(done))},
        compiler_params=params(58),
        cost_estimate=cost(6),
        name="prepare_back",
    )(*mid, *weights, kept, query, *done)


def backward_kernel(swaps, has_dq, offset, stride, n_kept, info_ref, base_ref, zl_ref, *refs):
    refs = list(refs)
    n_blocks = len(swaps)
    q_aug, o_aug, low_ref, high_ref = refs[:4]
    block_refs = refs[4 : 4 + n_blocks]
    refs = refs[4 + n_blocks :]
    if has_dq:
        dq_in = refs.pop(0)
    refs = refs[n_kept:]
    dq_ref = refs.pop(0)
    out_refs = refs[:n_blocks]
    key_scratch, value_scratch, d_key, d_value = refs[n_blocks:]
    i = offset + stride * pl.program_id(0)

    @pl.when(pl.program_id(0) == 0)
    def _():
        unpack_kv(swaps, block_refs, key_scratch, value_scratch)
        d_key[...] = jnp.zeros(d_key.shape, F32)
        d_value[...] = jnp.zeros(d_value.shape, F32)

    for j in range(2):
        if has_dq:
            dq_ref[j, 0] = dq_in[j, 0]
        else:
            dq_ref[j, 0] = jnp.zeros((CHUNK, LANES), F32)
    n_chunks = sum(r.shape[0] for r in block_refs) // CHUNK

    def visit(n, masked):
        rows = pl.ds(pl.multiple_of(n * CHUNK, CHUNK), CHUNK)
        if masked:
            at = lax.broadcasted_iota(jnp.int32, (CHUNK, CHUNK), 0)
            token = base_ref[n] + lax.rem(at + zl_ref[0] * PIECE, CHUNK)
            allowed = (token >= low_ref[0, 0:1, :]) & (token <= high_ref[0, 0:1, :])
        for j in range(2):
            keys = key_scratch[j, rows, :]
            probs = jnp.exp2(nt(keys, q_aug[j, 0]))
            if masked:
                probs = jnp.where(allowed, probs, 0.0)
            d_probs = nt(value_scratch[j, rows, :], o_aug[j, 0])
            low_probs = probs.astype(BF)
            d_scores = (probs * d_probs).astype(BF)
            d_value[j, rows, :] += nn(low_probs, o_aug[j, 0])
            d_key[j, rows, :] += nn(d_scores, q_aug[j, 0])
            dq_ref[j, 0] += tn(d_scores, keys)

    @pl.loop(0, n_chunks)
    def _(n):
        touched, full = chunk_state(info_ref, base_ref[n], i)

        @pl.when(touched & full)
        def _():
            visit(n, False)

        @pl.when(touched & jnp.logical_not(full))
        def _():
            visit(n, True)

    @pl.when(pl.program_id(0) == pl.num_programs(0) - 1)
    def _():
        at = 0
        for swap, ref in zip(swaps, out_refs):
            for start in range(0, ref.shape[0], CHUNK):
                parts = []
                for j in (swap, 1 - swap):
                    parts.append(d_key[j, at : at + CHUNK, :][:, 0:HEAD])
                    parts.append(d_value[j, at : at + CHUNK, :][:, 0:HEAD])
                ref[start : start + CHUNK, :] = jnp.concatenate(parts, 1).astype(ref.dtype)
                at += CHUNK


def attend_back(q_aug, o_aug, low, high, info, bases, zl, blocks, swaps, d_query, kinds, offset=0, stride=1, kept=()):
    count = q_aug.shape[1]
    n_keys = sum(b.shape[0] for b in blocks)
    per_piece = pl.BlockSpec((2, 1, CHUNK, LANES), lambda i, *_: (0, offset + stride * i, 0, 0))
    bound = pl.BlockSpec((1, 8, CHUNK), lambda i, *_: (offset + stride * i, 0, 0))
    whole = [pl.BlockSpec(b.shape, lambda i, *_: (0, 0)) for b in blocks]
    in_specs = [per_piece, per_piece, bound, bound, *whole]
    args = [q_aug, o_aug, low, high, *blocks]
    if d_query is not None:
        in_specs.append(per_piece)
        args.append(d_query)
    aliases = {3 + len(args) + n: n for n in range(len(kept))}
    in_specs += [pl.BlockSpec(memory_space=pl.ANY)] * len(kept)
    args += list(kept)
    return pl.pallas_call(
        functools.partial(backward_kernel, swaps, d_query is not None, offset, stride, len(kept)),
        grid_spec=pltpu.PrefetchScalarGridSpec(
            num_scalar_prefetch=3,
            grid=(count // stride,),
            in_specs=in_specs,
            out_specs=[per_piece, *whole],
            scratch_shapes=[
                pltpu.VMEM((2, n_keys, LANES), BF),
                pltpu.VMEM((2, n_keys, LANES), BF),
                pltpu.VMEM((2, n_keys, LANES), F32),
                pltpu.VMEM((2, n_keys, LANES), F32),
            ],
        ),
        out_shape=[jax.ShapeDtypeStruct((2, count, CHUNK, LANES), F32)]
        + [jax.ShapeDtypeStruct(b.shape, k) for b, k in zip(blocks, kinds)],
        input_output_aliases=aliases,
        compiler_params=params(56),
        cost_estimate=cost(n_keys / 64),
        name="attend_back",
    )(info, bases, zl, *args)


def ffn_kernel(tiles, n0, n1, g0, g1, *refs):
    own_refs, other_refs, refs = refs[0:3], refs[3:6], refs[6:]
    o0, o1, b0, b1, hidden_ref, dg_ref, du_ref, norm_t, grad_t, norm_ref, grad_ref, acc_out, acc_back = refs
    step = pl.program_id(0)

    @pl.when(step == 0)
    def _():
        norm_ref[0:PIECE] = n0[...]
        norm_ref[PIECE:] = n1[...]
        grad_ref[0:PIECE] = g0[...]
        grad_ref[PIECE:] = g1[...]

    def run(gate_ref, up_ref, down_ref, first):
        gate_w, up_w, down_w = gate_ref[...], up_ref[...], down_ref[...]
        gate = nn(norm_ref[...], gate_w)
        up = nn(norm_ref[...], up_w)
        d_hidden = nn(grad_ref[...], down_w)
        sig = 0.5 * jnp.tanh(0.5 * gate) + 0.5
        silu = gate * sig
        hidden = (silu * up).astype(BF)
        d_gate = (d_hidden * up * (sig + silu * (1.0 - sig))).astype(BF)
        d_up = (d_hidden * silu).astype(BF)
        hidden_ref[...] = hidden
        dg_ref[...] = d_gate
        du_ref[...] = d_up
        norm_t[...] = norm_ref[pl.ds(pl.multiple_of(step * LANES, LANES), LANES), :].T
        grad_t[...] = grad_ref[pl.ds(pl.multiple_of(step * LANES, LANES), LANES), :].T
        out = nt(hidden, down_w)
        back = nt(d_gate, gate_w) + nt(d_up, up_w)
        if first:
            acc_out[...] = out
            acc_back[...] = back
        else:
            acc_out[...] += out
            acc_back[...] += back

    @pl.when(step == 0)
    def _():
        run(*own_refs, True)

    @pl.when((step > 0) & (step < tiles))
    def _():
        run(*own_refs, False)

    @pl.when(step >= tiles)
    def _():
        run(*other_refs, False)

    @pl.when(step == pl.num_programs(0) - 1)
    def _():
        o0[...] = acc_out[0:PIECE].astype(BF)
        o1[...] = acc_out[PIECE:].astype(BF)
        b0[...] = acc_back[0:PIECE].astype(BF)
        b1[...] = acc_back[PIECE:].astype(BF)


def feed_forward(norm_rows, grad_rows, own, other):
    rows, width = norm_rows[0].shape
    half = 512
    tile = 256
    tiles = half // tile
    whole = pl.BlockSpec((rows, width), lambda s: (0, 0))

    def own_spec(at):
        return pl.BlockSpec((width, tile), lambda s: (0, at // tile + jnp.minimum(s, tiles - 1)))

    def other_spec(at):
        return pl.BlockSpec((width, tile), lambda s: (0, at // tile + jnp.maximum(s - tiles, 0)))

    hid = pl.BlockSpec((2 * rows, tile), lambda s: (0, s))
    turned = pl.BlockSpec((width, LANES), lambda s: (0, s))
    return pl.pallas_call(
        functools.partial(ffn_kernel, tiles),
        grid=(2 * tiles,),
        in_specs=[whole] * 4 + [own_spec(at) for _, at in own] + [other_spec(at) for _, at in other],
        out_specs=[whole] * 4 + [hid] * 3 + [turned] * 2,
        out_shape=[jax.ShapeDtypeStruct((rows, width), BF)] * 4
        + [jax.ShapeDtypeStruct((2 * rows, 2 * half), BF)] * 3
        + [jax.ShapeDtypeStruct((width, 2 * rows), BF)] * 2,
        scratch_shapes=[pltpu.VMEM((2 * rows, width), BF)] * 2 + [pltpu.VMEM((2 * rows, width), F32)] * 2,
        compiler_params=params(56),
        cost_estimate=cost(18),
        name="feed_forward",
    )(*norm_rows, *grad_rows, *(w for w, _ in own), *(w for w, _ in other))


def weight_grad_kernel(n_jobs, *refs):
    out_ref = refs[-1]
    for n in range(n_jobs):
        left_early, left_late, early, late = refs[4 * n : 4 * n + 4]

        @pl.when(pl.program_id(1) == n)
        def _():
            total = nn(left_early[...], early[...]) + nn(left_late[...], late[...])
            out_ref[...] = total.astype(BF)


def weight_grad(jobs, us):
    width, depth = jobs[0][0].shape
    half = jobs[0][2].shape[1] // 2
    count = len(jobs)
    left = pl.BlockSpec((width, depth), lambda s, n: (0, 0))
    cols = pl.BlockSpec((depth, half), lambda s, n: (0, s))
    return pl.pallas_call(
        functools.partial(weight_grad_kernel, count),
        grid=(2, count),
        in_specs=[left, left, cols, cols] * count,
        out_specs=pl.BlockSpec((width, half), lambda s, n: (0, s * count + n)),
        out_shape=jax.ShapeDtypeStruct((width, 2 * count * half), BF),
        compiler_params=params(48),
        cost_estimate=cost(us),
        name="weight_grad",
    )(*(value for job in jobs for value in job))


def head_grad_kernel(l0, l1, l2, l3, right_ref, out_ref):
    for j in range(2):
        total = None
        for k, left in enumerate((l0, l1, l2, l3)):
            term = tn(left[...], right_ref[j, k])
            total = term if total is None else total + term
        wide = jnp.concatenate([total, jnp.zeros((total.shape[0], 256 - 2 * HEAD), F32)], 1)
        out_ref[:, j * 256 : (j + 1) * 256] = wide.astype(BF)


def head_grad(left, right):
    rows, width = left[0].shape
    tile = 512
    return pl.pallas_call(
        head_grad_kernel,
        grid=(width // tile,),
        in_specs=[pl.BlockSpec((rows, tile), lambda s: (0, s))] * 4 + [pl.BlockSpec(right.shape, lambda s: (0, 0, 0, 0))],
        out_specs=pl.BlockSpec((tile, 512), lambda s: (s, 0)),
        out_shape=jax.ShapeDtypeStruct((width, 512), BF),
        compiler_params=params(40),
        cost_estimate=cost(3),
        name="head_grad",
    )(*left, right)


def gain_kernel(lane, *refs):
    out_ref = refs[-1]
    count = (len(refs) - 1) // 2
    at = lax.broadcasted_iota(jnp.int32, (PIECE, LANES), 1)
    pick = jnp.where(at == lane, 1.0, 0.0).astype(BF)
    total = None
    for share, normed in zip(refs[:count], refs[count : 2 * count]):
        product = (share[...].astype(F32) * normed[...].astype(F32)).astype(BF)
        term = tn(product, pick)
        total = term if total is None else total + term
    out_ref[...] = total


def gain_columns(shares, normed, lane):
    rows, width = shares[0].shape
    tile = 512
    spec = pl.BlockSpec((rows, tile), lambda s: (0, s))
    return pl.pallas_call(
        functools.partial(gain_kernel, lane),
        grid=(width // tile,),
        in_specs=[spec] * 8,
        out_specs=pl.BlockSpec((tile, LANES), lambda s: (s, 0)),
        out_shape=jax.ShapeDtypeStruct((width, LANES), F32),
        compiler_params=params(40),
        cost_estimate=cost(3),
        name="gain_columns",
    )(*shares, *normed)


def kv_grad_kernel(norm_ref, share_ref, dkv_ref, column_ref, *refs):
    out_ref = refs[-1]
    at = lax.broadcasted_iota(jnp.int32, (PIECE, LANES), 1)
    pick = jnp.where(at == 0, 1.0, 0.0).astype(BF)
    columns = column_ref[...]
    totals = [None, None]
    for k in range(4):
        normed = norm_ref[k]
        product = (share_ref[k].astype(F32) * normed.astype(F32)).astype(BF)
        columns = columns + tn(product, pick)
        for j in range(2):
            term = tn(normed, dkv_ref[j, k])
            totals[j] = term if totals[j] is None else totals[j] + term
    for j in range(2):
        out_ref[:, j * 256 : (j + 1) * 256] = jnp.concatenate([totals[j], columns[:, 0 : 256 - 2 * HEAD]], 1).astype(BF)


def kv_grad(normed, shares, d_kvs, columns):
    count, rows, width = normed.shape
    tile = 512
    spec = pl.BlockSpec((count, rows, tile), lambda s: (0, 0, s))
    return pl.pallas_call(
        kv_grad_kernel,
        grid=(width // tile,),
        in_specs=[
            spec,
            spec,
            pl.BlockSpec(d_kvs.shape, lambda s: (0, 0, 0, 0)),
            pl.BlockSpec((tile, LANES), lambda s: (s, 0)),
        ],
        out_specs=pl.BlockSpec((tile, 512), lambda s: (s, 0)),
        out_shape=jax.ShapeDtypeStruct((width, 512), BF),
        compiler_params=params(40),
        cost_estimate=cost(4),
        name="kv_grad",
    )(normed, shares, d_kvs, columns)


def output_kernel(mixed_ref, w0, w1, far_ref, near_ref):
    step = pl.program_id(0)
    total = None
    for j, weight in enumerate((w0, w1)):
        term = nt(mixed_ref[j, 0], weight[...][:, 0 : 2 * HEAD])
        total = term if total is None else total + term

    @pl.when(step == 0)
    def _():
        far_ref[...] = total.astype(BF)

    @pl.when(step == 1)
    def _():
        near_ref[...] = total


def output_projection(mixed, offset, weights, tile):
    _, count, rows, width_heads = mixed.shape
    width = weights[0].shape[0]
    whole = pl.BlockSpec((rows, width), lambda s: (0, 0))
    return pl.pallas_call(
        output_kernel,
        grid=(2,),
        in_specs=[pl.BlockSpec((2, 1, rows, width_heads), lambda s: (0, offset + 2 * (1 - s), 0, 0))]
        + [pl.BlockSpec((width, 256), lambda s: (0, tile))] * 2,
        out_specs=[whole, whole],
        out_shape=[jax.ShapeDtypeStruct((rows, width), BF), jax.ShapeDtypeStruct((rows, width), F32)],
        compiler_params=params(58),
        cost_estimate=cost(4),
        name="output_projection",
    )(mixed, *weights)


def add_kernel(near_ref, across_ref, out_ref):
    out_ref[...] = (near_ref[...].astype(F32) + across_ref[...].astype(F32)).astype(BF)


def add_rows(near, near_at, across, across_at):
    rows, width = PIECE, near.shape[1]
    return pl.pallas_call(
        add_kernel,
        grid=(1,),
        in_specs=[
            pl.BlockSpec((rows, width), lambda s: (near_at, 0)),
            pl.BlockSpec((rows, width), lambda s: (across_at, 0)),
        ],
        out_specs=pl.BlockSpec((rows, width), lambda s: (0, 0)),
        out_shape=jax.ShapeDtypeStruct((rows, width), BF),
        compiler_params=params(32),
        cost_estimate=cost(1),
        name="add_rows",
    )(near, across)


def forward_norm_kernel(x_ref, near_ref, across_ref, beside_ref, gain_ref, after_ref, norm_ref):
    rows = x_ref[...].astype(F32) + (near_ref[...] + across_ref[...].astype(F32) + beside_ref[...].astype(F32))
    after_ref[...] = rows
    r = lax.rsqrt(jnp.mean(rows * rows, axis=-1, keepdims=True) + epsilon)
    norm_ref[...] = (rows * r * gain_ref[1:2, :]).astype(BF)


def row_specs(width, n):
    return [pl.BlockSpec((LANES, width), lambda i: (i, 0))] * n


def forward_norm(x, near, across, beside, gain_rows):
    rows, width = x.shape
    return pl.pallas_call(
        forward_norm_kernel,
        grid=(rows // LANES,),
        in_specs=row_specs(width, 4) + [pl.BlockSpec((8, width), lambda i: (0, 0))],
        out_specs=row_specs(width, 2),
        out_shape=[jax.ShapeDtypeStruct((rows, width), F32), jax.ShapeDtypeStruct((rows, width), BF)],
        compiler_params=params(32),
        cost_estimate=cost(2),
        name="forward_norm",
    )(x, near, across, beside, gain_rows)


def backward_norm_kernel(which, share_ref, across_ref, beside_ref, rows_ref, base_ref, gain_ref, *out_refs):
    upstream = share_ref[...].astype(F32) + across_ref[...].astype(F32) + beside_ref[...].astype(F32)
    rows = rows_ref[...].astype(F32)
    r = lax.rsqrt(jnp.mean(rows * rows, axis=-1, keepdims=True) + epsilon)
    weighted = upstream * gain_ref[which : which + 1, :]
    inner = jnp.mean(weighted * rows, axis=-1, keepdims=True)
    out = base_ref[...].astype(F32) + (r * weighted - rows * (r * r * r) * inner)
    for ref in out_refs:
        ref[...] = out.astype(ref.dtype)


def backward_norm(which, share, across, beside, rows, base, gain_rows, kinds):
    count, width = rows.shape
    return pl.pallas_call(
        functools.partial(backward_norm_kernel, which),
        grid=(count // LANES,),
        in_specs=row_specs(width, 5) + [pl.BlockSpec((8, width), lambda i: (0, 0))],
        out_specs=row_specs(width, len(kinds)),
        out_shape=[jax.ShapeDtypeStruct((count, width), kind) for kind in kinds],
        compiler_params=params(32),
        cost_estimate=cost(2),
        name="backward_norm",
    )(share, across, beside, rows, base, gain_rows)


def token_tables(token, seq_lengths, piece_starts):
    n = seq_lengths.shape[0]
    upto = jnp.arange(n)[None, :] <= jnp.arange(n)[:, None]
    ends = jnp.sum(jnp.where(upto, seq_lengths[None, :], 0), axis=1)
    after = token[:, None] >= ends[None, :]
    start = jnp.sum(jnp.where(after, seq_lengths[None, :], 0), axis=1)
    end = jnp.min(jnp.where(after, far_away, ends[None, :]), axis=1)
    inside = (token[:, None] >= piece_starts[None, :]) & (token[:, None] < piece_starts[None, :] + PIECE)
    piece_end = jnp.max(jnp.where(inside, piece_starts[None, :] + PIECE, 0), axis=1)
    high = jnp.maximum(token, jnp.minimum(piece_end, end) - 1)
    return start, high


def may_meet(one, two, group_tokens, count):
    total = group_tokens * count
    regions = ((0, LEN_FIRST, LEN_FIRST), (LEN_FIRST, total - LEN_LAST, LEN_MAX), (total - LEN_LAST, total, LEN_LAST))
    for start, end, longest in regions:
        both = all(g * group_tokens < end and (g + 1) * group_tokens > start for g in (one, two))
        if both and (abs(one - two) - 1) * group_tokens + 1 < longest:
            return True
    return False


def body(
    inputs,
    first_gain,
    query_weight,
    key_matrix,
    value_matrix,
    output_weight,
    second_gain,
    gate_weight,
    up_weight,
    down_weight,
    seq_lengths,
    piece_starts,
    out_cotangent,
):
    g, c, zh, zl = (lax.axis_index(a) for a in AXES)
    groups = lax.axis_size("g")
    rows, width = inputs.shape
    span = 4 * rows
    group_tokens = 2 * span
    shard_rows = query_weight.shape[0]

    order = jnp.arange(4)
    piece_base = (2 * g + (c ^ (order >> 1))) * span + zh * CHUNK + (zl ^ (order & 1)) * rows
    token = (piece_base[:, None] + jnp.arange(rows)[None, :]).reshape(-1).astype(jnp.int32)
    low, high = token_tables(token, seq_lengths, piece_starts)
    position = (token - low).astype(F32)
    low, high = low.reshape(4, rows), high.reshape(4, rows)
    info = jnp.stack([low.min(1), low.max(1), high.min(1), high.max(1)], 1).astype(jnp.int32)
    low_wide = jnp.broadcast_to(low[:, :, None], (4, rows, LANES)).astype(jnp.int32)
    high_wide = jnp.broadcast_to(high[:, :, None], (4, rows, LANES)).astype(jnp.int32)
    low_rows = jnp.broadcast_to(jnp.tile(low, (1, 2))[:, None, :], (4, 8, CHUNK)).astype(jnp.int32)
    high_rows = jnp.broadcast_to(jnp.tile(high, (1, 2))[:, None, :], (4, 8, CHUNK)).astype(jnp.int32)
    zl_info = jnp.reshape(zl, (1,)).astype(jnp.int32)
    frequency = rope_base ** (-(2.0 / HEAD) * jnp.arange(HEAD // 2, dtype=F32))
    angles = position[:, None] * frequency[None, :]
    cosine, sine = jnp.cos(angles), jnp.sin(angles)
    pad = jnp.zeros((span, LANES - HEAD), F32)
    cos_table = jnp.concatenate([cosine, cosine, pad], 1).reshape(4, rows, LANES)
    sin_table = jnp.concatenate([-sine, sine, pad], 1).reshape(4, rows, LANES)

    def halves(matrix):
        return matrix.reshape(matrix.shape[0], 2, -1).transpose(1, 0, 2)

    blank = functools.partial(jnp.zeros, dtype=BF)
    half = gate_weight.shape[1] // 2
    zl_info = jnp.reshape(zl, (1,)).astype(jnp.int32)
    core = jnp.reshape(2 * c + zl, (1,)).astype(jnp.int32)
    shard_pair = 2 * shard_rows

    gains = jnp.broadcast_to(jnp.stack([first_gain, second_gain], 1)[None], (2, shard_rows, 2))
    qkv_shard = jnp.concatenate(
        [halves(query_weight), halves(key_matrix), halves(value_matrix), gains, blank((2, shard_rows, 126))], 2
    )
    qkv_keep, qkv_got = split_core(qkv_shard)
    ffn_shard = jnp.concatenate(
        [halves(gate_weight), halves(output_weight.T), blank((2, shard_rows, 64)), halves(up_weight), halves(down_weight.T)],
        2,
    )
    ffn_keep, ffn_got = split_core(ffn_shard)
    qkv_pair = jnp.concatenate([qkv_keep, qkv_got], 0)
    inputs, out_cotangent, qkv_pair, ffn_keep, ffn_got = sync(inputs, out_cotangent, qkv_pair, ffn_keep, ffn_got)

    qkv_other = flip(qkv_pair, "zh")
    hops = [k for k in range(1, groups) if k & -k == k]
    jumps = [k for k in range(1, groups) if k & -k != k]
    qkv_near = [flip(qkv_pair, "g", k) for k in (*hops, *jumps)]
    x_beside = flip(inputs, "zl")
    ffn_pair = in_order(ffn_keep, ffn_got)
    up_at = half + 2 * HEAD + 64
    first_pair = ffn_pair[:, :up_at]
    up_pair, down_pair = ffn_pair[:, up_at : up_at + half], ffn_pair[:, up_at + half :]
    (
        qkv_other, qkv_near, x_beside, ffn_pair, first_pair, up_pair, down_pair, cos_table, sin_table,
        info, low_wide, high_wide, low_rows, high_rows,
    ) = sync(
        qkv_other, qkv_near, x_beside, ffn_pair, first_pair, up_pair, down_pair, cos_table, sin_table,
        info, low_wide, high_wide, low_rows, high_rows,
    )
    x_near = jnp.concatenate([inputs, x_beside], 0)

    ffn_own = all_groups(ffn_pair)
    qkv_far = [flip(qkv_other, "g", k) for k in (*hops, *jumps)]
    x_far = flip(x_near, "c")
    first_other = flip(first_pair, "zh")
    qkv_far, x_far, first_other, up_pair, out_cotangent = sync(qkv_far, x_far, first_other, up_pair, out_cotangent)

    up_other = flip(up_pair, "zh")
    g_beside = flip(out_cotangent, "zl")
    k_order = jnp.array([0, *hops, *jumps])[:, None]
    piece_rows = (g ^ k_order) * shard_pair + (c ^ jnp.arange(2)[None, :]) * shard_rows
    norm_one, query, kv, qkv_w, gain_rows = project_qkv(
        piece_rows.reshape(-1).astype(jnp.int32),
        [qkv_pair, *qkv_near, qkv_other, *qkv_far],
        [],
        [inputs, x_beside],
        x_far,
        cos_table,
        sin_table,
    )
    first_piece = lax.dynamic_slice_in_dim(kv, (2 * c + zl) * rows, rows, 0)
    norm_one, query, kv, qkv_w, gain_rows, kv_chunks, first_piece, out_cotangent, g_beside, up_other, down_pair, first_other = sync(
        norm_one,
        query,
        kv,
        qkv_w,
        gain_rows,
        [kv[n * CHUNK : (n + 1) * CHUNK] for n in range(2)],
        first_piece,
        out_cotangent,
        g_beside,
        up_other,
        down_pair,
        first_other,
    )
    first_far = all_groups(first_other)

    def chunk_bases(group, side):
        return jnp.stack([(2 * group + (c ^ i)) * span + side * CHUNK for i in range(2)]).astype(jnp.int32)

    def shift_pairs(steps):
        return [(s, s + steps) for s in range(groups) if 0 <= s + steps < groups and may_meet(s, s + steps, group_tokens, groups)]

    def present(pairs, bases):
        target = functools.reduce(jnp.logical_or, [g == t for _, t in pairs])
        return jnp.where(target, bases, far_away).astype(jnp.int32)

    def reverse(pairs):
        return [(t, s) for s, t in pairs]

    shifts = [d for d in range(1, groups) if shift_pairs(d)]
    above_groups = [s for s in range(1, groups) if may_meet(s - 1, s, group_tokens, groups)]
    above_pairs = [(2 * s, 2 * (s - 1) + 1) for s in above_groups]
    own_bases, other_bases = chunk_bases(g, zh), chunk_bases(g, 1 - zh)
    same_bases = [present(shift_pairs(d), chunk_bases(g - d, zh)) for d in shifts]
    far_bases = [present(shift_pairs(d), chunk_bases(g - d, 1 - zh)) for d in shifts]
    if above_groups:
        is_target = functools.reduce(jnp.logical_or, [(g == s - 1) & (zh == 1) for s in above_groups])
        far_bases.append(jnp.where(is_target, jnp.reshape(2 * (g + 1) * span, (1,)), far_away).astype(jnp.int32))
    same_bases, far_bases = jnp.concatenate(same_bases), jnp.concatenate(far_bases)

    def step(blocks, bases, swap, state, *choice):
        swaps = [swap] * len(blocks)
        return attend(query, low_wide, high_wide, info, bases, zl_info, blocks, swaps, state, bool(choice), *choice)

    other = [flip(kv_chunks[0], "zh")]
    same = [lax.ppermute(kv, "g", shift_pairs(d)) for d in shifts]
    g_across = flip(out_cotangent, "c")
    state = step([kv], own_bases, 0, None)
    other, same, g_across, state, kv_late = sync(other, same, g_across, state, kv_chunks[1])

    other.append(flip(kv_late, "zh"))
    far_blocks = [[lax.ppermute(other[0], "g", shift_pairs(d))] for d in shifts]
    g_both = flip(g_beside, "c")
    state = step(same, same_bases, 0, state)
    other, far_blocks, g_both, state, down_pair, first_piece, ffn_own = sync(
        other, far_blocks, g_both, state, down_pair, first_piece, ffn_own
    )

    for n, d in enumerate(shifts):
        far_blocks[n].append(lax.ppermute(other[1], "g", shift_pairs(d)))
    far_blocks = [b for pair in far_blocks for b in pair]
    if above_groups:
        above = lax.ppermute(first_piece, ("g", "zh"), above_pairs)
        far_blocks.append(lax.dynamic_update_slice(jnp.zeros((CHUNK, 4 * HEAD), BF), above, (zl * rows, 0)))
    down_other = flip(down_pair, "zh")
    state = step(other, other_bases, 1, state)
    far_blocks, down_other, state = sync(far_blocks, down_other, state)

    second_far = all_groups(jnp.concatenate([up_other, down_other], 1))
    o_tile = half // 256
    mixed, kept = step(far_blocks, far_bases, 1, state, 1, 2)
    mixed, kept, first_far = sync(mixed, kept, first_far)

    far_share, near_share = output_projection(mixed, 1, (ffn_own, first_far), o_tile)
    beside_sum = add_rows(near_share, 0, flip(far_share, "c"), 0)
    beside_sum, state, mixed, kept = sync(beside_sum, state, mixed, kept)
    beside = flip(beside_sum, "zl")
    mixed, kept = step(far_blocks, far_bases, 1, state, 0, 2, (mixed, kept))
    far_share, near_share = output_projection(mixed, 0, (ffn_own, first_far), o_tile)
    across = flip(far_share, "c")
    beside, near_share, across, mixed, kept = sync(beside, near_share, across, mixed, kept)
    after_attn, norm_own = sync(*forward_norm(inputs, near_share, across, beside, gain_rows))

    norm_beside, norm_across = flip(norm_own, "zl"), flip(norm_own, "c")
    near_w = [(ffn_own, 0), (ffn_own, up_at), (ffn_own, up_at + half)]
    far_w = [(first_far, 0), (second_far, 0), (second_far, half)]
    early = feed_forward([norm_own, norm_across], [out_cotangent, g_across], near_w, far_w)
    norm_beside, norm_across, early = sync(norm_beside, norm_across, early)
    norm_both = flip(norm_beside, "c")
    late = feed_forward([norm_beside, norm_both], [g_beside, g_both], near_w, far_w)
    late, norm_both = sync(late, norm_both)

    across_both = flip(late[3], "c")
    beside_sum = add_rows(late[2], 0, across_both, 0)
    beside_sum, late, early = sync(beside_sum, late, early)
    beside = flip(beside_sum, "zl")
    across = flip(early[3], "c")
    out_across = [flip(late[1], "c"), flip(early[1], "c")]
    ffn_part = weight_grad(
        [
            (early[7], late[7], early[5], late[5]),
            (early[7], late[7], early[6], late[6]),
            (early[8], late[8], early[4], late[4]),
        ],
        12,
    )
    beside, across, out_across, ffn_part, early, late = sync(beside, across, out_across, ffn_part, early, late)
    ffn_sum = over_groups(ffn_part)
    grad_mid, mid_low = backward_norm(1, early[2], across, beside, after_attn, out_cotangent, gain_rows, [F32, BF])
    grad_mid, mid_low, early, late = sync(grad_mid, mid_low, early, late)

    mid_beside, mid_across = flip(mid_low, "zl"), flip(mid_low, "c")
    out_w = (ffn_own, first_far)
    aug = prepare_back([mid_low, mid_across], 0, out_w, o_tile, kept, query)

    def step_back(blocks, bases, swap, d_query, kinds, *choice):
        swaps = [swap] * len(blocks)
        out = attend_back(*aug, low_rows, high_rows, info, bases, zl_info, blocks, swaps, d_query, kinds, *choice)
        return out[0], list(out[1:])

    def other_half(summed):
        return flip(summed[:, summed.shape[1] // 2 :], "zh")

    kinds = [BF] * len(far_blocks)
    d_query, d_first = step_back(far_blocks, far_bases, 1, None, kinds, 0, 2)
    mid_beside, mid_across, aug, d_query, d_first = sync(mid_beside, mid_across, aug, d_query, d_first)
    mid_both = flip(mid_beside, "c")
    aug = prepare_back([mid_beside, mid_both], 1, out_w, o_tile, kept, query, aug)
    d_query, d_far = step_back(far_blocks, far_bases, 1, None, kinds, 1, 2, (d_query,))
    d_far = [(a.astype(F32) + b.astype(F32)).astype(BF) for a, b in zip(d_first, d_far)]
    mid_both, aug, d_query, d_far, early, late = sync(mid_both, aug, d_query, d_far, early, late)

    back = [lax.ppermute(d_far[2 * n + m], "g", reverse(shift_pairs(d))) for n, d in enumerate(shifts) for m in range(2)]
    d_query, d_other = step_back(other, other_bases, 1, d_query, [BF] * 2)
    d_query, d_same = step_back(same, same_bases, 0, d_query, [BF] * len(same))
    out_sum = add_rows(late[0], 0, out_across[0], 0)
    d_query, d_other, d_same, d_far, back, out_sum = sync(d_query, d_other, d_same, d_far, back, out_sum)

    other_sum = [d_other[m].astype(F32) for m in range(2)]
    for n in range(len(shifts)):
        for m in range(2):
            other_sum[m] = other_sum[m] + back[2 * n + m].astype(F32)
    other_sum = [o.astype(BF) for o in other_sum]
    other_back = [flip(other_sum[0], "zh")]
    same_back = [lax.ppermute(d_same[n], "g", reverse(shift_pairs(d))) for n, d in enumerate(shifts)]
    above_back = []
    if above_groups:
        above = lax.dynamic_slice_in_dim(d_far[-1], zl * rows, rows, 0)
        above_back.append(lax.ppermute(above, ("g", "zh"), reverse(above_pairs)))
    out_beside = flip(out_sum, "zl")
    d_query, d_own = step_back([kv], own_bases, 0, d_query, [F32])
    core = jnp.reshape(2 * c + zl, (1,)).astype(jnp.int32)
    d_q, shares = query_back(core, d_query, qkv_w, cos_table, sin_table)
    q_part = head_grad([norm_one[k] for k in range(4)], d_q)

    def group_slice(part, k):
        return lax.dynamic_slice_in_dim(part, (g ^ k) * shard_pair, shard_pair, 0)

    q_slices = [group_slice(q_part, k) for k in range(groups)]
    other_back, same_back, above_back, d_own, shares, q_slices, other_late, early, late, out_beside = sync(
        other_back, same_back, above_back, d_own, shares, q_slices, other_sum[1], early, late, out_beside
    )

    other_back.append(flip(other_late, "zh"))
    o_part = head_grad([mid_low, mid_beside, mid_across, mid_both], mixed)
    second_column = gain_columns([early[2], late[2], early[3], late[3]], [norm_own, norm_beside, norm_across, norm_both], 1)
    ffn_give = [ffn_sum[:, (3 + n) * half : (4 + n) * half] for n in range(3)]
    q_got = [flip(q_slices[k], "g", k) for k in range(1, groups)]
    other_back, same_back, above_back, d_own, shares, q_slices, q_got, o_part, second_column, ffn_sum, ffn_give = sync(
        other_back, same_back, above_back, d_own, shares, q_slices, q_got, o_part, second_column, ffn_sum, ffn_give
    )
    o_sum = over_groups(o_part)

    gate_far = flip(ffn_give[0], "zh")
    d_kvs, shares = kv_back(core, d_own[0], other_back, same_back, above_back, shares, qkv_w, cos_table, sin_table)
    share_rows = shares.reshape(span, width)
    share_far = share_rows[2 * rows :]
    gate_far, d_kvs, shares, share_rows, share_far, up_give = sync(gate_far, d_kvs, shares, share_rows, share_far, ffn_give[1])
    up_far = flip(up_give, "zh")
    across = flip(share_far, "c")
    kv_part = kv_grad(norm_one, shares, d_kvs, second_column)
    kv_slices = [group_slice(kv_part, k) for k in range(groups)]
    beside_sum = add_rows(share_rows, 1, across, 1)
    down_give = jnp.concatenate([ffn_give[2], o_sum[:, 256:]], 1)
    down_give, beside_sum, kv_slices, across, share_rows, up_far, gate_far, ffn_sum = sync(
        down_give, beside_sum, kv_slices, across, share_rows, up_far, gate_far, ffn_sum
    )

    kv_got = [flip(kv_slices[k], "g", k) for k in range(1, groups)]
    q_sum = q_slices[0].astype(F32) + sum(v.astype(F32) for v in q_got)
    beside = flip(beside_sum, "zl")
    down_far = flip(down_give, "zh")
    down_far, kv_got, q_sum, beside, o_sum, ffn_sum, gate_far, up_far = sync(
        down_far, kv_got, q_sum, beside, o_sum, ffn_sum, gate_far, up_far
    )

    kv_sum = kv_slices[0].astype(F32) + sum(v.astype(F32) for v in kv_got)
    kvq_own = jnp.concatenate([kv_sum[:, :256], q_sum[:, :256]], 1)
    kvq_give = jnp.concatenate([kv_sum[:, 256:], q_sum[:, 256:]], 1).astype(BF)
    kvq_own, kvq_give, down_far, beside = sync(kvq_own, kvq_give, down_far, beside)
    kvq_far = flip(kvq_give, "zh")
    [input_grad] = backward_norm(0, share_rows, across, beside, inputs, grad_mid, gain_rows, [BF])
    far_sum = jnp.concatenate([gate_far, up_far, down_far], 1).astype(F32)
    near_sum = jnp.concatenate([ffn_sum[:, : 3 * half], o_sum[:, :256]], 1).astype(F32)
    sum_own, sum_got = to_owner(near_sum + far_sum)
    layer_out = (after_attn + (early[0].astype(F32) + out_across[1].astype(F32) + out_beside.astype(F32))).astype(BF)
    kvq_far, sum_own, sum_got, input_grad, layer_out = sync(kvq_far, sum_own, sum_got, input_grad, layer_out)

    kvq_own, kvq_got = to_owner(kvq_own + kvq_far.astype(F32))
    gain_sums = (kvq_own + kvq_got)[:, 2 * HEAD : 2 * HEAD + 2]
    gain_sums = gain_sums + flip(gain_sums, "zl")

    def columns(own, got, start, size):
        return in_order(own[:, start : start + size], got[:, start : start + size], 1)

    return (
        layer_out,
        input_grad,
        gain_sums[:, 0] / first_gain.astype(F32),
        columns(kvq_own, kvq_got, 256, 2 * HEAD),
        columns(kvq_own, kvq_got, 0, HEAD),
        columns(kvq_own, kvq_got, HEAD, HEAD),
        columns(sum_own, sum_got, 3 * half, 2 * HEAD).T,
        gain_sums[:, 1] / second_gain.astype(F32),
        columns(sum_own, sum_got, 0, half),
        columns(sum_own, sum_got, half, half),
        columns(sum_own, sum_got, 2 * half, half).T,
    )


def solution(mesh):
    outer, inner = mesh.devices.shape
    fine = Mesh(mesh.devices.reshape(outer // 2, 2, inner // 2, 2), AXES)
    data, tensor = ("g", "c"), ("zh", "zl")
    rows, first = P(AXES, None), P(data)
    wide, tall = P(data, tensor), P(tensor, data)
    return jax.shard_map(
        body,
        mesh=fine,
        in_specs=(rows, first, wide, wide, wide, tall, first, wide, wide, tall, P(), P(), rows),
        out_specs=(rows, rows, first, wide, wide, wide, tall, first, wide, wide, tall),
        check_vma=False,
    )
```

```python
import functools
import math

import jax
import jax.numpy as jnp
from jax import lax
from jax.experimental import pallas as pl
from jax.experimental.layout import Layout, with_layout_constraint
from jax.experimental.pallas import tpu as pltpu
from jax.sharding import Mesh, PartitionSpec as P

HEAD = 96
LANES = 128
PIECE = 256
LEN_FIRST = 4096
LEN_LAST = 2048
LEN_MAX = 4096
epsilon = 1e-05
rope_base = 100000.0
negative = -1e30
far_away = 1 << 30
log2_e = 1.4426950408889634
score_scale = 1.0 / math.sqrt(HEAD)
BF = jnp.bfloat16
F32 = jnp.float32
AXES = ("g", "c", "zh", "zl")
MIB = 1024 * 1024
COST_SHARE = 0.01


def params(mib):
    return pltpu.CompilerParams(vmem_limit_bytes=mib * MIB)


def nn(left, right):
    return lax.dot_general(left, right, (((1,), (0,)), ((), ())), preferred_element_type=F32)


def nt(left, right):
    return lax.dot_general(left, right, (((1,), (1,)), ((), ())), preferred_element_type=F32)


def tn(left, right):
    return lax.dot_general(left, right, (((0,), (0,)), ((), ())), preferred_element_type=F32)


def after(value, *earlier):
    return lax.optimization_barrier((value, *earlier))[0]


def sync(*values):
    return lax.optimization_barrier(values)


def all_groups(value):
    return lax.all_gather(value, "g", axis=0, tiled=True)


def flip(value, axis, bit=1):
    count = lax.axis_size(axis)
    return lax.ppermute(value, axis, [(s, s ^ bit) for s in range(count)])


def cost(us):
    us = us * COST_SHARE
    return pl.CostEstimate(flops=int(us * 1.15e9), bytes_accessed=int(us * 3.6e6), transcendentals=0)


def gather_rows(own):
    beside = flip(own, "zl")
    across = flip(own, "c")
    both = flip(beside, "c")
    return [own, beside, across, both]


def from_groups(value):
    return [value] + [flip(value, "g", k) for k in range(1, lax.axis_size("g"))]


def split_core(shard):
    c = lax.axis_index("c")
    keep = lax.dynamic_index_in_dim(shard, c, 0, False)
    got = flip(lax.dynamic_index_in_dim(shard, 1 - c, 0, False), "c")
    return keep, got


def in_order(keep, got, axis=0):
    c = lax.axis_index("c")
    return jnp.where(c == 0, jnp.concatenate([keep, got], axis), jnp.concatenate([got, keep], axis))


def by_rows(value):
    return with_layout_constraint(value, Layout(major_to_minor=(0, 1)))


def over_groups(value):
    return lax.psum_scatter(value, "g", scatter_dimension=0, tiled=True)


def to_owner(mine):
    c = lax.axis_index("c")
    half = mine.shape[0] // 2
    own = lax.dynamic_slice_in_dim(mine, c * half, half, 0).astype(F32)
    got = flip(lax.dynamic_slice_in_dim(mine, (1 - c) * half, half, 0).astype(BF), "c").astype(F32)
    return own, got


def joined(own, got):
    return in_order(own, got, 1)


def swap_halves(value):
    lane = lax.broadcasted_iota(jnp.int32, value.shape, 1)
    return jnp.where(lane < HEAD // 2, pltpu.roll(value, LANES - HEAD // 2, 1), pltpu.roll(value, HEAD // 2, 1))


def turn(value, cosine, sine):
    return value * cosine + swap_halves(value) * sine


def unturn(value, cosine, sine):
    return value * cosine - swap_halves(value) * sine


def widen(value):
    pad = jnp.zeros((value.shape[0], LANES - HEAD), value.dtype)
    return jnp.concatenate([value, pad], 1)


def qkv_kernel(count, n_jumps, where_ref, *refs):
    pieces, refs = refs[: 2 * count], refs[2 * count :]
    jumps, refs = refs[:n_jumps], refs[n_jumps:]
    x0, x1, x_far, cos_ref, sin_ref, norm_ref, query_ref, kv_ref, weight_ref, gains_ref, x_ref = refs
    step = pl.program_id(0)

    @pl.when(step == 0)
    def _():
        half = pieces[0].shape[0] // 2

        def place(block, n, value):
            for part in range(2):
                at = pl.multiple_of(where_ref[2 * n + part], 64)
                weight_ref[block, pl.ds(at, half), :] = value[part * half : (part + 1) * half, :]

        for block in range(2):
            for n in range(count):
                place(block, n, pieces[block * count + n])
            for n in range(n_jumps):
                place(block, count + n, jumps[n][2 * half * block : 2 * half * (block + 1), :])
        row = lax.broadcasted_iota(jnp.int32, (8, LANES), 0)
        lane = lax.broadcasted_iota(jnp.int32, (8, LANES), 1)
        pick = jnp.where(row == lane, 1.0, 0.0).astype(BF)
        gains_ref[...] = nt(pick, weight_ref[0][:, 4 * HEAD :])

    for k in range(4):

        @pl.when(step == k)
        def _():
            x_ref[...] = (x0, x1)[k][...] if k < 2 else x_far[(k - 2) * PIECE : (k - 1) * PIECE, :]

    x = x_ref[...].astype(F32)
    r = lax.rsqrt(jnp.mean(x * x, axis=-1, keepdims=True) + epsilon)
    normed = (x * r * gains_ref[0:1, :]).astype(BF)
    norm_ref[0] = normed
    cosine, sine = cos_ref[0], sin_ref[0]
    packs = []
    for j in range(2):
        pre = nn(normed, weight_ref[j][:, 0 : 4 * HEAD])
        for h in range(2):
            turned = turn(widen(pre[:, h * HEAD : (h + 1) * HEAD]), cosine, sine)
            query_ref[j, 0, h * PIECE : (h + 1) * PIECE] = (turned * (score_scale * log2_e)).astype(BF)
        packs.append(turn(widen(pre[:, 2 * HEAD : 3 * HEAD]), cosine, sine)[:, 0:HEAD])
        packs.append(pre[:, 3 * HEAD :])
    kv_ref[...] = jnp.concatenate(packs, 1).astype(BF)


def project_qkv(where, pieces, jumps, x_rows, x_far, cos_table, sin_table):
    rows, width = x_rows[0].shape
    n_cols = pieces[0].shape[1]
    table = pl.BlockSpec((1, rows, LANES), lambda i, *_: (i, 0, 0))
    return pl.pallas_call(
        functools.partial(qkv_kernel, len(pieces) // 2, len(jumps)),
        grid_spec=pltpu.PrefetchScalarGridSpec(
            num_scalar_prefetch=1,
            grid=(4,),
            in_specs=[pl.BlockSpec(v.shape, lambda i, *_: (0, 0)) for v in (*pieces, *jumps, *x_rows, x_far)] + [table, table],
            out_specs=[
                pl.BlockSpec((1, rows, width), lambda i, *_: (i, 0, 0)),
                pl.BlockSpec((2, 1, 2 * rows, LANES), lambda i, *_: (0, i, 0, 0)),
                pl.BlockSpec((rows, 4 * HEAD), lambda i, *_: (i, 0)),
                pl.BlockSpec((2, width, n_cols), lambda i, *_: (0, 0, 0)),
                pl.BlockSpec((8, width), lambda i, *_: (0, 0)),
            ],
            scratch_shapes=[pltpu.VMEM((rows, width), BF)],
        ),
        out_shape=[
            jax.ShapeDtypeStruct((4, rows, width), BF),
            jax.ShapeDtypeStruct((2, 4, 2 * rows, LANES), BF),
            jax.ShapeDtypeStruct((4 * rows, 4 * HEAD), BF),
            jax.ShapeDtypeStruct((2, width, n_cols), BF),
            jax.ShapeDtypeStruct((8, width), F32),
        ],
        compiler_params=params(58),
        cost_estimate=cost(8),
        name="project_qkv",
    )(where, *pieces, *jumps, *x_rows, x_far, cos_table, sin_table)


def query_back_kernel(core_ref, dq_ref, weight_ref, cos_ref, sin_ref, grad_ref, share_ref):
    total = None
    for j in range(2):
        heads = []
        for h in range(2):
            turned = unturn(dq_ref[j, 0, h * PIECE : (h + 1) * PIECE], cos_ref[0], sin_ref[0])
            heads.append((turned * score_scale)[:, 0:HEAD])
        grad = jnp.concatenate(heads, 1).astype(BF)
        grad_ref[j, 0] = grad
        term = nt(grad, weight_ref[j][:, 0 : 2 * HEAD])
        total = term if total is None else total + term
    share_ref[0] = total.astype(BF)


def kv_back_kernel(n_same, has_above, core_ref, *refs):
    refs = list(refs)
    own_ref, first_ref, second_ref = refs[:3]
    same_refs = refs[3 : 3 + n_same]
    refs = refs[3 + n_same :]
    i = pl.program_id(0)
    late = i >= 2
    d_kv = own_ref[...] + jnp.where(late, second_ref[...], first_ref[...]).astype(F32)
    for ref in same_refs:
        d_kv = d_kv + ref[...].astype(F32)
    if has_above:
        d_kv = d_kv + jnp.where(i == core_ref[0], refs.pop(0)[...], 0).astype(F32)
    share_in_ref, weight_ref, cos_ref, sin_ref, grad_ref, share_ref = refs
    total = share_in_ref[0].astype(F32)
    for j in range(2):
        both = d_kv[:, 2 * HEAD * j : 2 * HEAD * (j + 1)]
        turned = unturn(widen(both[:, 0:HEAD]), cos_ref[0], sin_ref[0]) * (1.0 / log2_e)
        grad = jnp.concatenate([turned[:, 0:HEAD], both[:, HEAD:]], 1).astype(BF)
        grad_ref[j, 0] = grad
        total = total + nt(grad, weight_ref[j][:, 2 * HEAD : 4 * HEAD])
    share_ref[0] = total.astype(BF)


def project_back(kernel, core, args, specs, weights, cos_table, sin_table, name, mib):
    count, rows, _ = cos_table.shape
    width = weights.shape[1]
    piece = pl.BlockSpec((1, rows, width), lambda i, *_: (i, 0, 0))
    table = pl.BlockSpec((1, rows, cos_table.shape[2]), lambda i, *_: (i, 0, 0))
    return pl.pallas_call(
        kernel,
        grid_spec=pltpu.PrefetchScalarGridSpec(
            num_scalar_prefetch=1,
            grid=(count,),
            in_specs=specs + [pl.BlockSpec((2, width, 4 * HEAD), lambda i, *_: (0, 0, 0)), table, table],
            out_specs=[pl.BlockSpec((2, 1, rows, 2 * HEAD), lambda i, *_: (0, i, 0, 0)), piece],
        ),
        out_shape=[
            jax.ShapeDtypeStruct((2, count, rows, 2 * HEAD), BF),
            jax.ShapeDtypeStruct((count, rows, width), BF),
        ],
        compiler_params=params(mib),
        cost_estimate=cost(4),
        name=name,
    )(core, *args, weights, cos_table, sin_table)


def query_back(core, d_query, weights, cos_table, sin_table):
    spec = pl.BlockSpec((2, 1, 2 * PIECE, LANES), lambda i, *_: (0, i, 0, 0))
    return project_back(query_back_kernel, core, [d_query], [spec], weights, cos_table, sin_table, "query_back", 40)


def kv_back(core, own, other, same, above, shares, weights, cos_table, sin_table):
    rows = pl.BlockSpec((PIECE, 4 * HEAD), lambda i, *_: (i, 0))
    chunk = pl.BlockSpec((PIECE, 4 * HEAD), lambda i, *_: (i % 2, 0))
    args = [own, *other, *same, *above, shares]
    specs = [rows, chunk, chunk] + [rows] * len(same)
    specs += [pl.BlockSpec((PIECE, 4 * HEAD), lambda i, *_: (0, 0))] * len(above)
    specs.append(pl.BlockSpec((1, *shares.shape[1:]), lambda i, *_: (i, 0, 0)))
    kernel = functools.partial(kv_back_kernel, len(same), bool(above))
    return project_back(kernel, core, args, specs, weights, cos_table, sin_table, "kv_back", 58)


CHUNK = 2 * PIECE


def unpack_kv(swaps, block_refs, key_scratch, value_scratch):
    lane = lax.broadcasted_iota(jnp.int32, (CHUNK, LANES - HEAD), 1)
    ones = jnp.where(lane < 3, 1.0, 0.0).astype(BF)
    at = 0
    for swap, ref in zip(swaps, block_refs):
        for start in range(0, ref.shape[0], CHUNK):
            block = ref[start : start + CHUNK, :]
            for j in range(2):
                first = 2 * HEAD * (j ^ swap)
                k = block[:, first : first + HEAD]
                v = block[:, first + HEAD : first + 2 * HEAD]
                key_scratch[j, at : at + CHUNK, :] = jnp.concatenate([k, ones], 1)
                value_scratch[j, at : at + CHUNK, :] = jnp.concatenate([v, ones], 1)
            at += CHUNK


def chunk_state(info_ref, base, i):
    last = base + (CHUNK - 1)
    touched = (base <= info_ref[i, 3]) & (last >= info_ref[i, 0])
    full = (base >= info_ref[i, 1]) & (last <= info_ref[i, 2])
    return touched, full


def forward_kernel(swaps, first, last, offset, stride, n_kept, info_ref, base_ref, zl_ref, *refs):
    refs = list(refs)
    n_blocks = len(swaps)
    query_ref, low_ref, high_ref = refs[:3]
    block_refs = refs[3 : 3 + n_blocks]
    refs = refs[3 + n_blocks :]
    if not first:
        acc_in = refs.pop(0)
    refs = refs[n_kept:]
    if last:
        mixed_ref = refs.pop(0)
    kept_ref = refs.pop(0)
    key_scratch, value_scratch, acc, top = refs
    i = offset + stride * pl.program_id(0)

    @pl.when(pl.program_id(0) == 0)
    def _():
        unpack_kv(swaps, block_refs, key_scratch, value_scratch)

    for j in range(2):
        if first:
            acc[j] = jnp.zeros((CHUNK, LANES), F32)
            top[j] = jnp.full((CHUNK, LANES), negative, F32)
        else:
            acc[j] = acc_in[j, 0]
            top[j] = jnp.broadcast_to(acc_in[j, 0][:, HEAD + 1 : HEAD + 2], (CHUNK, LANES))
    n_chunks = sum(r.shape[0] for r in block_refs) // CHUNK

    def visit(n, masked):
        rows = pl.ds(pl.multiple_of(n * CHUNK, CHUNK), CHUNK)
        if masked:
            at = lax.broadcasted_iota(jnp.int32, (PIECE, CHUNK), 1)
            token = base_ref[n] + lax.rem(at + zl_ref[0] * PIECE, CHUNK)
            low = jnp.concatenate([low_ref[0]] * (CHUNK // LANES), 1)
            high = jnp.concatenate([high_ref[0]] * (CHUNK // LANES), 1)
            allowed = (token >= low) & (token <= high)
        for j in range(2):
            scores = nt(query_ref[j, 0], key_scratch[j, rows, :])
            if masked:
                scores = jnp.concatenate(
                    [jnp.where(allowed, scores[h * PIECE : (h + 1) * PIECE], negative) for h in range(2)], 0
                )
            old = top[j]
            new = jnp.maximum(old, jnp.max(scores, axis=1, keepdims=True))
            top[j] = new
            probs = jnp.exp2(scores - jnp.concatenate([new] * (CHUNK // LANES), 1)).astype(BF)
            acc[j] = acc[j] * jnp.exp2(old - new) + nn(probs, value_scratch[j, rows, :])

    @pl.loop(0, n_chunks)
    def _(n):
        touched, full = chunk_state(info_ref, base_ref[n], i)

        @pl.when(touched & full)
        def _():
            visit(n, False)

        @pl.when(touched & jnp.logical_not(full))
        def _():
            visit(n, True)

    lane = lax.broadcasted_iota(jnp.int32, (CHUNK, LANES), 1)
    if last:
        for j in range(2):
            total = acc[j][:, HEAD : HEAD + 1]
            out = acc[j] / total
            kept_ref[j, 0] = jnp.where(lane < HEAD, out, top[j] + jnp.log2(total))
            mixed_ref[j, 0] = jnp.concatenate([out[0:PIECE, 0:HEAD], out[PIECE:, 0:HEAD]], 1).astype(BF)
    else:
        for j in range(2):
            kept_ref[j, 0] = jnp.where(lane == HEAD + 1, top[j], acc[j])


def attend(query, low, high, info, bases, zl, blocks, swaps, state, last, offset=0, stride=1, kept=()):
    count = query.shape[1]
    n_keys = sum(b.shape[0] for b in blocks)
    per_piece = pl.BlockSpec((2, 1, CHUNK, LANES), lambda i, *_: (0, offset + stride * i, 0, 0))
    bound = pl.BlockSpec((1, PIECE, LANES), lambda i, *_: (offset + stride * i, 0, 0))
    in_specs = [per_piece, bound, bound]
    in_specs += [pl.BlockSpec(b.shape, lambda i, *_: (0, 0)) for b in blocks]
    args = [query, low, high, *blocks]
    if state is not None:
        in_specs.append(per_piece)
        args.append(state)
    aliases = {3 + len(args) + n: n for n in range(len(kept))}
    in_specs += [pl.BlockSpec(memory_space=pl.ANY)] * len(kept)
    args += list(kept)
    wide = jax.ShapeDtypeStruct((2, count, CHUNK, LANES), F32)
    if last:
        out_shape = [jax.ShapeDtypeStruct((2, count, PIECE, 2 * HEAD), BF), wide]
        out_specs = [pl.BlockSpec((2, 1, PIECE, 2 * HEAD), lambda i, *_: (0, offset + stride * i, 0, 0)), per_piece]
    else:
        out_shape = wide
        out_specs = per_piece
    return pl.pallas_call(
        functools.partial(forward_kernel, swaps, state is None, last, offset, stride, len(kept)),
        grid_spec=pltpu.PrefetchScalarGridSpec(
            num_scalar_prefetch=3,
            grid=(count // stride,),
            in_specs=in_specs,
            out_specs=out_specs,
            scratch_shapes=[
                pltpu.VMEM((2, n_keys, LANES), BF),
                pltpu.VMEM((2, n_keys, LANES), BF),
                pltpu.VMEM((2, CHUNK, LANES), F32),
                pltpu.VMEM((2, CHUNK, LANES), F32),
            ],
        ),
        out_shape=out_shape,
        input_output_aliases=aliases,
        compiler_params=params(48),
        cost_estimate=cost(n_keys / 100),
        name="attend",
    )(info, bases, zl, *args)


def split_three(value):
    first = value.astype(BF)
    rest = value - first.astype(F32)
    second = rest.astype(BF)
    third = (rest - second.astype(F32)).astype(BF)
    return first, second, third


def augment(wide, extra):
    lane = lax.broadcasted_iota(jnp.int32, wide.shape, 1)
    a, b, c = (part.astype(F32) for part in split_three(extra))
    out = wide.astype(F32)
    out = jnp.where(lane == HEAD, a, out)
    out = jnp.where(lane == HEAD + 1, b, out)
    out = jnp.where(lane == HEAD + 2, c, out)
    return out.astype(BF)


def prepare_kernel(n_kept, m0, m1, w0, w1, kept_ref, query_ref, *refs):
    q_aug_ref, o_aug_ref, mid_ref = refs[n_kept:]
    step = pl.program_id(0)
    for k, ref in enumerate((m0, m1)):

        @pl.when(step == k)
        def _():
            mid_ref[...] = ref[...]

    mid = mid_ref[...]
    for j, weight_ref in enumerate((w0, w1)):
        grad = nn(mid, weight_ref[...][:, 0 : 2 * HEAD])
        wide = jnp.concatenate([widen(grad[:, 0:HEAD]), widen(grad[:, HEAD : 2 * HEAD])], 0).astype(BF)
        kept = kept_ref[j, 0]
        delta = jnp.sum(wide.astype(F32) * kept, axis=1, keepdims=True)
        q_aug_ref[j, 0] = augment(query_ref[j, 0], -kept[:, HEAD : HEAD + 1])
        o_aug_ref[j, 0] = augment(wide, -delta)


def prepare_back(mid, offset, weights, tile, kept, query, done=()):
    rows, width = mid[0].shape
    per_piece = pl.BlockSpec((2, 1, CHUNK, LANES), lambda i: (0, offset + 2 * i, 0, 0))
    return pl.pallas_call(
        functools.partial(prepare_kernel, len(done)),
        grid=(2,),
        in_specs=[pl.BlockSpec((rows, width), lambda i: (0, 0))] * 2
        + [pl.BlockSpec((width, 256), lambda i: (0, tile))] * 2
        + [per_piece, per_piece]
        + [pl.BlockSpec(memory_space=pl.ANY)] * len(done),
        out_specs=[per_piece, per_piece],
        out_shape=[jax.ShapeDtypeStruct(query.shape, BF)] * 2,
        scratch_shapes=[pltpu.VMEM((rows, width), BF)],
        input_output_aliases={6 + n: n for n in range(len(done))},
        compiler_params=params(58),
        cost_estimate=cost(6),
        name="prepare_back",
    )(*mid, *weights, kept, query, *done)


def backward_kernel(swaps, has_dq, offset, stride, n_kept, n_more, info_ref, base_ref, zl_ref, *refs):
    refs = list(refs)
    n_blocks = len(swaps)
    q_aug, o_aug, low_ref, high_ref = refs[:4]
    block_refs = refs[4 : 4 + n_blocks]
    refs = refs[4 + n_blocks :]
    if has_dq:
        dq_in = refs.pop(0)
    more_refs, refs = refs[:n_more], refs[n_more + n_kept :]
    dq_ref = refs.pop(0)
    out_refs = refs[:n_blocks]
    key_scratch, value_scratch, d_key, d_value = refs[n_blocks:]
    i = offset + stride * pl.program_id(0)

    @pl.when(pl.program_id(0) == 0)
    def _():
        unpack_kv(swaps, block_refs, key_scratch, value_scratch)
        d_key[...] = jnp.zeros(d_key.shape, F32)
        d_value[...] = jnp.zeros(d_value.shape, F32)

    for j in range(2):
        if has_dq:
            dq_ref[j, 0] = dq_in[j, 0]
        else:
            dq_ref[j, 0] = jnp.zeros((CHUNK, LANES), F32)
    n_chunks = sum(r.shape[0] for r in block_refs) // CHUNK

    def visit(n, masked):
        rows = pl.ds(pl.multiple_of(n * CHUNK, CHUNK), CHUNK)
        if masked:
            at = lax.broadcasted_iota(jnp.int32, (CHUNK, CHUNK), 0)
            token = base_ref[n] + lax.rem(at + zl_ref[0] * PIECE, CHUNK)
            allowed = (token >= low_ref[0, 0:1, :]) & (token <= high_ref[0, 0:1, :])
        for j in range(2):
            keys = key_scratch[j, rows, :]
            probs = jnp.exp2(nt(keys, q_aug[j, 0]))
            if masked:
                probs = jnp.where(allowed, probs, 0.0)
            d_probs = nt(value_scratch[j, rows, :], o_aug[j, 0])
            low_probs = probs.astype(BF)
            d_scores = (probs * d_probs).astype(BF)
            d_value[j, rows, :] += nn(low_probs, o_aug[j, 0])
            d_key[j, rows, :] += nn(d_scores, q_aug[j, 0])
            dq_ref[j, 0] += tn(d_scores, keys)

    @pl.loop(0, n_chunks)
    def _(n):
        touched, full = chunk_state(info_ref, base_ref[n], i)

        @pl.when(touched & full)
        def _():
            visit(n, False)

        @pl.when(touched & jnp.logical_not(full))
        def _():
            visit(n, True)

    @pl.when(pl.program_id(0) == pl.num_programs(0) - 1)
    def _():
        at = 0
        for n, (swap, ref) in enumerate(zip(swaps, out_refs)):
            for start in range(0, ref.shape[0], CHUNK):
                parts = []
                for j in (swap, 1 - swap):
                    parts.append(d_key[j, at : at + CHUNK, :][:, 0:HEAD])
                    parts.append(d_value[j, at : at + CHUNK, :][:, 0:HEAD])
                whole = jnp.concatenate(parts, 1)
                if n_more:
                    whole = whole + more_refs[n][start : start + CHUNK, :].astype(F32)
                ref[start : start + CHUNK, :] = whole.astype(ref.dtype)
                at += CHUNK


def attend_back(q_aug, o_aug, low, high, info, bases, zl, blocks, swaps, d_query, kinds, offset=0, stride=1, kept=(), more=()):
    count = q_aug.shape[1]
    n_keys = sum(b.shape[0] for b in blocks)
    per_piece = pl.BlockSpec((2, 1, CHUNK, LANES), lambda i, *_: (0, offset + stride * i, 0, 0))
    bound = pl.BlockSpec((1, 8, CHUNK), lambda i, *_: (offset + stride * i, 0, 0))
    whole = [pl.BlockSpec(b.shape, lambda i, *_: (0, 0)) for b in blocks]
    in_specs = [per_piece, per_piece, bound, bound, *whole]
    args = [q_aug, o_aug, low, high, *blocks]
    if d_query is not None:
        in_specs.append(per_piece)
        args.append(d_query)
    in_specs += [pl.BlockSpec(m.shape, lambda i, *_: (0, 0)) for m in more]
    args += list(more)
    aliases = {3 + len(args) + n: n for n in range(len(kept))}
    in_specs += [pl.BlockSpec(memory_space=pl.ANY)] * len(kept)
    args += list(kept)
    return pl.pallas_call(
        functools.partial(backward_kernel, swaps, d_query is not None, offset, stride, len(kept), len(more)),
        grid_spec=pltpu.PrefetchScalarGridSpec(
            num_scalar_prefetch=3,
            grid=(count // stride,),
            in_specs=in_specs,
            out_specs=[per_piece, *whole],
            scratch_shapes=[
                pltpu.VMEM((2, n_keys, LANES), BF),
                pltpu.VMEM((2, n_keys, LANES), BF),
                pltpu.VMEM((2, n_keys, LANES), F32),
                pltpu.VMEM((2, n_keys, LANES), F32),
            ],
        ),
        out_shape=[jax.ShapeDtypeStruct((2, count, CHUNK, LANES), F32)]
        + [jax.ShapeDtypeStruct(b.shape, k) for b, k in zip(blocks, kinds)],
        input_output_aliases=aliases,
        compiler_params=params(56),
        cost_estimate=cost(n_keys / 64),
        name="attend_back",
    )(info, bases, zl, *args)


def ffn_kernel(tiles, n0, n1, g0, g1, *refs):
    own_refs, other_refs, refs = refs[0:3], refs[3:6], refs[6:]
    o0, o1, b0, b1, hidden_ref, dg_ref, du_ref, norm_t, grad_t, norm_ref, grad_ref, acc_out, acc_back = refs
    step = pl.program_id(0)

    @pl.when(step == 0)
    def _():
        norm_ref[0:PIECE] = n0[...]
        norm_ref[PIECE:] = n1[...]
        grad_ref[0:PIECE] = g0[...]
        grad_ref[PIECE:] = g1[...]

    def run(gate_ref, up_ref, down_ref, first):
        gate_w, up_w, down_w = gate_ref[...], up_ref[...], down_ref[...]
        gate = nn(norm_ref[...], gate_w)
        up = nn(norm_ref[...], up_w)
        d_hidden = nn(grad_ref[...], down_w)
        sig = 0.5 * jnp.tanh(0.5 * gate) + 0.5
        silu = gate * sig
        hidden = (silu * up).astype(BF)
        d_gate = (d_hidden * up * (sig + silu * (1.0 - sig))).astype(BF)
        d_up = (d_hidden * silu).astype(BF)
        hidden_ref[...] = hidden
        dg_ref[...] = d_gate
        du_ref[...] = d_up
        norm_t[...] = norm_ref[pl.ds(pl.multiple_of(step * LANES, LANES), LANES), :].T
        grad_t[...] = grad_ref[pl.ds(pl.multiple_of(step * LANES, LANES), LANES), :].T
        out = nt(hidden, down_w)
        back = nt(d_gate, gate_w) + nt(d_up, up_w)
        if first:
            acc_out[...] = out
            acc_back[...] = back
        else:
            acc_out[...] += out
            acc_back[...] += back

    @pl.when(step == 0)
    def _():
        run(*own_refs, True)

    @pl.when((step > 0) & (step < tiles))
    def _():
        run(*own_refs, False)

    @pl.when(step >= tiles)
    def _():
        run(*other_refs, False)

    @pl.when(step == pl.num_programs(0) - 1)
    def _():
        o0[...] = acc_out[0:PIECE].astype(BF)
        o1[...] = acc_out[PIECE:].astype(BF)
        b0[...] = acc_back[0:PIECE].astype(BF)
        b1[...] = acc_back[PIECE:].astype(BF)


def feed_forward(norm_rows, grad_rows, own, other):
    rows, width = norm_rows[0].shape
    half = 512
    tile = 256
    tiles = half // tile
    whole = pl.BlockSpec((rows, width), lambda s: (0, 0))

    def own_spec(at):
        return pl.BlockSpec((width, tile), lambda s: (0, at // tile + jnp.minimum(s, tiles - 1)))

    def other_spec(at):
        return pl.BlockSpec((width, tile), lambda s: (0, at // tile + jnp.maximum(s - tiles, 0)))

    hid = pl.BlockSpec((2 * rows, tile), lambda s: (0, s))
    turned = pl.BlockSpec((width, LANES), lambda s: (0, s))
    return pl.pallas_call(
        functools.partial(ffn_kernel, tiles),
        grid=(2 * tiles,),
        in_specs=[whole] * 4 + [own_spec(at) for _, at in own] + [other_spec(at) for _, at in other],
        out_specs=[whole] * 4 + [hid] * 3 + [turned] * 2,
        out_shape=[jax.ShapeDtypeStruct((rows, width), BF)] * 4
        + [jax.ShapeDtypeStruct((2 * rows, 2 * half), BF)] * 3
        + [jax.ShapeDtypeStruct((width, 2 * rows), BF)] * 2,
        scratch_shapes=[pltpu.VMEM((2 * rows, width), BF)] * 2 + [pltpu.VMEM((2 * rows, width), F32)] * 2,
        compiler_params=params(56),
        cost_estimate=cost(18),
        name="feed_forward",
    )(*norm_rows, *grad_rows, *(w for w, _ in own), *(w for w, _ in other))


def weight_grad_kernel(n_jobs, *refs):
    out_ref = refs[-1]
    for n in range(n_jobs):
        left_early, left_late, early, late = refs[4 * n : 4 * n + 4]

        @pl.when(pl.program_id(1) == n)
        def _():
            total = nn(left_early[...], early[...]) + nn(left_late[...], late[...])
            out_ref[...] = total.astype(BF)


def weight_grad(jobs, us):
    width, depth = jobs[0][0].shape
    half = jobs[0][2].shape[1] // 2
    count = len(jobs)
    left = pl.BlockSpec((width, depth), lambda s, n: (0, 0))
    cols = pl.BlockSpec((depth, half), lambda s, n: (0, s))
    return pl.pallas_call(
        functools.partial(weight_grad_kernel, count),
        grid=(2, count),
        in_specs=[left, left, cols, cols] * count,
        out_specs=pl.BlockSpec((width, half), lambda s, n: (0, s * count + n)),
        out_shape=jax.ShapeDtypeStruct((width, 2 * count * half), BF),
        compiler_params=params(48),
        cost_estimate=cost(us),
        name="weight_grad",
    )(*(value for job in jobs for value in job))


def head_grad_kernel(l0, l1, l2, l3, right_ref, out_ref):
    for j in range(2):
        total = None
        for k, left in enumerate((l0, l1, l2, l3)):
            term = tn(left[...], right_ref[j, k])
            total = term if total is None else total + term
        wide = jnp.concatenate([total, jnp.zeros((total.shape[0], 256 - 2 * HEAD), F32)], 1)
        out_ref[:, j * 256 : (j + 1) * 256] = wide.astype(BF)


def head_grad(left, right):
    rows, width = left[0].shape
    tile = 512
    return pl.pallas_call(
        head_grad_kernel,
        grid=(width // tile,),
        in_specs=[pl.BlockSpec((rows, tile), lambda s: (0, s))] * 4 + [pl.BlockSpec(right.shape, lambda s: (0, 0, 0, 0))],
        out_specs=pl.BlockSpec((tile, 512), lambda s: (s, 0)),
        out_shape=jax.ShapeDtypeStruct((width, 512), BF),
        compiler_params=params(40),
        cost_estimate=cost(3),
        name="head_grad",
    )(*left, right)


def gain_kernel(lane, *refs):
    out_ref = refs[-1]
    count = (len(refs) - 1) // 2
    at = lax.broadcasted_iota(jnp.int32, (PIECE, LANES), 1)
    pick = jnp.where(at == lane, 1.0, 0.0).astype(BF)
    total = None
    for share, normed in zip(refs[:count], refs[count : 2 * count]):
        product = (share[...].astype(F32) * normed[...].astype(F32)).astype(BF)
        term = tn(product, pick)
        total = term if total is None else total + term
    out_ref[...] = total


def gain_columns(shares, normed, lane):
    rows, width = shares[0].shape
    tile = 512
    spec = pl.BlockSpec((rows, tile), lambda s: (0, s))
    return pl.pallas_call(
        functools.partial(gain_kernel, lane),
        grid=(width // tile,),
        in_specs=[spec] * 8,
        out_specs=pl.BlockSpec((tile, LANES), lambda s: (s, 0)),
        out_shape=jax.ShapeDtypeStruct((width, LANES), F32),
        compiler_params=params(40),
        cost_estimate=cost(3),
        name="gain_columns",
    )(*shares, *normed)


def kv_grad_kernel(norm_ref, share_ref, dkv_ref, column_ref, *refs):
    out_ref = refs[-1]
    at = lax.broadcasted_iota(jnp.int32, (PIECE, LANES), 1)
    pick = jnp.where(at == 0, 1.0, 0.0).astype(BF)
    columns = column_ref[...]
    totals = [None, None]
    for k in range(4):
        normed = norm_ref[k]
        product = (share_ref[k].astype(F32) * normed.astype(F32)).astype(BF)
        columns = columns + tn(product, pick)
        for j in range(2):
            term = tn(normed, dkv_ref[j, k])
            totals[j] = term if totals[j] is None else totals[j] + term
    for j in range(2):
        out_ref[:, j * 256 : (j + 1) * 256] = jnp.concatenate([totals[j], columns[:, 0 : 256 - 2 * HEAD]], 1).astype(BF)


def kv_grad(normed, shares, d_kvs, columns):
    count, rows, width = normed.shape
    tile = 512
    spec = pl.BlockSpec((count, rows, tile), lambda s: (0, 0, s))
    return pl.pallas_call(
        kv_grad_kernel,
        grid=(width // tile,),
        in_specs=[
            spec,
            spec,
            pl.BlockSpec(d_kvs.shape, lambda s: (0, 0, 0, 0)),
            pl.BlockSpec((tile, LANES), lambda s: (s, 0)),
        ],
        out_specs=pl.BlockSpec((tile, 512), lambda s: (s, 0)),
        out_shape=jax.ShapeDtypeStruct((width, 512), BF),
        compiler_params=params(40),
        cost_estimate=cost(4),
        name="kv_grad",
    )(normed, shares, d_kvs, columns)


def output_kernel(mixed_ref, w0, w1, far_ref, near_ref):
    step = pl.program_id(0)
    total = None
    for j, weight in enumerate((w0, w1)):
        term = nt(mixed_ref[j, 0], weight[...][:, 0 : 2 * HEAD])
        total = term if total is None else total + term

    @pl.when(step == 0)
    def _():
        far_ref[...] = total.astype(BF)

    @pl.when(step == 1)
    def _():
        near_ref[...] = total


def output_projection(mixed, offset, weights, tile):
    _, count, rows, width_heads = mixed.shape
    width = weights[0].shape[0]
    whole = pl.BlockSpec((rows, width), lambda s: (0, 0))
    return pl.pallas_call(
        output_kernel,
        grid=(2,),
        in_specs=[pl.BlockSpec((2, 1, rows, width_heads), lambda s: (0, offset + 2 * (1 - s), 0, 0))]
        + [pl.BlockSpec((width, 256), lambda s: (0, tile))] * 2,
        out_specs=[whole, whole],
        out_shape=[jax.ShapeDtypeStruct((rows, width), BF), jax.ShapeDtypeStruct((rows, width), F32)],
        compiler_params=params(58),
        cost_estimate=cost(4),
        name="output_projection",
    )(mixed, *weights)


def add_kernel(near_ref, across_ref, out_ref):
    out_ref[...] = (near_ref[...].astype(F32) + across_ref[...].astype(F32)).astype(BF)


def add_rows(near, near_at, across, across_at):
    rows, width = PIECE, near.shape[1]
    return pl.pallas_call(
        add_kernel,
        grid=(1,),
        in_specs=[
            pl.BlockSpec((rows, width), lambda s: (near_at, 0)),
            pl.BlockSpec((rows, width), lambda s: (across_at, 0)),
        ],
        out_specs=pl.BlockSpec((rows, width), lambda s: (0, 0)),
        out_shape=jax.ShapeDtypeStruct((rows, width), BF),
        compiler_params=params(32),
        cost_estimate=cost(1),
        name="add_rows",
    )(near, across)


def forward_norm_kernel(x_ref, near_ref, across_ref, beside_ref, gain_ref, after_ref, norm_ref):
    rows = x_ref[...].astype(F32) + (near_ref[...] + across_ref[...].astype(F32) + beside_ref[...].astype(F32))
    after_ref[...] = rows
    r = lax.rsqrt(jnp.mean(rows * rows, axis=-1, keepdims=True) + epsilon)
    norm_ref[...] = (rows * r * gain_ref[1:2, :]).astype(BF)


def row_specs(width, n):
    return [pl.BlockSpec((LANES, width), lambda i: (i, 0))] * n


def forward_norm(x, near, across, beside, gain_rows):
    rows, width = x.shape
    return pl.pallas_call(
        forward_norm_kernel,
        grid=(rows // LANES,),
        in_specs=row_specs(width, 4) + [pl.BlockSpec((8, width), lambda i: (0, 0))],
        out_specs=row_specs(width, 2),
        out_shape=[jax.ShapeDtypeStruct((rows, width), F32), jax.ShapeDtypeStruct((rows, width), BF)],
        compiler_params=params(32),
        cost_estimate=cost(2),
        name="forward_norm",
    )(x, near, across, beside, gain_rows)


def backward_norm_kernel(which, share_ref, across_ref, beside_ref, rows_ref, base_ref, gain_ref, *out_refs):
    upstream = share_ref[...].astype(F32) + across_ref[...].astype(F32) + beside_ref[...].astype(F32)
    rows = rows_ref[...].astype(F32)
    r = lax.rsqrt(jnp.mean(rows * rows, axis=-1, keepdims=True) + epsilon)
    weighted = upstream * gain_ref[which : which + 1, :]
    inner = jnp.mean(weighted * rows, axis=-1, keepdims=True)
    out = base_ref[...].astype(F32) + (r * weighted - rows * (r * r * r) * inner)
    for ref in out_refs:
        ref[...] = out.astype(ref.dtype)


def backward_norm(which, share, across, beside, rows, base, gain_rows, kinds):
    count, width = rows.shape
    return pl.pallas_call(
        functools.partial(backward_norm_kernel, which),
        grid=(count // LANES,),
        in_specs=row_specs(width, 5) + [pl.BlockSpec((8, width), lambda i: (0, 0))],
        out_specs=row_specs(width, len(kinds)),
        out_shape=[jax.ShapeDtypeStruct((count, width), kind) for kind in kinds],
        compiler_params=params(32),
        cost_estimate=cost(2),
        name="backward_norm",
    )(share, across, beside, rows, base, gain_rows)


def token_tables(token, seq_lengths, piece_starts):
    n = seq_lengths.shape[0]
    upto = jnp.arange(n)[None, :] <= jnp.arange(n)[:, None]
    ends = jnp.sum(jnp.where(upto, seq_lengths[None, :], 0), axis=1)
    after = token[:, None] >= ends[None, :]
    start = jnp.sum(jnp.where(after, seq_lengths[None, :], 0), axis=1)
    end = jnp.min(jnp.where(after, far_away, ends[None, :]), axis=1)
    inside = (token[:, None] >= piece_starts[None, :]) & (token[:, None] < piece_starts[None, :] + PIECE)
    piece_end = jnp.max(jnp.where(inside, piece_starts[None, :] + PIECE, 0), axis=1)
    high = jnp.maximum(token, jnp.minimum(piece_end, end) - 1)
    return start, high


def may_meet(one, two, group_tokens, count):
    total = group_tokens * count
    regions = ((0, LEN_FIRST, LEN_FIRST), (LEN_FIRST, total - LEN_LAST, LEN_MAX), (total - LEN_LAST, total, LEN_LAST))
    for start, end, longest in regions:
        both = all(g * group_tokens < end and (g + 1) * group_tokens > start for g in (one, two))
        if both and (abs(one - two) - 1) * group_tokens + 1 < longest:
            return True
    return False


def body(
    inputs,
    first_gain,
    query_weight,
    key_matrix,
    value_matrix,
    output_weight,
    second_gain,
    gate_weight,
    up_weight,
    down_weight,
    seq_lengths,
    piece_starts,
    out_cotangent,
):
    g, c, zh, zl = (lax.axis_index(a) for a in AXES)
    groups = lax.axis_size("g")
    rows, width = inputs.shape
    span = 4 * rows
    group_tokens = 2 * span
    shard_rows = query_weight.shape[0]

    order = jnp.arange(4)
    piece_base = (2 * g + (c ^ (order >> 1))) * span + zh * CHUNK + (zl ^ (order & 1)) * rows
    token = (piece_base[:, None] + jnp.arange(rows)[None, :]).reshape(-1).astype(jnp.int32)
    low, high = token_tables(token, seq_lengths, piece_starts)
    position = (token - low).astype(F32)
    low, high = low.reshape(4, rows), high.reshape(4, rows)
    info = jnp.stack([low.min(1), low.max(1), high.min(1), high.max(1)], 1).astype(jnp.int32)
    low_wide = jnp.broadcast_to(low[:, :, None], (4, rows, LANES)).astype(jnp.int32)
    high_wide = jnp.broadcast_to(high[:, :, None], (4, rows, LANES)).astype(jnp.int32)
    low_rows = jnp.broadcast_to(jnp.tile(low, (1, 2))[:, None, :], (4, 8, CHUNK)).astype(jnp.int32)
    high_rows = jnp.broadcast_to(jnp.tile(high, (1, 2))[:, None, :], (4, 8, CHUNK)).astype(jnp.int32)
    zl_info = jnp.reshape(zl, (1,)).astype(jnp.int32)
    frequency = rope_base ** (-(2.0 / HEAD) * jnp.arange(HEAD // 2, dtype=F32))
    angles = position[:, None] * frequency[None, :]
    cosine, sine = jnp.cos(angles), jnp.sin(angles)
    pad = jnp.zeros((span, LANES - HEAD), F32)
    cos_table = jnp.concatenate([cosine, cosine, pad], 1).reshape(4, rows, LANES)
    sin_table = jnp.concatenate([-sine, sine, pad], 1).reshape(4, rows, LANES)

    def halves(matrix):
        return matrix.reshape(matrix.shape[0], 2, -1).transpose(1, 0, 2)

    blank = functools.partial(jnp.zeros, dtype=BF)
    half = gate_weight.shape[1] // 2
    zl_info = jnp.reshape(zl, (1,)).astype(jnp.int32)
    core = jnp.reshape(2 * c + zl, (1,)).astype(jnp.int32)
    shard_pair = 2 * shard_rows

    gains = jnp.broadcast_to(jnp.stack([first_gain, second_gain], 1)[None], (2, shard_rows, 2))
    qkv_shard = jnp.concatenate(
        [halves(query_weight), halves(key_matrix), halves(value_matrix), gains, blank((2, shard_rows, 126))], 2
    )
    qkv_keep, qkv_got = split_core(qkv_shard)
    ffn_shard = jnp.concatenate(
        [halves(gate_weight), halves(output_weight.T), blank((2, shard_rows, 64)), halves(up_weight), halves(down_weight.T)],
        2,
    )
    ffn_keep, ffn_got = split_core(ffn_shard)
    qkv_pair = jnp.concatenate([qkv_keep, qkv_got], 0)
    inputs, out_cotangent, qkv_pair, ffn_keep, ffn_got = sync(inputs, out_cotangent, qkv_pair, ffn_keep, ffn_got)

    qkv_other = flip(qkv_pair, "zh")
    hops = [k for k in range(1, groups) if k & -k == k]
    jumps = [k for k in range(1, groups) if k & -k != k]
    qkv_near = [flip(qkv_pair, "g", k) for k in (*hops, *jumps)]
    x_beside = flip(inputs, "zl")
    ffn_pair = in_order(ffn_keep, ffn_got)
    up_at = half + 2 * HEAD + 64
    first_pair = ffn_pair[:, :up_at]
    up_pair, down_pair = ffn_pair[:, up_at : up_at + half], ffn_pair[:, up_at + half :]
    (
        qkv_other, qkv_near, x_beside, ffn_pair, first_pair, up_pair, down_pair, cos_table, sin_table,
        info, low_wide, high_wide, low_rows, high_rows,
    ) = sync(
        qkv_other, qkv_near, x_beside, ffn_pair, first_pair, up_pair, down_pair, cos_table, sin_table,
        info, low_wide, high_wide, low_rows, high_rows,
    )
    x_near = jnp.concatenate([inputs, x_beside], 0)

    ffn_own = all_groups(ffn_pair)
    qkv_far = [flip(qkv_other, "g", k) for k in (*hops, *jumps)]
    x_far = flip(x_near, "c")
    first_other = flip(first_pair, "zh")
    qkv_far, x_far, first_other, up_pair, out_cotangent = sync(qkv_far, x_far, first_other, up_pair, out_cotangent)

    up_other = flip(up_pair, "zh")
    k_order = jnp.array([0, *hops, *jumps])[:, None]
    piece_rows = (g ^ k_order) * shard_pair + (c ^ jnp.arange(2)[None, :]) * shard_rows
    norm_one, query, kv, qkv_w, gain_rows = project_qkv(
        piece_rows.reshape(-1).astype(jnp.int32),
        [qkv_pair, *qkv_near, qkv_other, *qkv_far],
        [],
        [inputs, x_beside],
        x_far,
        cos_table,
        sin_table,
    )
    first_piece = lax.dynamic_slice_in_dim(kv, (2 * c + zl) * rows, rows, 0)
    norm_one, query, kv, qkv_w, gain_rows, kv_chunks, first_piece, out_cotangent, up_other, down_pair, first_other = sync(
        norm_one,
        query,
        kv,
        qkv_w,
        gain_rows,
        [kv[n * CHUNK : (n + 1) * CHUNK] for n in range(2)],
        first_piece,
        out_cotangent,
        up_other,
        down_pair,
        first_other,
    )
    first_far = all_groups(first_other)

    def chunk_bases(group, side):
        return jnp.stack([(2 * group + (c ^ i)) * span + side * CHUNK for i in range(2)]).astype(jnp.int32)

    def shift_pairs(steps):
        return [(s, s + steps) for s in range(groups) if 0 <= s + steps < groups and may_meet(s, s + steps, group_tokens, groups)]

    def present(pairs, bases):
        target = functools.reduce(jnp.logical_or, [g == t for _, t in pairs])
        return jnp.where(target, bases, far_away).astype(jnp.int32)

    def reverse(pairs):
        return [(t, s) for s, t in pairs]

    shifts = [d for d in range(1, groups) if shift_pairs(d)]
    above_groups = [s for s in range(1, groups) if may_meet(s - 1, s, group_tokens, groups)]
    above_pairs = [(2 * s, 2 * (s - 1) + 1) for s in above_groups]
    own_bases, other_bases = chunk_bases(g, zh), chunk_bases(g, 1 - zh)
    same_bases = [present(shift_pairs(d), chunk_bases(g - d, zh)) for d in shifts]
    far_bases = [present(shift_pairs(d), chunk_bases(g - d, 1 - zh)) for d in shifts]
    if above_groups:
        is_target = functools.reduce(jnp.logical_or, [(g == s - 1) & (zh == 1) for s in above_groups])
        far_bases.append(jnp.where(is_target, jnp.reshape(2 * (g + 1) * span, (1,)), far_away).astype(jnp.int32))
    same_bases, far_bases = jnp.concatenate(same_bases), jnp.concatenate(far_bases)

    def step(blocks, bases, swap, state, *choice):
        swaps = [swap] * len(blocks)
        return attend(query, low_wide, high_wide, info, bases, zl_info, blocks, swaps, state, bool(choice), *choice)

    other = [flip(kv_chunks[0], "zh")]
    same = [lax.ppermute(kv, "g", shift_pairs(d)) for d in shifts]
    g_beside, g_across = flip(out_cotangent, "zl"), flip(out_cotangent, "c")
    state = step([kv], own_bases, 0, None)
    other, same, g_beside, g_across, state, kv_late = sync(other, same, g_beside, g_across, state, kv_chunks[1])

    other.append(flip(kv_late, "zh"))
    far_blocks = [[lax.ppermute(other[0], "g", shift_pairs(d))] for d in shifts]
    state = step(same, same_bases, 0, state)
    g_both = flip(g_beside, "c")
    other, far_blocks, g_both, state, down_pair, first_piece, ffn_own = sync(
        other, far_blocks, g_both, state, down_pair, first_piece, ffn_own
    )

    for n, d in enumerate(shifts):
        far_blocks[n].append(lax.ppermute(other[1], "g", shift_pairs(d)))
    far_blocks = [b for pair in far_blocks for b in pair]
    if above_groups:
        above = lax.ppermute(first_piece, ("g", "zh"), above_pairs)
        far_blocks.append(lax.dynamic_update_slice(jnp.zeros((CHUNK, 4 * HEAD), BF), above, (zl * rows, 0)))
    down_other = flip(down_pair, "zh")
    state = step(other, other_bases, 1, state)
    far_blocks, down_other, state = sync(far_blocks, down_other, state)

    second_far = all_groups(jnp.concatenate([up_other, down_other], 1))
    o_tile = half // 256
    mixed, kept = step(far_blocks, far_bases, 1, state, 1, 2)
    mixed, kept, first_far = sync(mixed, kept, first_far)

    far_share, near_share = output_projection(mixed, 1, (ffn_own, first_far), o_tile)
    beside_sum = add_rows(near_share, 0, flip(far_share, "c"), 0)
    beside_sum, state, mixed, kept = sync(beside_sum, state, mixed, kept)
    beside = flip(beside_sum, "zl")
    mixed, kept = step(far_blocks, far_bases, 1, state, 0, 2, (mixed, kept))
    far_share, near_share = output_projection(mixed, 0, (ffn_own, first_far), o_tile)
    across = flip(far_share, "c")
    beside, near_share, across, mixed, kept = sync(beside, near_share, across, mixed, kept)
    after_attn, norm_own = sync(*forward_norm(inputs, near_share, across, beside, gain_rows))

    norm_beside, norm_across = flip(norm_own, "zl"), flip(norm_own, "c")
    near_w = [(ffn_own, 0), (ffn_own, up_at), (ffn_own, up_at + half)]
    far_w = [(first_far, 0), (second_far, 0), (second_far, half)]
    early = feed_forward([norm_own, norm_across], [out_cotangent, g_across], near_w, far_w)
    norm_beside, norm_across, early = sync(norm_beside, norm_across, early)
    norm_both = flip(norm_beside, "c")
    late = feed_forward([norm_beside, norm_both], [g_beside, g_both], near_w, far_w)
    late, norm_both = sync(late, norm_both)

    across_both = flip(late[3], "c")
    beside_sum = add_rows(late[2], 0, across_both, 0)
    beside_sum, late, early = sync(beside_sum, late, early)
    beside = flip(beside_sum, "zl")
    across = flip(early[3], "c")
    out_across = [flip(late[1], "c"), flip(early[1], "c")]
    ffn_part = weight_grad(
        [
            (early[7], late[7], early[5], late[5]),
            (early[7], late[7], early[6], late[6]),
            (early[8], late[8], early[4], late[4]),
        ],
        12,
    )
    beside, across, out_across, ffn_part, early, late = sync(beside, across, out_across, ffn_part, early, late)
    ffn_sum = over_groups(ffn_part)
    grad_mid, mid_low = backward_norm(1, early[2], across, beside, after_attn, out_cotangent, gain_rows, [F32, BF])
    grad_mid, mid_low, early, late = sync(grad_mid, mid_low, early, late)

    mid_beside, mid_across = flip(mid_low, "zl"), flip(mid_low, "c")
    out_w = (ffn_own, first_far)
    aug = prepare_back([mid_low, mid_across], 0, out_w, o_tile, kept, query)

    def step_back(blocks, bases, swap, d_query, kinds, *choice):
        swaps = [swap] * len(blocks)
        out = attend_back(*aug, low_rows, high_rows, info, bases, zl_info, blocks, swaps, d_query, kinds, *choice)
        return out[0], list(out[1:])

    def other_half(summed):
        return flip(summed[:, summed.shape[1] // 2 :], "zh")

    kinds = [BF] * len(far_blocks)
    d_query, d_first = step_back(far_blocks, far_bases, 1, None, kinds, 0, 2)
    mid_beside, mid_across, aug, d_query, d_first = sync(mid_beside, mid_across, aug, d_query, d_first)
    mid_both = flip(mid_beside, "c")
    aug = prepare_back([mid_beside, mid_both], 1, out_w, o_tile, kept, query, aug)
    d_query, d_far = step_back(far_blocks, far_bases, 1, None, kinds, 1, 2, (d_query,), d_first)
    mid_both, aug, d_query, d_far, early, late = sync(mid_both, aug, d_query, d_far, early, late)

    back = [lax.ppermute(d_far[2 * n + m], "g", reverse(shift_pairs(d))) for n, d in enumerate(shifts) for m in range(2)]
    d_query, d_other = step_back(other, other_bases, 1, d_query, [BF] * 2)
    d_query, d_same = step_back(same, same_bases, 0, d_query, [BF] * len(same))
    out_sum = add_rows(late[0], 0, out_across[0], 0)
    d_query, d_other, d_same, d_far, back, out_sum = sync(d_query, d_other, d_same, d_far, back, out_sum)

    other_sum = [d_other[m].astype(F32) for m in range(2)]
    for n in range(len(shifts)):
        for m in range(2):
            other_sum[m] = other_sum[m] + back[2 * n + m].astype(F32)
    other_sum = [o.astype(BF) for o in other_sum]
    other_back = [flip(other_sum[0], "zh")]
    same_back = [lax.ppermute(d_same[n], "g", reverse(shift_pairs(d))) for n, d in enumerate(shifts)]
    above_back = []
    if above_groups:
        above = lax.dynamic_slice_in_dim(d_far[-1], zl * rows, rows, 0)
        above_back.append(lax.ppermute(above, ("g", "zh"), reverse(above_pairs)))
    out_beside = flip(out_sum, "zl")
    d_query, d_own = step_back([kv], own_bases, 0, d_query, [F32])
    core = jnp.reshape(2 * c + zl, (1,)).astype(jnp.int32)
    d_q, shares = query_back(core, d_query, qkv_w, cos_table, sin_table)
    q_part = head_grad([norm_one[k] for k in range(4)], d_q)

    def group_slice(part, k):
        return lax.dynamic_slice_in_dim(part, (g ^ k) * shard_pair, shard_pair, 0)

    q_slices = [group_slice(q_part, k) for k in range(groups)]
    other_back, same_back, above_back, d_own, shares, q_slices, other_late, early, late, out_beside = sync(
        other_back, same_back, above_back, d_own, shares, q_slices, other_sum[1], early, late, out_beside
    )

    other_back.append(flip(other_late, "zh"))
    o_part = head_grad([mid_low, mid_beside, mid_across, mid_both], mixed)
    second_column = gain_columns([early[2], late[2], early[3], late[3]], [norm_own, norm_beside, norm_across, norm_both], 1)
    ffn_give = [ffn_sum[:, (3 + n) * half : (4 + n) * half] for n in range(3)]
    q_got = [flip(q_slices[k], "g", k) for k in range(1, groups)]
    other_back, same_back, above_back, d_own, shares, q_slices, q_got, o_part, second_column, ffn_sum, ffn_give = sync(
        other_back, same_back, above_back, d_own, shares, q_slices, q_got, o_part, second_column, ffn_sum, ffn_give
    )
    o_sum = over_groups(o_part)

    gate_far = flip(ffn_give[0], "zh")
    d_kvs, shares = kv_back(core, d_own[0], other_back, same_back, above_back, shares, qkv_w, cos_table, sin_table)
    share_rows = shares.reshape(span, width)
    share_far = share_rows[2 * rows :]
    gate_far, d_kvs, shares, share_rows, share_far, up_give = sync(gate_far, d_kvs, shares, share_rows, share_far, ffn_give[1])
    up_far = flip(up_give, "zh")
    across = flip(share_far, "c")
    kv_part = kv_grad(norm_one, shares, d_kvs, second_column)
    kv_slices = [group_slice(kv_part, k) for k in range(groups)]
    beside_sum = add_rows(share_rows, 1, across, 1)
    down_give = jnp.concatenate([ffn_give[2], o_sum[:, 256:]], 1)
    down_give, beside_sum, kv_slices, across, share_rows, up_far, gate_far, ffn_sum = sync(
        down_give, beside_sum, kv_slices, across, share_rows, up_far, gate_far, ffn_sum
    )

    kv_got = [flip(kv_slices[k], "g", k) for k in range(1, groups)]
    q_sum = q_slices[0].astype(F32) + sum(v.astype(F32) for v in q_got)
    beside = flip(beside_sum, "zl")
    down_far = flip(down_give, "zh")
    down_far, kv_got, q_sum, beside, o_sum, ffn_sum, gate_far, up_far = sync(
        down_far, kv_got, q_sum, beside, o_sum, ffn_sum, gate_far, up_far
    )

    kv_sum = kv_slices[0].astype(F32) + sum(v.astype(F32) for v in kv_got)
    kvq_own = jnp.concatenate([kv_sum[:, :256], q_sum[:, :256]], 1)
    kvq_give = jnp.concatenate([kv_sum[:, 256:], q_sum[:, 256:]], 1).astype(BF)
    kvq_own, kvq_give, down_far, beside = sync(kvq_own, kvq_give, down_far, beside)
    kvq_far = flip(kvq_give, "zh")
    [input_grad] = backward_norm(0, share_rows, across, beside, inputs, grad_mid, gain_rows, [BF])
    far_sum = jnp.concatenate([gate_far, up_far, down_far], 1).astype(F32)
    near_sum = jnp.concatenate([ffn_sum[:, : 3 * half], o_sum[:, :256]], 1).astype(F32)
    sum_own, sum_got = to_owner(near_sum + far_sum)
    layer_out = (after_attn + (early[0].astype(F32) + out_across[1].astype(F32) + out_beside.astype(F32))).astype(BF)
    kvq_far, sum_own, sum_got, input_grad, layer_out = sync(kvq_far, sum_own, sum_got, input_grad, layer_out)

    kvq_own, kvq_got = to_owner(kvq_own + kvq_far.astype(F32))
    gain_sums = (kvq_own + kvq_got)[:, 2 * HEAD : 2 * HEAD + 2]
    gain_sums = gain_sums + flip(gain_sums, "zl")

    def columns(own, got, start, size):
        return in_order(own[:, start : start + size], got[:, start : start + size], 1)

    return (
        layer_out,
        input_grad,
        gain_sums[:, 0] / first_gain.astype(F32),
        columns(kvq_own, kvq_got, 256, 2 * HEAD),
        columns(kvq_own, kvq_got, 0, HEAD),
        columns(kvq_own, kvq_got, HEAD, HEAD),
        columns(sum_own, sum_got, 3 * half, 2 * HEAD).T,
        gain_sums[:, 1] / second_gain.astype(F32),
        columns(sum_own, sum_got, 0, half),
        columns(sum_own, sum_got, half, half),
        columns(sum_own, sum_got, 2 * half, half).T,
    )


def solution(mesh):
    outer, inner = mesh.devices.shape
    fine = Mesh(mesh.devices.reshape(outer // 2, 2, inner // 2, 2), AXES)
    data, tensor = ("g", "c"), ("zh", "zl")
    rows, first = P(AXES, None), P(data)
    wide, tall = P(data, tensor), P(tensor, data)
    return jax.shard_map(
        body,
        mesh=fine,
        in_specs=(rows, first, wide, wide, wide, tall, first, wide, wide, tall, P(), P(), rows),
        out_specs=(rows, rows, first, wide, wide, wide, tall, first, wide, wide, tall),
        check_vma=False,
    )
```

```python
import functools
import math

import jax
import jax.numpy as jnp
from jax import lax
from jax.experimental import pallas as pl
from jax.experimental.layout import Layout, with_layout_constraint
from jax.experimental.pallas import tpu as pltpu
from jax.sharding import Mesh, PartitionSpec as P

HEAD = 96
LANES = 128
PIECE = 256
LEN_FIRST = 4096
LEN_LAST = 2048
LEN_MAX = 4096
epsilon = 1e-05
rope_base = 100000.0
negative = -1e30
far_away = 1 << 30
log2_e = 1.4426950408889634
score_scale = 1.0 / math.sqrt(HEAD)
BF = jnp.bfloat16
F32 = jnp.float32
AXES = ("g", "c", "zh", "zl")
MIB = 1024 * 1024
COST_SHARE = 0.01


def params(mib):
    return pltpu.CompilerParams(vmem_limit_bytes=mib * MIB)


def nn(left, right):
    return lax.dot_general(left, right, (((1,), (0,)), ((), ())), preferred_element_type=F32)


def nt(left, right):
    return lax.dot_general(left, right, (((1,), (1,)), ((), ())), preferred_element_type=F32)


def tn(left, right):
    return lax.dot_general(left, right, (((0,), (0,)), ((), ())), preferred_element_type=F32)


def after(value, *earlier):
    return lax.optimization_barrier((value, *earlier))[0]


def sync(*values):
    return lax.optimization_barrier(values)


def all_groups(value):
    return lax.all_gather(value, "g", axis=0, tiled=True)


def flip(value, axis, bit=1):
    count = lax.axis_size(axis)
    return lax.ppermute(value, axis, [(s, s ^ bit) for s in range(count)])


def cost(us):
    us = us * COST_SHARE
    return pl.CostEstimate(flops=int(us * 1.15e9), bytes_accessed=int(us * 3.6e6), transcendentals=0)


def gather_rows(own):
    beside = flip(own, "zl")
    across = flip(own, "c")
    both = flip(beside, "c")
    return [own, beside, across, both]


def from_groups(value):
    return [value] + [flip(value, "g", k) for k in range(1, lax.axis_size("g"))]


def split_core(shard):
    c = lax.axis_index("c")
    keep = lax.dynamic_index_in_dim(shard, c, 0, False)
    got = flip(lax.dynamic_index_in_dim(shard, 1 - c, 0, False), "c")
    return keep, got


def in_order(keep, got, axis=0):
    c = lax.axis_index("c")
    return jnp.where(c == 0, jnp.concatenate([keep, got], axis), jnp.concatenate([got, keep], axis))


def by_rows(value):
    return with_layout_constraint(value, Layout(major_to_minor=(0, 1)))


def over_groups(value):
    return lax.psum_scatter(value, "g", scatter_dimension=0, tiled=True)


def to_owner(mine):
    c = lax.axis_index("c")
    half = mine.shape[0] // 2
    own = lax.dynamic_slice_in_dim(mine, c * half, half, 0).astype(F32)
    got = flip(lax.dynamic_slice_in_dim(mine, (1 - c) * half, half, 0).astype(BF), "c").astype(F32)
    return own, got


def joined(own, got):
    return in_order(own, got, 1)


def swap_halves(value):
    lane = lax.broadcasted_iota(jnp.int32, value.shape, 1)
    return jnp.where(lane < HEAD // 2, pltpu.roll(value, LANES - HEAD // 2, 1), pltpu.roll(value, HEAD // 2, 1))


def turn(value, cosine, sine):
    return value * cosine + swap_halves(value) * sine


def unturn(value, cosine, sine):
    return value * cosine - swap_halves(value) * sine


def widen(value):
    pad = jnp.zeros((value.shape[0], LANES - HEAD), value.dtype)
    return jnp.concatenate([value, pad], 1)


def qkv_kernel(count, n_jumps, where_ref, *refs):
    pieces, refs = refs[: 2 * count], refs[2 * count :]
    jumps, refs = refs[:n_jumps], refs[n_jumps:]
    x0, x1, x_far, cos_ref, sin_ref, norm_ref, query_ref, kv_ref, weight_ref, gains_ref, x_ref = refs
    step = pl.program_id(0)

    @pl.when(step == 0)
    def _():
        half = pieces[0].shape[0] // 2

        def place(block, n, value):
            for part in range(2):
                at = pl.multiple_of(where_ref[2 * n + part], 64)
                weight_ref[block, pl.ds(at, half), :] = value[part * half : (part + 1) * half, :]

        for block in range(2):
            for n in range(count):
                place(block, n, pieces[block * count + n])
            for n in range(n_jumps):
                place(block, count + n, jumps[n][2 * half * block : 2 * half * (block + 1), :])
        row = lax.broadcasted_iota(jnp.int32, (8, LANES), 0)
        lane = lax.broadcasted_iota(jnp.int32, (8, LANES), 1)
        pick = jnp.where(row == lane, 1.0, 0.0).astype(BF)
        gains_ref[...] = nt(pick, weight_ref[0][:, 4 * HEAD :])

    for k in range(4):

        @pl.when(step == k)
        def _():
            x_ref[...] = (x0, x1)[k][...] if k < 2 else x_far[(k - 2) * PIECE : (k - 1) * PIECE, :]

    x = x_ref[...].astype(F32)
    r = lax.rsqrt(jnp.mean(x * x, axis=-1, keepdims=True) + epsilon)
    normed = (x * r * gains_ref[0:1, :]).astype(BF)
    norm_ref[0] = normed
    cosine, sine = cos_ref[0], sin_ref[0]
    packs = []
    for j in range(2):
        pre = nn(normed, weight_ref[j][:, 0 : 4 * HEAD])
        for h in range(2):
            turned = turn(widen(pre[:, h * HEAD : (h + 1) * HEAD]), cosine, sine)
            query_ref[j, 0, h * PIECE : (h + 1) * PIECE] = (turned * (score_scale * log2_e)).astype(BF)
        packs.append(turn(widen(pre[:, 2 * HEAD : 3 * HEAD]), cosine, sine)[:, 0:HEAD])
        packs.append(pre[:, 3 * HEAD :])
    kv_ref[...] = jnp.concatenate(packs, 1).astype(BF)


def project_qkv(where, pieces, jumps, x_rows, x_far, cos_table, sin_table):
    rows, width = x_rows[0].shape
    n_cols = pieces[0].shape[1]
    table = pl.BlockSpec((1, rows, LANES), lambda i, *_: (i, 0, 0))
    return pl.pallas_call(
        functools.partial(qkv_kernel, len(pieces) // 2, len(jumps)),
        grid_spec=pltpu.PrefetchScalarGridSpec(
            num_scalar_prefetch=1,
            grid=(4,),
            in_specs=[pl.BlockSpec(v.shape, lambda i, *_: (0, 0)) for v in (*pieces, *jumps, *x_rows, x_far)] + [table, table],
            out_specs=[
                pl.BlockSpec((1, rows, width), lambda i, *_: (i, 0, 0)),
                pl.BlockSpec((2, 1, 2 * rows, LANES), lambda i, *_: (0, i, 0, 0)),
                pl.BlockSpec((rows, 4 * HEAD), lambda i, *_: (i, 0)),
                pl.BlockSpec((2, width, n_cols), lambda i, *_: (0, 0, 0)),
                pl.BlockSpec((8, width), lambda i, *_: (0, 0)),
            ],
            scratch_shapes=[pltpu.VMEM((rows, width), BF)],
        ),
        out_shape=[
            jax.ShapeDtypeStruct((4, rows, width), BF),
            jax.ShapeDtypeStruct((2, 4, 2 * rows, LANES), BF),
            jax.ShapeDtypeStruct((4 * rows, 4 * HEAD), BF),
            jax.ShapeDtypeStruct((2, width, n_cols), BF),
            jax.ShapeDtypeStruct((8, width), F32),
        ],
        compiler_params=params(58),
        cost_estimate=cost(8),
        name="project_qkv",
    )(where, *pieces, *jumps, *x_rows, x_far, cos_table, sin_table)


def query_back_kernel(core_ref, dq_ref, weight_ref, cos_ref, sin_ref, grad_ref, share_ref):
    total = None
    for j in range(2):
        heads = []
        for h in range(2):
            turned = unturn(dq_ref[j, 0, h * PIECE : (h + 1) * PIECE], cos_ref[0], sin_ref[0])
            heads.append((turned * score_scale)[:, 0:HEAD])
        grad = jnp.concatenate(heads, 1).astype(BF)
        grad_ref[j, 0] = grad
        term = nt(grad, weight_ref[j][:, 0 : 2 * HEAD])
        total = term if total is None else total + term
    share_ref[0] = total.astype(BF)


def kv_back_kernel(n_same, has_above, core_ref, *refs):
    refs = list(refs)
    own_ref, first_ref, second_ref = refs[:3]
    same_refs = refs[3 : 3 + n_same]
    refs = refs[3 + n_same :]
    i = pl.program_id(0)
    late = i >= 2
    d_kv = own_ref[...] + jnp.where(late, second_ref[...], first_ref[...]).astype(F32)
    for ref in same_refs:
        d_kv = d_kv + ref[...].astype(F32)
    if has_above:
        d_kv = d_kv + jnp.where(i == core_ref[0], refs.pop(0)[...], 0).astype(F32)
    share_in_ref, weight_ref, cos_ref, sin_ref, grad_ref, share_ref = refs
    total = share_in_ref[0].astype(F32)
    for j in range(2):
        both = d_kv[:, 2 * HEAD * j : 2 * HEAD * (j + 1)]
        turned = unturn(widen(both[:, 0:HEAD]), cos_ref[0], sin_ref[0]) * (1.0 / log2_e)
        grad = jnp.concatenate([turned[:, 0:HEAD], both[:, HEAD:]], 1).astype(BF)
        grad_ref[j, 0] = grad
        total = total + nt(grad, weight_ref[j][:, 2 * HEAD : 4 * HEAD])
    share_ref[0] = total.astype(BF)


def project_back(kernel, core, args, specs, weights, cos_table, sin_table, name, mib):
    count, rows, _ = cos_table.shape
    width = weights.shape[1]
    piece = pl.BlockSpec((1, rows, width), lambda i, *_: (i, 0, 0))
    table = pl.BlockSpec((1, rows, cos_table.shape[2]), lambda i, *_: (i, 0, 0))
    return pl.pallas_call(
        kernel,
        grid_spec=pltpu.PrefetchScalarGridSpec(
            num_scalar_prefetch=1,
            grid=(count,),
            in_specs=specs + [pl.BlockSpec((2, width, 4 * HEAD), lambda i, *_: (0, 0, 0)), table, table],
            out_specs=[pl.BlockSpec((2, 1, rows, 2 * HEAD), lambda i, *_: (0, i, 0, 0)), piece],
        ),
        out_shape=[
            jax.ShapeDtypeStruct((2, count, rows, 2 * HEAD), BF),
            jax.ShapeDtypeStruct((count, rows, width), BF),
        ],
        compiler_params=params(mib),
        cost_estimate=cost(4),
        name=name,
    )(core, *args, weights, cos_table, sin_table)


def query_back(core, d_query, weights, cos_table, sin_table):
    spec = pl.BlockSpec((2, 1, 2 * PIECE, LANES), lambda i, *_: (0, i, 0, 0))
    return project_back(query_back_kernel, core, [d_query], [spec], weights, cos_table, sin_table, "query_back", 40)


def kv_back(core, own, other, same, above, shares, weights, cos_table, sin_table):
    rows = pl.BlockSpec((PIECE, 4 * HEAD), lambda i, *_: (i, 0))
    chunk = pl.BlockSpec((PIECE, 4 * HEAD), lambda i, *_: (i % 2, 0))
    args = [own, *other, *same, *above, shares]
    specs = [rows, chunk, chunk] + [rows] * len(same)
    specs += [pl.BlockSpec((PIECE, 4 * HEAD), lambda i, *_: (0, 0))] * len(above)
    specs.append(pl.BlockSpec((1, *shares.shape[1:]), lambda i, *_: (i, 0, 0)))
    kernel = functools.partial(kv_back_kernel, len(same), bool(above))
    return project_back(kernel, core, args, specs, weights, cos_table, sin_table, "kv_back", 58)


CHUNK = 2 * PIECE


def unpack_kv(swaps, block_refs, key_scratch, value_scratch):
    lane = lax.broadcasted_iota(jnp.int32, (CHUNK, LANES - HEAD), 1)
    ones = jnp.where(lane < 3, 1.0, 0.0).astype(BF)
    at = 0
    for swap, ref in zip(swaps, block_refs):
        for start in range(0, ref.shape[0], CHUNK):
            block = ref[start : start + CHUNK, :]
            for j in range(2):
                first = 2 * HEAD * (j ^ swap)
                k = block[:, first : first + HEAD]
                v = block[:, first + HEAD : first + 2 * HEAD]
                key_scratch[j, at : at + CHUNK, :] = jnp.concatenate([k, ones], 1)
                value_scratch[j, at : at + CHUNK, :] = jnp.concatenate([v, ones], 1)
            at += CHUNK


def chunk_state(info_ref, base, i):
    last = base + (CHUNK - 1)
    touched = (base <= info_ref[i, 3]) & (last >= info_ref[i, 0])
    full = (base >= info_ref[i, 1]) & (last <= info_ref[i, 2])
    return touched, full


def forward_kernel(swaps, first, last, offset, stride, n_kept, info_ref, base_ref, zl_ref, *refs):
    refs = list(refs)
    n_blocks = len(swaps)
    query_ref, low_ref, high_ref = refs[:3]
    block_refs = refs[3 : 3 + n_blocks]
    refs = refs[3 + n_blocks :]
    if not first:
        acc_in = refs.pop(0)
    refs = refs[n_kept:]
    if last:
        mixed_ref = refs.pop(0)
    kept_ref = refs.pop(0)
    key_scratch, value_scratch, acc, top = refs
    i = offset + stride * pl.program_id(0)

    @pl.when(pl.program_id(0) == 0)
    def _():
        unpack_kv(swaps, block_refs, key_scratch, value_scratch)

    for j in range(2):
        if first:
            acc[j] = jnp.zeros((CHUNK, LANES), F32)
            top[j] = jnp.full((CHUNK, LANES), negative, F32)
        else:
            acc[j] = acc_in[j, 0]
            top[j] = jnp.broadcast_to(acc_in[j, 0][:, HEAD + 1 : HEAD + 2], (CHUNK, LANES))
    n_chunks = sum(r.shape[0] for r in block_refs) // CHUNK

    def visit(n, masked):
        rows = pl.ds(pl.multiple_of(n * CHUNK, CHUNK), CHUNK)
        if masked:
            at = lax.broadcasted_iota(jnp.int32, (PIECE, CHUNK), 1)
            token = base_ref[n] + lax.rem(at + zl_ref[0] * PIECE, CHUNK)
            low = jnp.concatenate([low_ref[0]] * (CHUNK // LANES), 1)
            high = jnp.concatenate([high_ref[0]] * (CHUNK // LANES), 1)
            allowed = (token >= low) & (token <= high)
        for j in range(2):
            scores = nt(query_ref[j, 0], key_scratch[j, rows, :])
            if masked:
                scores = jnp.concatenate(
                    [jnp.where(allowed, scores[h * PIECE : (h + 1) * PIECE], negative) for h in range(2)], 0
                )
            old = top[j]
            new = jnp.maximum(old, jnp.max(scores, axis=1, keepdims=True))
            top[j] = new
            probs = jnp.exp2(scores - jnp.concatenate([new] * (CHUNK // LANES), 1)).astype(BF)
            acc[j] = acc[j] * jnp.exp2(old - new) + nn(probs, value_scratch[j, rows, :])

    @pl.loop(0, n_chunks)
    def _(n):
        touched, full = chunk_state(info_ref, base_ref[n], i)

        @pl.when(touched & full)
        def _():
            visit(n, False)

        @pl.when(touched & jnp.logical_not(full))
        def _():
            visit(n, True)

    lane = lax.broadcasted_iota(jnp.int32, (CHUNK, LANES), 1)
    if last:
        for j in range(2):
            total = acc[j][:, HEAD : HEAD + 1]
            out = acc[j] / total
            kept_ref[j, 0] = jnp.where(lane < HEAD, out, top[j] + jnp.log2(total))
            mixed_ref[j, 0] = jnp.concatenate([out[0:PIECE, 0:HEAD], out[PIECE:, 0:HEAD]], 1).astype(BF)
    else:
        for j in range(2):
            kept_ref[j, 0] = jnp.where(lane == HEAD + 1, top[j], acc[j])


def attend(query, low, high, info, bases, zl, blocks, swaps, state, last, offset=0, stride=1, kept=()):
    count = query.shape[1]
    n_keys = sum(b.shape[0] for b in blocks)
    per_piece = pl.BlockSpec((2, 1, CHUNK, LANES), lambda i, *_: (0, offset + stride * i, 0, 0))
    bound = pl.BlockSpec((1, PIECE, LANES), lambda i, *_: (offset + stride * i, 0, 0))
    in_specs = [per_piece, bound, bound]
    in_specs += [pl.BlockSpec(b.shape, lambda i, *_: (0, 0)) for b in blocks]
    args = [query, low, high, *blocks]
    if state is not None:
        in_specs.append(per_piece)
        args.append(state)
    aliases = {3 + len(args) + n: n for n in range(len(kept))}
    in_specs += [pl.BlockSpec(memory_space=pl.ANY)] * len(kept)
    args += list(kept)
    wide = jax.ShapeDtypeStruct((2, count, CHUNK, LANES), F32)
    if last:
        out_shape = [jax.ShapeDtypeStruct((2, count, PIECE, 2 * HEAD), BF), wide]
        out_specs = [pl.BlockSpec((2, 1, PIECE, 2 * HEAD), lambda i, *_: (0, offset + stride * i, 0, 0)), per_piece]
    else:
        out_shape = wide
        out_specs = per_piece
    return pl.pallas_call(
        functools.partial(forward_kernel, swaps, state is None, last, offset, stride, len(kept)),
        grid_spec=pltpu.PrefetchScalarGridSpec(
            num_scalar_prefetch=3,
            grid=(count // stride,),
            in_specs=in_specs,
            out_specs=out_specs,
            scratch_shapes=[
                pltpu.VMEM((2, n_keys, LANES), BF),
                pltpu.VMEM((2, n_keys, LANES), BF),
                pltpu.VMEM((2, CHUNK, LANES), F32),
                pltpu.VMEM((2, CHUNK, LANES), F32),
            ],
        ),
        out_shape=out_shape,
        input_output_aliases=aliases,
        compiler_params=params(58),
        cost_estimate=cost(n_keys / 100),
        name="attend",
    )(info, bases, zl, *args)


def split_three(value):
    first = value.astype(BF)
    rest = value - first.astype(F32)
    second = rest.astype(BF)
    third = (rest - second.astype(F32)).astype(BF)
    return first, second, third


def augment(wide, extra):
    lane = lax.broadcasted_iota(jnp.int32, wide.shape, 1)
    a, b, c = (part.astype(F32) for part in split_three(extra))
    out = wide.astype(F32)
    out = jnp.where(lane == HEAD, a, out)
    out = jnp.where(lane == HEAD + 1, b, out)
    out = jnp.where(lane == HEAD + 2, c, out)
    return out.astype(BF)


def prepare_kernel(n_kept, m0, m1, w0, w1, kept_ref, query_ref, *refs):
    q_aug_ref, o_aug_ref, mid_ref = refs[n_kept:]
    step = pl.program_id(0)
    for k, ref in enumerate((m0, m1)):

        @pl.when(step == k)
        def _():
            mid_ref[...] = ref[...]

    mid = mid_ref[...]
    for j, weight_ref in enumerate((w0, w1)):
        grad = nn(mid, weight_ref[...][:, 0 : 2 * HEAD])
        wide = jnp.concatenate([widen(grad[:, 0:HEAD]), widen(grad[:, HEAD : 2 * HEAD])], 0).astype(BF)
        kept = kept_ref[j, 0]
        delta = jnp.sum(wide.astype(F32) * kept, axis=1, keepdims=True)
        q_aug_ref[j, 0] = augment(query_ref[j, 0], -kept[:, HEAD : HEAD + 1])
        o_aug_ref[j, 0] = augment(wide, -delta)


def prepare_back(mid, offset, weights, tile, kept, query, done=()):
    rows, width = mid[0].shape
    per_piece = pl.BlockSpec((2, 1, CHUNK, LANES), lambda i: (0, offset + 2 * i, 0, 0))
    return pl.pallas_call(
        functools.partial(prepare_kernel, len(done)),
        grid=(2,),
        in_specs=[pl.BlockSpec((rows, width), lambda i: (0, 0))] * 2
        + [pl.BlockSpec((width, 256), lambda i: (0, tile))] * 2
        + [per_piece, per_piece]
        + [pl.BlockSpec(memory_space=pl.ANY)] * len(done),
        out_specs=[per_piece, per_piece],
        out_shape=[jax.ShapeDtypeStruct(query.shape, BF)] * 2,
        scratch_shapes=[pltpu.VMEM((rows, width), BF)],
        input_output_aliases={6 + n: n for n in range(len(done))},
        compiler_params=params(58),
        cost_estimate=cost(6),
        name="prepare_back",
    )(*mid, *weights, kept, query, *done)


def backward_kernel(swaps, has_dq, offset, stride, n_kept, n_more, info_ref, base_ref, zl_ref, *refs):
    refs = list(refs)
    n_blocks = len(swaps)
    q_aug, o_aug, low_ref, high_ref = refs[:4]
    block_refs = refs[4 : 4 + n_blocks]
    refs = refs[4 + n_blocks :]
    if has_dq:
        dq_in = refs.pop(0)
    more_refs, refs = refs[:n_more], refs[n_more + n_kept :]
    dq_ref = refs.pop(0)
    out_refs = refs[:n_blocks]
    key_scratch, value_scratch, d_key, d_value = refs[n_blocks:]
    i = offset + stride * pl.program_id(0)

    @pl.when(pl.program_id(0) == 0)
    def _():
        unpack_kv(swaps, block_refs, key_scratch, value_scratch)
        d_key[...] = jnp.zeros(d_key.shape, F32)
        d_value[...] = jnp.zeros(d_value.shape, F32)

    for j in range(2):
        if has_dq:
            dq_ref[j, 0] = dq_in[j, 0]
        else:
            dq_ref[j, 0] = jnp.zeros((CHUNK, LANES), F32)
    n_chunks = sum(r.shape[0] for r in block_refs) // CHUNK

    def visit(n, masked):
        rows = pl.ds(pl.multiple_of(n * CHUNK, CHUNK), CHUNK)
        if masked:
            at = lax.broadcasted_iota(jnp.int32, (CHUNK, CHUNK), 0)
            token = base_ref[n] + lax.rem(at + zl_ref[0] * PIECE, CHUNK)
            allowed = (token >= low_ref[0, 0:1, :]) & (token <= high_ref[0, 0:1, :])
        for j in range(2):
            keys = key_scratch[j, rows, :]
            probs = jnp.exp2(nt(keys, q_aug[j, 0]))
            if masked:
                probs = jnp.where(allowed, probs, 0.0)
            d_probs = nt(value_scratch[j, rows, :], o_aug[j, 0])
            low_probs = probs.astype(BF)
            d_scores = (probs * d_probs).astype(BF)
            d_value[j, rows, :] += nn(low_probs, o_aug[j, 0])
            d_key[j, rows, :] += nn(d_scores, q_aug[j, 0])
            dq_ref[j, 0] += tn(d_scores, keys)

    @pl.loop(0, n_chunks)
    def _(n):
        touched, full = chunk_state(info_ref, base_ref[n], i)

        @pl.when(touched & full)
        def _():
            visit(n, False)

        @pl.when(touched & jnp.logical_not(full))
        def _():
            visit(n, True)

    @pl.when(pl.program_id(0) == pl.num_programs(0) - 1)
    def _():
        at = 0
        for n, (swap, ref) in enumerate(zip(swaps, out_refs)):
            for start in range(0, ref.shape[0], CHUNK):
                parts = []
                for j in (swap, 1 - swap):
                    parts.append(d_key[j, at : at + CHUNK, :][:, 0:HEAD])
                    parts.append(d_value[j, at : at + CHUNK, :][:, 0:HEAD])
                whole = jnp.concatenate(parts, 1)
                if n_more:
                    whole = whole + more_refs[n][start : start + CHUNK, :].astype(F32)
                ref[start : start + CHUNK, :] = whole.astype(ref.dtype)
                at += CHUNK


def attend_back(q_aug, o_aug, low, high, info, bases, zl, blocks, swaps, d_query, kinds, offset=0, stride=1, kept=(), more=()):
    count = q_aug.shape[1]
    n_keys = sum(b.shape[0] for b in blocks)
    per_piece = pl.BlockSpec((2, 1, CHUNK, LANES), lambda i, *_: (0, offset + stride * i, 0, 0))
    bound = pl.BlockSpec((1, 8, CHUNK), lambda i, *_: (offset + stride * i, 0, 0))
    whole = [pl.BlockSpec(b.shape, lambda i, *_: (0, 0)) for b in blocks]
    in_specs = [per_piece, per_piece, bound, bound, *whole]
    args = [q_aug, o_aug, low, high, *blocks]
    if d_query is not None:
        in_specs.append(per_piece)
        args.append(d_query)
    in_specs += [pl.BlockSpec(m.shape, lambda i, *_: (0, 0)) for m in more]
    args += list(more)
    aliases = {3 + len(args) + n: n for n in range(len(kept))}
    in_specs += [pl.BlockSpec(memory_space=pl.ANY)] * len(kept)
    args += list(kept)
    return pl.pallas_call(
        functools.partial(backward_kernel, swaps, d_query is not None, offset, stride, len(kept), len(more)),
        grid_spec=pltpu.PrefetchScalarGridSpec(
            num_scalar_prefetch=3,
            grid=(count // stride,),
            in_specs=in_specs,
            out_specs=[per_piece, *whole],
            scratch_shapes=[
                pltpu.VMEM((2, n_keys, LANES), BF),
                pltpu.VMEM((2, n_keys, LANES), BF),
                pltpu.VMEM((2, n_keys, LANES), F32),
                pltpu.VMEM((2, n_keys, LANES), F32),
            ],
        ),
        out_shape=[jax.ShapeDtypeStruct((2, count, CHUNK, LANES), F32)]
        + [jax.ShapeDtypeStruct(b.shape, k) for b, k in zip(blocks, kinds)],
        input_output_aliases=aliases,
        compiler_params=params(56),
        cost_estimate=cost(n_keys / 64),
        name="attend_back",
    )(info, bases, zl, *args)


def ffn_kernel(tiles, n0, n1, g0, g1, *refs):
    own_refs, other_refs, refs = refs[0:3], refs[3:6], refs[6:]
    o0, o1, b0, b1, hidden_ref, dg_ref, du_ref, norm_t, grad_t, norm_ref, grad_ref, acc_out, acc_back = refs
    step = pl.program_id(0)

    @pl.when(step == 0)
    def _():
        norm_ref[0:PIECE] = n0[...]
        norm_ref[PIECE:] = n1[...]
        grad_ref[0:PIECE] = g0[...]
        grad_ref[PIECE:] = g1[...]

    def run(gate_ref, up_ref, down_ref, first):
        gate_w, up_w, down_w = gate_ref[...], up_ref[...], down_ref[...]
        gate = nn(norm_ref[...], gate_w)
        up = nn(norm_ref[...], up_w)
        d_hidden = nn(grad_ref[...], down_w)
        sig = 0.5 * jnp.tanh(0.5 * gate) + 0.5
        silu = gate * sig
        hidden = (silu * up).astype(BF)
        d_gate = (d_hidden * up * (sig + silu * (1.0 - sig))).astype(BF)
        d_up = (d_hidden * silu).astype(BF)
        hidden_ref[...] = hidden
        dg_ref[...] = d_gate
        du_ref[...] = d_up
        norm_t[...] = norm_ref[pl.ds(pl.multiple_of(step * LANES, LANES), LANES), :].T
        grad_t[...] = grad_ref[pl.ds(pl.multiple_of(step * LANES, LANES), LANES), :].T
        out = nt(hidden, down_w)
        back = nt(d_gate, gate_w) + nt(d_up, up_w)
        if first:
            acc_out[...] = out
            acc_back[...] = back
        else:
            acc_out[...] += out
            acc_back[...] += back

    @pl.when(step == 0)
    def _():
        run(*own_refs, True)

    @pl.when((step > 0) & (step < tiles))
    def _():
        run(*own_refs, False)

    @pl.when(step >= tiles)
    def _():
        run(*other_refs, False)

    @pl.when(step == pl.num_programs(0) - 1)
    def _():
        o0[...] = acc_out[0:PIECE].astype(BF)
        o1[...] = acc_out[PIECE:].astype(BF)
        b0[...] = acc_back[0:PIECE].astype(BF)
        b1[...] = acc_back[PIECE:].astype(BF)


def feed_forward(norm_rows, grad_rows, own, other):
    rows, width = norm_rows[0].shape
    half = 512
    tile = 256
    tiles = half // tile
    whole = pl.BlockSpec((rows, width), lambda s: (0, 0))

    def own_spec(at):
        return pl.BlockSpec((width, tile), lambda s: (0, at // tile + jnp.minimum(s, tiles - 1)))

    def other_spec(at):
        return pl.BlockSpec((width, tile), lambda s: (0, at // tile + jnp.maximum(s - tiles, 0)))

    hid = pl.BlockSpec((2 * rows, tile), lambda s: (0, s))
    turned = pl.BlockSpec((width, LANES), lambda s: (0, s))
    return pl.pallas_call(
        functools.partial(ffn_kernel, tiles),
        grid=(2 * tiles,),
        in_specs=[whole] * 4 + [own_spec(at) for _, at in own] + [other_spec(at) for _, at in other],
        out_specs=[whole] * 4 + [hid] * 3 + [turned] * 2,
        out_shape=[jax.ShapeDtypeStruct((rows, width), BF)] * 4
        + [jax.ShapeDtypeStruct((2 * rows, 2 * half), BF)] * 3
        + [jax.ShapeDtypeStruct((width, 2 * rows), BF)] * 2,
        scratch_shapes=[pltpu.VMEM((2 * rows, width), BF)] * 2 + [pltpu.VMEM((2 * rows, width), F32)] * 2,
        compiler_params=params(56),
        cost_estimate=cost(18),
        name="feed_forward",
    )(*norm_rows, *grad_rows, *(w for w, _ in own), *(w for w, _ in other))


def weight_grad_kernel(n_jobs, *refs):
    out_ref = refs[-1]
    for n in range(n_jobs):
        left_early, left_late, early, late = refs[4 * n : 4 * n + 4]

        @pl.when(pl.program_id(1) == n)
        def _():
            total = nn(left_early[...], early[...]) + nn(left_late[...], late[...])
            out_ref[...] = total.astype(BF)


def weight_grad(jobs, us):
    width, depth = jobs[0][0].shape
    half = jobs[0][2].shape[1] // 2
    count = len(jobs)
    left = pl.BlockSpec((width, depth), lambda s, n: (0, 0))
    cols = pl.BlockSpec((depth, half), lambda s, n: (0, s))
    return pl.pallas_call(
        functools.partial(weight_grad_kernel, count),
        grid=(2, count),
        in_specs=[left, left, cols, cols] * count,
        out_specs=pl.BlockSpec((width, half), lambda s, n: (0, s * count + n)),
        out_shape=jax.ShapeDtypeStruct((width, 2 * count * half), BF),
        compiler_params=params(48),
        cost_estimate=cost(us),
        name="weight_grad",
    )(*(value for job in jobs for value in job))


def head_grad_kernel(l0, l1, l2, l3, right_ref, out_ref):
    for j in range(2):
        total = None
        for k, left in enumerate((l0, l1, l2, l3)):
            term = tn(left[...], right_ref[j, k])
            total = term if total is None else total + term
        wide = jnp.concatenate([total, jnp.zeros((total.shape[0], 256 - 2 * HEAD), F32)], 1)
        out_ref[:, j * 256 : (j + 1) * 256] = wide.astype(BF)


def head_grad(left, right):
    rows, width = left[0].shape
    tile = 512
    return pl.pallas_call(
        head_grad_kernel,
        grid=(width // tile,),
        in_specs=[pl.BlockSpec((rows, tile), lambda s: (0, s))] * 4 + [pl.BlockSpec(right.shape, lambda s: (0, 0, 0, 0))],
        out_specs=pl.BlockSpec((tile, 512), lambda s: (s, 0)),
        out_shape=jax.ShapeDtypeStruct((width, 512), BF),
        compiler_params=params(40),
        cost_estimate=cost(3),
        name="head_grad",
    )(*left, right)


def gain_kernel(lane, *refs):
    out_ref = refs[-1]
    count = (len(refs) - 1) // 2
    at = lax.broadcasted_iota(jnp.int32, (PIECE, LANES), 1)
    pick = jnp.where(at == lane, 1.0, 0.0).astype(BF)
    total = None
    for share, normed in zip(refs[:count], refs[count : 2 * count]):
        product = (share[...].astype(F32) * normed[...].astype(F32)).astype(BF)
        term = tn(product, pick)
        total = term if total is None else total + term
    out_ref[...] = total


def gain_columns(shares, normed, lane):
    rows, width = shares[0].shape
    tile = 512
    spec = pl.BlockSpec((rows, tile), lambda s: (0, s))
    return pl.pallas_call(
        functools.partial(gain_kernel, lane),
        grid=(width // tile,),
        in_specs=[spec] * 8,
        out_specs=pl.BlockSpec((tile, LANES), lambda s: (s, 0)),
        out_shape=jax.ShapeDtypeStruct((width, LANES), F32),
        compiler_params=params(40),
        cost_estimate=cost(3),
        name="gain_columns",
    )(*shares, *normed)


def kv_grad_kernel(norm_ref, share_ref, dkv_ref, column_ref, *refs):
    out_ref = refs[-1]
    at = lax.broadcasted_iota(jnp.int32, (PIECE, LANES), 1)
    pick = jnp.where(at == 0, 1.0, 0.0).astype(BF)
    columns = column_ref[...]
    totals = [None, None]
    for k in range(4):
        normed = norm_ref[k]
        product = (share_ref[k].astype(F32) * normed.astype(F32)).astype(BF)
        columns = columns + tn(product, pick)
        for j in range(2):
            term = tn(normed, dkv_ref[j, k])
            totals[j] = term if totals[j] is None else totals[j] + term
    for j in range(2):
        out_ref[:, j * 256 : (j + 1) * 256] = jnp.concatenate([totals[j], columns[:, 0 : 256 - 2 * HEAD]], 1).astype(BF)


def kv_grad(normed, shares, d_kvs, columns):
    count, rows, width = normed.shape
    tile = 512
    spec = pl.BlockSpec((count, rows, tile), lambda s: (0, 0, s))
    return pl.pallas_call(
        kv_grad_kernel,
        grid=(width // tile,),
        in_specs=[
            spec,
            spec,
            pl.BlockSpec(d_kvs.shape, lambda s: (0, 0, 0, 0)),
            pl.BlockSpec((tile, LANES), lambda s: (s, 0)),
        ],
        out_specs=pl.BlockSpec((tile, 512), lambda s: (s, 0)),
        out_shape=jax.ShapeDtypeStruct((width, 512), BF),
        compiler_params=params(40),
        cost_estimate=cost(4),
        name="kv_grad",
    )(normed, shares, d_kvs, columns)


def output_kernel(mixed_ref, w0, w1, far_ref, near_ref):
    step = pl.program_id(0)
    total = None
    for j, weight in enumerate((w0, w1)):
        term = nt(mixed_ref[j, 0], weight[...][:, 0 : 2 * HEAD])
        total = term if total is None else total + term

    @pl.when(step == 0)
    def _():
        far_ref[...] = total.astype(BF)

    @pl.when(step == 1)
    def _():
        near_ref[...] = total


def output_projection(mixed, offset, weights, tile):
    _, count, rows, width_heads = mixed.shape
    width = weights[0].shape[0]
    whole = pl.BlockSpec((rows, width), lambda s: (0, 0))
    return pl.pallas_call(
        output_kernel,
        grid=(2,),
        in_specs=[pl.BlockSpec((2, 1, rows, width_heads), lambda s: (0, offset + 2 * (1 - s), 0, 0))]
        + [pl.BlockSpec((width, 256), lambda s: (0, tile))] * 2,
        out_specs=[whole, whole],
        out_shape=[jax.ShapeDtypeStruct((rows, width), BF), jax.ShapeDtypeStruct((rows, width), F32)],
        compiler_params=params(58),
        cost_estimate=cost(4),
        name="output_projection",
    )(mixed, *weights)


def add_kernel(near_ref, across_ref, out_ref):
    out_ref[...] = (near_ref[...].astype(F32) + across_ref[...].astype(F32)).astype(BF)


def add_rows(near, near_at, across, across_at):
    rows, width = PIECE, near.shape[1]
    return pl.pallas_call(
        add_kernel,
        grid=(1,),
        in_specs=[
            pl.BlockSpec((rows, width), lambda s: (near_at, 0)),
            pl.BlockSpec((rows, width), lambda s: (across_at, 0)),
        ],
        out_specs=pl.BlockSpec((rows, width), lambda s: (0, 0)),
        out_shape=jax.ShapeDtypeStruct((rows, width), BF),
        compiler_params=params(32),
        cost_estimate=cost(1),
        name="add_rows",
    )(near, across)


def forward_norm_kernel(x_ref, near_ref, across_ref, beside_ref, gain_ref, after_ref, norm_ref):
    rows = x_ref[...].astype(F32) + (near_ref[...] + across_ref[...].astype(F32) + beside_ref[...].astype(F32))
    after_ref[...] = rows
    r = lax.rsqrt(jnp.mean(rows * rows, axis=-1, keepdims=True) + epsilon)
    norm_ref[...] = (rows * r * gain_ref[1:2, :]).astype(BF)


def row_specs(width, n):
    return [pl.BlockSpec((LANES, width), lambda i: (i, 0))] * n


def forward_norm(x, near, across, beside, gain_rows):
    rows, width = x.shape
    return pl.pallas_call(
        forward_norm_kernel,
        grid=(rows // LANES,),
        in_specs=row_specs(width, 4) + [pl.BlockSpec((8, width), lambda i: (0, 0))],
        out_specs=row_specs(width, 2),
        out_shape=[jax.ShapeDtypeStruct((rows, width), F32), jax.ShapeDtypeStruct((rows, width), BF)],
        compiler_params=params(32),
        cost_estimate=cost(2),
        name="forward_norm",
    )(x, near, across, beside, gain_rows)


def backward_norm_kernel(which, share_ref, across_ref, beside_ref, rows_ref, base_ref, gain_ref, *out_refs):
    upstream = share_ref[...].astype(F32) + across_ref[...].astype(F32) + beside_ref[...].astype(F32)
    rows = rows_ref[...].astype(F32)
    r = lax.rsqrt(jnp.mean(rows * rows, axis=-1, keepdims=True) + epsilon)
    weighted = upstream * gain_ref[which : which + 1, :]
    inner = jnp.mean(weighted * rows, axis=-1, keepdims=True)
    out = base_ref[...].astype(F32) + (r * weighted - rows * (r * r * r) * inner)
    for ref in out_refs:
        ref[...] = out.astype(ref.dtype)


def backward_norm(which, share, across, beside, rows, base, gain_rows, kinds):
    count, width = rows.shape
    return pl.pallas_call(
        functools.partial(backward_norm_kernel, which),
        grid=(count // LANES,),
        in_specs=row_specs(width, 5) + [pl.BlockSpec((8, width), lambda i: (0, 0))],
        out_specs=row_specs(width, len(kinds)),
        out_shape=[jax.ShapeDtypeStruct((count, width), kind) for kind in kinds],
        compiler_params=params(32),
        cost_estimate=cost(2),
        name="backward_norm",
    )(share, across, beside, rows, base, gain_rows)


def token_tables(token, seq_lengths, piece_starts):
    n = seq_lengths.shape[0]
    upto = jnp.arange(n)[None, :] <= jnp.arange(n)[:, None]
    ends = jnp.sum(jnp.where(upto, seq_lengths[None, :], 0), axis=1)
    after = token[:, None] >= ends[None, :]
    start = jnp.sum(jnp.where(after, seq_lengths[None, :], 0), axis=1)
    end = jnp.min(jnp.where(after, far_away, ends[None, :]), axis=1)
    inside = (token[:, None] >= piece_starts[None, :]) & (token[:, None] < piece_starts[None, :] + PIECE)
    piece_end = jnp.max(jnp.where(inside, piece_starts[None, :] + PIECE, 0), axis=1)
    high = jnp.maximum(token, jnp.minimum(piece_end, end) - 1)
    return start, high


def may_meet(one, two, group_tokens, count):
    total = group_tokens * count
    regions = ((0, LEN_FIRST, LEN_FIRST), (LEN_FIRST, total - LEN_LAST, LEN_MAX), (total - LEN_LAST, total, LEN_LAST))
    for start, end, longest in regions:
        both = all(g * group_tokens < end and (g + 1) * group_tokens > start for g in (one, two))
        if both and (abs(one - two) - 1) * group_tokens + 1 < longest:
            return True
    return False


def body(
    inputs,
    first_gain,
    query_weight,
    key_matrix,
    value_matrix,
    output_weight,
    second_gain,
    gate_weight,
    up_weight,
    down_weight,
    seq_lengths,
    piece_starts,
    out_cotangent,
):
    g, c, zh, zl = (lax.axis_index(a) for a in AXES)
    groups = lax.axis_size("g")
    rows, width = inputs.shape
    span = 4 * rows
    group_tokens = 2 * span
    shard_rows = query_weight.shape[0]

    order = jnp.arange(4)
    piece_base = (2 * g + (c ^ (order >> 1))) * span + zh * CHUNK + (zl ^ (order & 1)) * rows
    token = (piece_base[:, None] + jnp.arange(rows)[None, :]).reshape(-1).astype(jnp.int32)
    low, high = token_tables(token, seq_lengths, piece_starts)
    position = (token - low).astype(F32)
    low, high = low.reshape(4, rows), high.reshape(4, rows)
    info = jnp.stack([low.min(1), low.max(1), high.min(1), high.max(1)], 1).astype(jnp.int32)
    low_wide = jnp.broadcast_to(low[:, :, None], (4, rows, LANES)).astype(jnp.int32)
    high_wide = jnp.broadcast_to(high[:, :, None], (4, rows, LANES)).astype(jnp.int32)
    low_rows = jnp.broadcast_to(jnp.tile(low, (1, 2))[:, None, :], (4, 8, CHUNK)).astype(jnp.int32)
    high_rows = jnp.broadcast_to(jnp.tile(high, (1, 2))[:, None, :], (4, 8, CHUNK)).astype(jnp.int32)
    zl_info = jnp.reshape(zl, (1,)).astype(jnp.int32)
    frequency = rope_base ** (-(2.0 / HEAD) * jnp.arange(HEAD // 2, dtype=F32))
    angles = position[:, None] * frequency[None, :]
    cosine, sine = jnp.cos(angles), jnp.sin(angles)
    pad = jnp.zeros((span, LANES - HEAD), F32)
    cos_table = jnp.concatenate([cosine, cosine, pad], 1).reshape(4, rows, LANES)
    sin_table = jnp.concatenate([-sine, sine, pad], 1).reshape(4, rows, LANES)

    def halves(matrix):
        return matrix.reshape(matrix.shape[0], 2, -1).transpose(1, 0, 2)

    blank = functools.partial(jnp.zeros, dtype=BF)
    half = gate_weight.shape[1] // 2
    zl_info = jnp.reshape(zl, (1,)).astype(jnp.int32)
    core = jnp.reshape(2 * c + zl, (1,)).astype(jnp.int32)
    shard_pair = 2 * shard_rows

    gains = jnp.broadcast_to(jnp.stack([first_gain, second_gain], 1)[None], (2, shard_rows, 2))
    qkv_shard = jnp.concatenate(
        [halves(query_weight), halves(key_matrix), halves(value_matrix), gains, blank((2, shard_rows, 126))], 2
    )
    qkv_keep, qkv_got = split_core(qkv_shard)
    ffn_shard = jnp.concatenate(
        [halves(gate_weight), halves(output_weight.T), blank((2, shard_rows, 64)), halves(up_weight), halves(down_weight.T)],
        2,
    )
    ffn_keep, ffn_got = split_core(ffn_shard)
    qkv_pair = jnp.concatenate([qkv_keep, qkv_got], 0)
    inputs, out_cotangent, qkv_pair, ffn_keep, ffn_got = sync(inputs, out_cotangent, qkv_pair, ffn_keep, ffn_got)

    qkv_other = flip(qkv_pair, "zh")
    hops = [k for k in range(1, groups) if k & -k == k]
    jumps = [k for k in range(1, groups) if k & -k != k]
    qkv_near = [flip(qkv_pair, "g", k) for k in (*hops, *jumps)]
    x_beside = flip(inputs, "zl")
    ffn_pair = in_order(ffn_keep, ffn_got)
    up_at = half + 2 * HEAD + 64
    first_pair = ffn_pair[:, :up_at]
    up_pair, down_pair = ffn_pair[:, up_at : up_at + half], ffn_pair[:, up_at + half :]
    (
        qkv_other, qkv_near, x_beside, ffn_pair, first_pair, up_pair, down_pair, cos_table, sin_table,
        info, low_wide, high_wide, low_rows, high_rows,
    ) = sync(
        qkv_other, qkv_near, x_beside, ffn_pair, first_pair, up_pair, down_pair, cos_table, sin_table,
        info, low_wide, high_wide, low_rows, high_rows,
    )
    x_near = jnp.concatenate([inputs, x_beside], 0)

    ffn_own = all_groups(ffn_pair)
    qkv_far = [flip(qkv_other, "g", k) for k in (*hops, *jumps)]
    x_far = flip(x_near, "c")
    first_other = flip(first_pair, "zh")
    qkv_far, x_far, first_other, up_pair, out_cotangent = sync(qkv_far, x_far, first_other, up_pair, out_cotangent)

    up_other = flip(up_pair, "zh")
    k_order = jnp.array([0, *hops, *jumps])[:, None]
    piece_rows = (g ^ k_order) * shard_pair + (c ^ jnp.arange(2)[None, :]) * shard_rows
    norm_one, query, kv, qkv_w, gain_rows = project_qkv(
        piece_rows.reshape(-1).astype(jnp.int32),
        [qkv_pair, *qkv_near, qkv_other, *qkv_far],
        [],
        [inputs, x_beside],
        x_far,
        cos_table,
        sin_table,
    )
    first_piece = lax.dynamic_slice_in_dim(kv, (2 * c + zl) * rows, rows, 0)
    norm_one, query, kv, qkv_w, gain_rows, kv_chunks, first_piece, out_cotangent, up_other, down_pair, first_other = sync(
        norm_one,
        query,
        kv,
        qkv_w,
        gain_rows,
        [kv[n * CHUNK : (n + 1) * CHUNK] for n in range(2)],
        first_piece,
        out_cotangent,
        up_other,
        down_pair,
        first_other,
    )
    first_far = all_groups(first_other)

    def chunk_bases(group, side):
        return jnp.stack([(2 * group + (c ^ i)) * span + side * CHUNK for i in range(2)]).astype(jnp.int32)

    def shift_pairs(steps):
        return [(s, s + steps) for s in range(groups) if 0 <= s + steps < groups and may_meet(s, s + steps, group_tokens, groups)]

    def present(pairs, bases):
        target = functools.reduce(jnp.logical_or, [g == t for _, t in pairs])
        return jnp.where(target, bases, far_away).astype(jnp.int32)

    def reverse(pairs):
        return [(t, s) for s, t in pairs]

    shifts = [d for d in range(1, groups) if shift_pairs(d)]
    above_groups = [s for s in range(1, groups) if may_meet(s - 1, s, group_tokens, groups)]
    above_pairs = [(2 * s, 2 * (s - 1) + 1) for s in above_groups]
    own_bases, other_bases = chunk_bases(g, zh), chunk_bases(g, 1 - zh)
    same_bases = [present(shift_pairs(d), chunk_bases(g - d, zh)) for d in shifts]
    far_bases = [present(shift_pairs(d), chunk_bases(g - d, 1 - zh)) for d in shifts]
    if above_groups:
        is_target = functools.reduce(jnp.logical_or, [(g == s - 1) & (zh == 1) for s in above_groups])
        far_bases.append(jnp.where(is_target, jnp.reshape(2 * (g + 1) * span, (1,)), far_away).astype(jnp.int32))
    same_bases, far_bases = jnp.concatenate(same_bases), jnp.concatenate(far_bases)

    def step(blocks, bases, swap, state, *choice):
        swaps = [swap] * len(blocks)
        return attend(query, low_wide, high_wide, info, bases, zl_info, blocks, swaps, state, bool(choice), *choice)

    other = [flip(kv_chunks[0], "zh")]
    same = [lax.ppermute(kv, "g", shift_pairs(d)) for d in shifts]
    g_beside, g_across = flip(out_cotangent, "zl"), flip(out_cotangent, "c")
    state = step([kv], own_bases, 0, None)
    other, same, g_beside, g_across, state, kv_late = sync(other, same, g_beside, g_across, state, kv_chunks[1])

    other.append(flip(kv_late, "zh"))
    far_blocks = [[lax.ppermute(other[0], "g", shift_pairs(d))] for d in shifts]
    state = step(same, same_bases, 0, state)
    g_both = flip(g_beside, "c")
    other, far_blocks, g_both, state, down_pair, first_piece, ffn_own = sync(
        other, far_blocks, g_both, state, down_pair, first_piece, ffn_own
    )

    for n, d in enumerate(shifts):
        far_blocks[n].append(lax.ppermute(other[1], "g", shift_pairs(d)))
    far_blocks = [b for pair in far_blocks for b in pair]
    if above_groups:
        above = lax.ppermute(first_piece, ("g", "zh"), above_pairs)
        far_blocks.append(lax.dynamic_update_slice(jnp.zeros((CHUNK, 4 * HEAD), BF), above, (zl * rows, 0)))
    down_other = flip(down_pair, "zh")
    state = step(other, other_bases, 1, state)
    far_blocks, down_other, state = sync(far_blocks, down_other, state)

    second_far = all_groups(jnp.concatenate([up_other, down_other], 1))
    o_tile = half // 256
    mixed, kept = step(far_blocks, far_bases, 1, state, 1, 2)
    mixed, kept, first_far = sync(mixed, kept, first_far)

    far_share, near_share = output_projection(mixed, 1, (ffn_own, first_far), o_tile)
    beside_sum = add_rows(near_share, 0, flip(far_share, "c"), 0)
    beside_sum, state, mixed, kept = sync(beside_sum, state, mixed, kept)
    beside = flip(beside_sum, "zl")
    mixed, kept = step(far_blocks, far_bases, 1, state, 0, 2, (mixed, kept))
    far_share, near_share = output_projection(mixed, 0, (ffn_own, first_far), o_tile)
    across = flip(far_share, "c")
    beside, near_share, across, mixed, kept = sync(beside, near_share, across, mixed, kept)
    after_attn, norm_own = sync(*forward_norm(inputs, near_share, across, beside, gain_rows))

    norm_beside, norm_across = flip(norm_own, "zl"), flip(norm_own, "c")
    near_w = [(ffn_own, 0), (ffn_own, up_at), (ffn_own, up_at + half)]
    far_w = [(first_far, 0), (second_far, 0), (second_far, half)]
    early = feed_forward([norm_own, norm_across], [out_cotangent, g_across], near_w, far_w)
    norm_beside, norm_across, early = sync(norm_beside, norm_across, early)
    norm_both = flip(norm_beside, "c")
    late = feed_forward([norm_beside, norm_both], [g_beside, g_both], near_w, far_w)
    late, norm_both = sync(late, norm_both)

    across_both = flip(late[3], "c")
    beside_sum = add_rows(late[2], 0, across_both, 0)
    beside_sum, late, early = sync(beside_sum, late, early)
    beside = flip(beside_sum, "zl")
    across = flip(early[3], "c")
    out_across = [flip(late[1], "c"), flip(early[1], "c")]
    ffn_part = weight_grad(
        [
            (early[7], late[7], early[5], late[5]),
            (early[7], late[7], early[6], late[6]),
            (early[8], late[8], early[4], late[4]),
        ],
        12,
    )
    beside, across, out_across, ffn_part, early, late = sync(beside, across, out_across, ffn_part, early, late)
    ffn_sum = over_groups(ffn_part)
    grad_mid, mid_low = backward_norm(1, early[2], across, beside, after_attn, out_cotangent, gain_rows, [F32, BF])
    grad_mid, mid_low, early, late = sync(grad_mid, mid_low, early, late)

    mid_beside, mid_across = flip(mid_low, "zl"), flip(mid_low, "c")
    out_w = (ffn_own, first_far)
    aug = prepare_back([mid_low, mid_across], 0, out_w, o_tile, kept, query)

    def step_back(blocks, bases, swap, d_query, kinds, *choice):
        swaps = [swap] * len(blocks)
        out = attend_back(*aug, low_rows, high_rows, info, bases, zl_info, blocks, swaps, d_query, kinds, *choice)
        return out[0], list(out[1:])

    def other_half(summed):
        return flip(summed[:, summed.shape[1] // 2 :], "zh")

    kinds = [BF] * len(far_blocks)
    d_query, d_first = step_back(far_blocks, far_bases, 1, None, kinds, 0, 2)
    mid_beside, mid_across, aug, d_query, d_first = sync(mid_beside, mid_across, aug, d_query, d_first)
    mid_both = flip(mid_beside, "c")
    aug = prepare_back([mid_beside, mid_both], 1, out_w, o_tile, kept, query, aug)
    d_query, d_far = step_back(far_blocks, far_bases, 1, None, kinds, 1, 2, (d_query,), d_first)
    mid_both, aug, d_query, d_far, early, late = sync(mid_both, aug, d_query, d_far, early, late)

    back = [lax.ppermute(d_far[2 * n + m], "g", reverse(shift_pairs(d))) for n, d in enumerate(shifts) for m in range(2)]
    d_query, d_other = step_back(other, other_bases, 1, d_query, [BF] * 2)
    d_query, d_same = step_back(same, same_bases, 0, d_query, [BF] * len(same))
    out_sum = add_rows(late[0], 0, out_across[0], 0)
    d_query, d_other, d_same, d_far, back, out_sum = sync(d_query, d_other, d_same, d_far, back, out_sum)

    other_sum = [d_other[m].astype(F32) for m in range(2)]
    for n in range(len(shifts)):
        for m in range(2):
            other_sum[m] = other_sum[m] + back[2 * n + m].astype(F32)
    other_sum = [o.astype(BF) for o in other_sum]
    other_back = [flip(other_sum[0], "zh")]
    same_back = [lax.ppermute(d_same[n], "g", reverse(shift_pairs(d))) for n, d in enumerate(shifts)]
    above_back = []
    if above_groups:
        above = lax.dynamic_slice_in_dim(d_far[-1], zl * rows, rows, 0)
        above_back.append(lax.ppermute(above, ("g", "zh"), reverse(above_pairs)))
    out_beside = flip(out_sum, "zl")
    d_query, d_own = step_back([kv], own_bases, 0, d_query, [F32])
    core = jnp.reshape(2 * c + zl, (1,)).astype(jnp.int32)
    d_q, shares = query_back(core, d_query, qkv_w, cos_table, sin_table)
    q_part = head_grad([norm_one[k] for k in range(4)], d_q)

    def group_slice(part, k):
        return lax.dynamic_slice_in_dim(part, (g ^ k) * shard_pair, shard_pair, 0)

    q_slices = [group_slice(q_part, k) for k in range(groups)]
    other_back, same_back, above_back, d_own, shares, q_slices, other_late, early, late, out_beside = sync(
        other_back, same_back, above_back, d_own, shares, q_slices, other_sum[1], early, late, out_beside
    )

    other_back.append(flip(other_late, "zh"))
    o_part = head_grad([mid_low, mid_beside, mid_across, mid_both], mixed)
    second_column = gain_columns([early[2], late[2], early[3], late[3]], [norm_own, norm_beside, norm_across, norm_both], 1)
    ffn_give = [ffn_sum[:, (3 + n) * half : (4 + n) * half] for n in range(3)]
    q_got = [flip(q_slices[k], "g", k) for k in range(1, groups)]
    other_back, same_back, above_back, d_own, shares, q_slices, q_got, o_part, second_column, ffn_sum, ffn_give = sync(
        other_back, same_back, above_back, d_own, shares, q_slices, q_got, o_part, second_column, ffn_sum, ffn_give
    )
    o_sum = over_groups(o_part)

    gate_far = flip(ffn_give[0], "zh")
    d_kvs, shares = kv_back(core, d_own[0], other_back, same_back, above_back, shares, qkv_w, cos_table, sin_table)
    share_rows = shares.reshape(span, width)
    share_far = share_rows[2 * rows :]
    gate_far, d_kvs, shares, share_rows, share_far, up_give = sync(gate_far, d_kvs, shares, share_rows, share_far, ffn_give[1])
    up_far = flip(up_give, "zh")
    across = flip(share_far, "c")
    kv_part = kv_grad(norm_one, shares, d_kvs, second_column)
    kv_slices = [group_slice(kv_part, k) for k in range(groups)]
    beside_sum = add_rows(share_rows, 1, across, 1)
    down_give = jnp.concatenate([ffn_give[2], o_sum[:, 256:]], 1)
    down_give, beside_sum, kv_slices, across, share_rows, up_far, gate_far, ffn_sum = sync(
        down_give, beside_sum, kv_slices, across, share_rows, up_far, gate_far, ffn_sum
    )

    kv_got = [flip(kv_slices[k], "g", k) for k in range(1, groups)]
    q_sum = q_slices[0].astype(F32) + sum(v.astype(F32) for v in q_got)
    beside = flip(beside_sum, "zl")
    down_far = flip(down_give, "zh")
    down_far, kv_got, q_sum, beside, o_sum, ffn_sum, gate_far, up_far = sync(
        down_far, kv_got, q_sum, beside, o_sum, ffn_sum, gate_far, up_far
    )

    kv_sum = kv_slices[0].astype(F32) + sum(v.astype(F32) for v in kv_got)
    kvq_own = jnp.concatenate([kv_sum[:, :256], q_sum[:, :256]], 1)
    kvq_give = jnp.concatenate([kv_sum[:, 256:], q_sum[:, 256:]], 1).astype(BF)
    kvq_own, kvq_give, down_far, beside = sync(kvq_own, kvq_give, down_far, beside)
    kvq_far = flip(kvq_give, "zh")
    [input_grad] = backward_norm(0, share_rows, across, beside, inputs, grad_mid, gain_rows, [BF])
    far_sum = jnp.concatenate([gate_far, up_far, down_far], 1).astype(F32)
    near_sum = jnp.concatenate([ffn_sum[:, : 3 * half], o_sum[:, :256]], 1).astype(F32)
    sum_own, sum_got = to_owner(near_sum + far_sum)
    layer_out = (after_attn + (early[0].astype(F32) + out_across[1].astype(F32) + out_beside.astype(F32))).astype(BF)
    kvq_far, sum_own, sum_got, input_grad, layer_out = sync(kvq_far, sum_own, sum_got, input_grad, layer_out)

    kvq_own, kvq_got = to_owner(kvq_own + kvq_far.astype(F32))
    gain_sums = (kvq_own + kvq_got)[:, 2 * HEAD : 2 * HEAD + 2]
    gain_sums = gain_sums + flip(gain_sums, "zl")

    def columns(own, got, start, size):
        return in_order(own[:, start : start + size], got[:, start : start + size], 1)

    return (
        layer_out,
        input_grad,
        gain_sums[:, 0] / first_gain.astype(F32),
        columns(kvq_own, kvq_got, 256, 2 * HEAD),
        columns(kvq_own, kvq_got, 0, HEAD),
        columns(kvq_own, kvq_got, HEAD, HEAD),
        columns(sum_own, sum_got, 3 * half, 2 * HEAD).T,
        gain_sums[:, 1] / second_gain.astype(F32),
        columns(sum_own, sum_got, 0, half),
        columns(sum_own, sum_got, half, half),
        columns(sum_own, sum_got, 2 * half, half).T,
    )


def solution(mesh):
    outer, inner = mesh.devices.shape
    fine = Mesh(mesh.devices.reshape(outer // 2, 2, inner // 2, 2), AXES)
    data, tensor = ("g", "c"), ("zh", "zl")
    rows, first = P(AXES, None), P(data)
    wide, tall = P(data, tensor), P(tensor, data)
    return jax.shard_map(
        body,
        mesh=fine,
        in_specs=(rows, first, wide, wide, wide, tall, first, wide, wide, tall, P(), P(), rows),
        out_specs=(rows, rows, first, wide, wide, wide, tall, first, wide, wide, tall),
        check_vma=False,
    )
```
